32 devices in a mesh: exp: 8 (over z, y), dp: 4 (over x, core).
Axes of the slice: x: 2, y: 2, z: 4, core: 2. Of those that a mesh axis runs over, the one named last changes fastest.
Arguments:
- tokens: bfloat16 [4096, 768], P(('exp', 'dp')), may hold values from -6 to 6
- norm_gain: float32 [768], replicated, may hold values from 0.5 to 1.5
- w_query: bfloat16 [768, 768], replicated, may hold values from -0.21875 to 0.21875
- w_key: bfloat16 [768, 768], replicated, may hold values from -0.21875 to 0.21875
- w_value: bfloat16 [768, 768], replicated, may hold values from -0.21875 to 0.21875
- w_output: bfloat16 [768, 768], replicated, may hold values from -1.75 to 1.75
- rel_bias: float32 [32, 12], replicated, may hold values from -3 to 3
- ffn_gain: float32 [768], replicated, may hold values from 0.5 to 1.5
- w_router: bfloat16 [768, 8], replicated, may hold values from -0.375 to 0.375
- w_in: bfloat16 [8, 768, 3072], P('exp', None, 'dp'), may hold values from -0.21875 to 0.21875
- w_out: bfloat16 [8, 3072, 768], P('exp', 'dp'), may hold values from -2 to 2
- routes: int32 [4096, 1], P(('exp', 'dp')), may hold values from 0 to 7; in each aligned block of 128 rows (0 to 127, 128 to 255, ...) at most 40 rows name the same one
- lengths: int32 [32], P(('exp', 'dp')), may hold values from 32 to 128, as said below
- cotangent: bfloat16 [4096, 768], P(('exp', 'dp')), may hold values from -6 to 6
Outputs:
- output: bfloat16 [4096, 768], P(('exp', 'dp'))
- grad_input: bfloat16 [4096, 768], P(('exp', 'dp'))
- grad_norm_gain: float32 [768], replicated
- grad_query: float32 [768, 768], replicated
- grad_key: float32 [768, 768], replicated
- grad_value: float32 [768, 768], replicated
- grad_output_proj: float32 [768, 768], replicated
- grad_rel_bias: float32 [32, 12], replicated
- grad_ffn_gain: float32 [768], replicated
- grad_router: float32 [768, 8], replicated
- grad_w_in: float32 [8, 768, 3072], P('exp', None, 'dp')
- grad_w_out: float32 [8, 3072, 768], P('exp', 'dp')
The draws below stay inside these ranges and needn't reach their ends.
Inputs may be any that keep to these rules, and one draw needn't show every extreme that they name: `lengths`: each sequence's live tokens come first; some sequence has all 128 live in every draw. `routes`: among the 128 tokens of one sequence no expert is named more than 2 * 20 times, and in every draw some expert is named exactly 2 * 20 times in some sequence.
All inputs are finite; a program needn't handle non-finite values.
Results may differ from the reference program's by a relative error of at most 0.014.
The reference program's roundings to bfloat16 on the way count: a program that leaves them out, or rounds other values in their place, can miss the bound.
Values may be sent and summed in bfloat16 or wider, within the bound.
No kernel may reach another device: no remote copies, remote signals or barrier semaphores. Data moves between devices by JAX's collectives and lax.ppermute only.
A program may use at most 128 MiB of HBM per device.

```python
import math
import jax
import jax.numpy as jnp
import numpy as np
from jax import lax

D = 768
HEADS = 12
HEAD_DIM = 64
FF = 3072
BUCKETS = 32
TOK_DEV = 128
SEQS = 32
TOKENS = 4096
EXPERTS = 8
CAP = 20


def draw_lengths(key, part):
    base_lengths = jax.random.randint(key, (SEQS,), TOK_DEV // 4, TOK_DEV + 1)
    chosen = jax.random.randint(jax.random.fold_in(key, 7), (), 0, SEQS)
    return jnp.where(jnp.arange(SEQS) == chosen, TOK_DEV, base_lengths).astype(jnp.int32)


def levels(key, extent, cuts, low, high):
    loudness = 1.0
    for axis_at, shards_of in cuts:
        heights = jax.random.uniform(jax.random.fold_in(jax.random.fold_in(key, 6), axis_at), (shards_of,), jnp.float32, low / len(cuts), high / len(cuts))
        loudness = loudness * jnp.repeat(jnp.exp(heights), extent[axis_at] // shards_of).reshape((-1,) + (1,) * (len(extent) - 1 - axis_at))
    return loudness


def routed_block(stream_key, own, number, rows, count, top, most, lean):
    sequence = jax.random.permutation(stream_key, count)
    crowded, ordinary = portions_of(count, rows * top, most, lean, True), portions_of(count, rows * top, most, lean, False)
    places = jnp.arange(count)

    def named(sizes, offset_by):
        used = int((sizes > 0).sum())
        fixed = max(1, used // 4)
        passed = fixed + (places - fixed + offset_by * (used - fixed)) % max(1, count - fixed)
        return jnp.zeros((count,), jnp.int32).at[sequence[jnp.where(places < fixed, places, passed)]].set(jnp.asarray(sizes, jnp.int32))

    sizes = jnp.where(number % 4 == 0, named(crowded, number // 4), named(ordinary, number - number // 4 - 1))
    mixed = jax.random.permutation(jax.random.fold_in(own, 3), count)
    donor, receiver = mixed[0:count // 2 * 2:2], mixed[1:count // 2 * 2:2]
    slack = jnp.minimum(sizes[donor] - 1, most - sizes[receiver]) // 2
    slack = jnp.where((donor == sequence[0]) | (receiver == sequence[0]) | (sizes[receiver] == 0), 0, jnp.maximum(slack, 0))
    passed = jax.random.randint(jax.random.fold_in(own, 4), (count // 2,), 0, 1 << 20) % (slack + 1)
    sizes = sizes.at[donor].add(-passed).at[receiver].add(passed)
    items = jnp.searchsorted(jnp.cumsum(sizes), jnp.arange(rows * top), side="right").astype(jnp.int32)
    grid = items.reshape(top, rows).T
    grid = grid[jax.random.permutation(jax.random.fold_in(own, 1), rows)]
    offset_by = jax.random.randint(jax.random.fold_in(own, 2), (rows, 1), 0, top)
    return jnp.take_along_axis(grid, (jnp.arange(top)[None, :] + offset_by) % top, axis=1)


def portions_of(amount, total, reach, skew, full):
    loads = [(1 << 20) // math.isqrt(standing ** skew) + 1 for standing in range(1, amount + 1)]
    largest = reach if full else min(reach, max(-(-total // amount), total * loads[0] // sum(loads)))
    least = 1 if total - largest >= amount - 1 else 0
    counts, spare = [largest] + [least] * (amount - 1), total - largest - least * (amount - 1)
    while spare > 0:
        candidates = [i for i in range(1, amount) if counts[i] < largest] or [i for i in range(1, amount) if counts[i] < reach]
        pool, budget = sum([loads[i] for i in candidates]), spare
        for i in candidates:
            addition = min(reach - counts[i], max(1, budget * loads[i] // pool), spare)
            counts[i] = counts[i] + addition
            spare = spare - addition
    return np.array(counts)


def bell_draw(key, dims, width, reach, cuts=(), kind=jnp.bfloat16):
    array = width * jax.random.normal(key, dims, jnp.float32)
    if cuts:
        array = array * levels(key, dims, cuts, -0.22, 0.18)
    return jnp.clip(array, -reach, reach).astype(kind)


def setup_inputs(seed: int = 0) -> dict:
    arg_keys = jax.random.split(jax.random.key(seed), 15)
    tokens = bell_draw(arg_keys[0], (TOKENS, D), 1.0, 6.0, ((0, 32),))
    norm_gain = jnp.clip(1.0 + 0.1 * jax.random.normal(arg_keys[1], (D,), jnp.float32), 0.5, 1.5)
    w_query = bell_draw(arg_keys[2], (D, D), D ** -0.5, 0.21875)
    w_key = bell_draw(arg_keys[3], (D, D), D ** -0.5, 0.21875)
    w_value = bell_draw(arg_keys[4], (D, D), D ** -0.5, 0.21875)
    w_output = bell_draw(arg_keys[5], (D, D), (D // 64) ** -0.5, 1.75)
    rel_bias = bell_draw(arg_keys[6], (BUCKETS, HEADS), 0.5, 3.0, (), jnp.float32)
    ffn_gain = jnp.clip(1.0 + 0.1 * jax.random.normal(arg_keys[7], (D,), jnp.float32), 0.5, 1.5)
    w_router = bell_draw(arg_keys[8], (D, EXPERTS), (0.7 * D ** -0.5), 0.375)
    w_in = bell_draw(arg_keys[9], (EXPERTS, D, FF), D ** -0.5, 0.21875, ((0, 8), (2, 4)))
    w_out = bell_draw(arg_keys[10], (EXPERTS, FF, D), (EXPERTS * FF ** -0.5), 2.0, ((0, 8), (1, 4)))
    routes_keys = jax.random.split(jax.random.fold_in(arg_keys[11], 1), TOKENS // TOK_DEV)
    routes_turns = jax.random.permutation(jax.random.fold_in(arg_keys[11], 3), TOKENS // TOK_DEV)
    routes = jax.vmap(lambda own, number: routed_block(jax.random.fold_in(arg_keys[11], 2), own, number, TOK_DEV, EXPERTS, 1, 2 * CAP, 1))(routes_keys, routes_turns).reshape((TOKENS, 1))
    lengths = draw_lengths(jax.random.fold_in(arg_keys[14], 71), 0)
    cotangent = bell_draw(arg_keys[13], (TOKENS, D), 1.0, 6.0, ((0, 32),))
    return dict(tokens=tokens, norm_gain=norm_gain, w_query=w_query, w_key=w_key, w_value=w_value, w_output=w_output, rel_bias=rel_bias, ffn_gain=ffn_gain, w_router=w_router, w_in=w_in, w_out=w_out, routes=routes, lengths=lengths, cotangent=cotangent)


@jax.custom_vjp
def low(v):
    return lax.optimization_barrier(v.astype(jnp.bfloat16)).astype(jnp.float32)

@jax.custom_vjp
def low_back(v):
    return v

def low_keep(v):
    return (low(v), None)

def low_pass(kept, grad):
    return (grad,)

def back_keep(v):
    return (v, None)

def back_low(kept, grad):
    return (low(grad),)
low.defvjp(low_keep, low_pass)
low_back.defvjp(back_keep, back_low)
norm_eps = 1e-06
score_scale = 0.125
masked_score = -1e+30
far_limits = (11, 16, 22, 32, 45, 64, 90)

def bucket_index(length):
    places = jnp.arange(length, dtype=jnp.int32)
    offset = places[None, :] - places[:, None]
    distance = jnp.abs(offset)
    far_bucket = jnp.full(distance.shape, 8, jnp.int32)
    for limit_value in far_limits:
        far_bucket = far_bucket + (distance >= limit_value).astype(jnp.int32)
    near_bucket = jnp.where(distance < 8, distance, far_bucket)
    return near_bucket + 16 * (offset > 0).astype(jnp.int32)

def rms_norm(values, gain):
    return values * lax.rsqrt(lax.optimization_barrier(jnp.mean(values * values, axis=-1, keepdims=True)) + norm_eps) * gain

def layer_group(params, inputs, routes_group, live_group):
    norm_gain, w_query, w_key, w_value, w_output, rel_bias, ffn_gain, w_router, w_in, w_out = params
    highest = lax.Precision.HIGHEST
    group_size, length, model_width = inputs.shape
    normed = low(rms_norm(inputs, norm_gain))

    def project(weight):
        values = low(low_back(jnp.einsum('gsd,de->gse', normed, weight, precision=highest)))
        return values.reshape(group_size, length, HEADS, HEAD_DIM)
    query_heads = project(w_query)
    key_heads = project(w_key)
    value_heads = project(w_value)
    bias_field = jnp.take(rel_bias, bucket_index(length), axis=0).transpose(2, 0, 1)
    scores = jnp.einsum('gqhe,gkhe->ghqk', query_heads, key_heads, precision=highest) * score_scale + bias_field[None]
    scores = low_back(scores)
    scores = jnp.where(live_group[:, None, None, :] > 0, scores, masked_score)
    weights = low(jax.nn.softmax(scores, axis=-1))
    attended = jnp.einsum('ghqk,gkhe->gqhe', weights, value_heads, precision=highest).reshape(group_size, length, model_width)
    attended = low(low_back(attended))
    attn_out = low_back(jnp.einsum('gsd,de->gse', attended, w_output, precision=highest))
    hidden = inputs + attn_out
    normed_two = low(rms_norm(hidden, ffn_gain))
    logits = low_back(jnp.einsum('gsd,de->gse', normed_two, w_router, precision=highest))
    router_probs = jax.nn.softmax(logits, axis=-1)
    experts = w_router.shape[1]
    choose = routes_group[..., None] == jnp.arange(experts, dtype=jnp.int32)
    choose_int = choose.astype(jnp.int32)
    running = jnp.cumsum(choose_int * live_group[..., None], axis=1)
    slot_index = lax.optimization_barrier(jnp.sum(running * choose_int, axis=-1)) - 1
    kept_mask = (live_group > 0) & (slot_index < CAP)
    dispatch = (choose[..., None] & (slot_index[..., None, None] == jnp.arange(CAP, dtype=jnp.int32)) & kept_mask[..., None, None]).astype(jnp.float32)
    gate_value = lax.optimization_barrier(jnp.sum(router_probs * choose.astype(jnp.float32), axis=-1))
    slots = low_back(jnp.einsum('gsec,gsd->gecd', dispatch, normed_two, precision=highest))
    inner_sum = low_back(jnp.einsum('gecd,edf->gecf', slots, w_in, precision=highest))
    active = low(jax.nn.gelu(inner_sum))
    result = low(low_back(jnp.einsum('gecf,efd->gecd', active, w_out, precision=highest)))
    returned = jnp.einsum('gsec,gecd->gsd', dispatch, result, precision=highest)
    return hidden + gate_value[..., None] * returned

def reference(tokens, norm_gain, w_query, w_key, w_value, w_output, rel_bias, ffn_gain, w_router, w_in, w_out, routes, lengths, cotangent):
    group_size = math.gcd(SEQS, max(1, 4096 // TOK_DEV))
    rounds = SEQS // group_size
    inputs = tokens.astype(jnp.float32).reshape(rounds, group_size, TOK_DEV, D)
    route_ids = routes.reshape(rounds, group_size, TOK_DEV).astype(jnp.int32)
    live_mask = (jnp.arange(TOK_DEV, dtype=jnp.int32)[None, :] < lengths[:, None]).astype(jnp.int32)
    live_mask = live_mask.reshape(rounds, group_size, TOK_DEV)
    params = tuple((source_array.astype(jnp.float32) for source_array in (norm_gain, w_query, w_key, w_value, w_output, rel_bias, ffn_gain, w_router, w_in, w_out)))

    def forward(inputs, params):
        step_fn = jax.checkpoint(layer_group)

        def scan_body(carry_state, pieces):
            return (carry_state, step_fn(params, pieces[0], pieces[1], pieces[2]))
        _, outputs = lax.scan(scan_body, None, (inputs, route_ids, live_mask))
        return outputs
    outputs, pullback = jax.vjp(forward, inputs, params)
    grad_inputs, gradients = pullback(cotangent.astype(jnp.float32).reshape(rounds, group_size, TOK_DEV, D))
    return (outputs.reshape(TOKENS, D).astype(jnp.bfloat16), grad_inputs.reshape(TOKENS, D).astype(jnp.bfloat16), gradients[0], gradients[1], gradients[2], gradients[3], gradients[4], gradients[5], gradients[6], gradients[7], gradients[8], gradients[9])
```

```python
import jax
import jax.numpy as jnp
from jax import lax
from jax.sharding import Mesh
from jax.sharding import PartitionSpec as P

HEADS = 12
HEAD_DIM = 64
BUCKETS = 32
LANES = 128

norm_eps = 1e-06
score_scale = 0.125
masked_score = -1e30
far_limits = (11, 16, 22, 32, 45, 64, 90)

EXPERT_AXES = ("eh", "em", "ey", "dx")
GROUP_AXES = ("em", "ey", "dx", "dc")
TOKEN_AXES = ("eh", "em", "ey", "dx", "dc")


def bucket_of(offset):
    distance = jnp.abs(offset)
    far_bucket = jnp.full(distance.shape, 8, jnp.int32)
    for limit_value in far_limits:
        far_bucket = far_bucket + (distance >= limit_value).astype(jnp.int32)
    near_bucket = jnp.where(distance < 8, distance, far_bucket)
    return near_bucket + 16 * (offset > 0).astype(jnp.int32)


def bucket_index(length):
    places = jnp.arange(length, dtype=jnp.int32)
    return bucket_of(places[None, :] - places[:, None])


def dot_last(left_side, right_side):
    return lax.dot_general(
        left_side, right_side, (((1,), (1,)), ((), ())), preferred_element_type=jnp.float32
    )


def dot_first(left_side, right_side):
    return lax.dot_general(
        left_side, right_side, (((0,), (0,)), ((), ())), preferred_element_type=jnp.float32
    )


def gelu_grad(inner_sum, upstream):
    _, pullback = jax.vjp(jax.nn.gelu, inner_sum)
    return pullback(upstream)[0]


def norm_backward(values, factor, gain, grad_normed):
    scaled = gain * grad_normed
    grad_gain = jnp.sum(grad_normed * values * factor, axis=0)
    grad_values = factor * scaled - values * factor * factor * factor * jnp.mean(
        scaled * values, axis=-1, keepdims=True
    )
    return (grad_values, grad_gain)


def swap(array, axis):
    return lax.ppermute(array, axis, perm=[(0, 1), (1, 0)])


def in_order(own, other, axis):
    first = lax.axis_index(axis) == 0
    return jnp.stack([jnp.where(first, own, other), jnp.where(first, other, own)])


def gather_pair(array, axis):
    return in_order(array, swap(array, axis), axis)


def split_two(values):
    high = values.astype(jnp.bfloat16)
    low = (values - high.astype(jnp.float32)).astype(jnp.bfloat16)
    return high, low


def per_device(
    tokens,
    norm_gain,
    w_query,
    w_key,
    w_value,
    w_output,
    rel_bias,
    ffn_gain,
    w_router,
    w_in,
    w_out,
    routes,
    lengths,
    cotangent,
):
    low_type = jnp.bfloat16
    length, model_width = tokens.shape
    experts = w_router.shape[1]
    eh_count = lax.axis_size("eh")
    group = lax.axis_size(GROUP_AXES)
    capacity = max(2, (5 * length + 4 * experts - 1) // (4 * experts))

    w_in_own, w_out_own = w_in[0], w_out[0]
    w_in_other, w_out_other = swap(w_in_own, "dc"), swap(w_out_own, "dc")
    tokens_all = lax.all_gather(tokens, GROUP_AXES, axis=0, tiled=True)

    inputs = tokens.astype(jnp.float32)
    live_mask = jnp.arange(length, dtype=jnp.int32) < lengths[0]
    factor_one = lax.rsqrt(jnp.mean(inputs * inputs, axis=-1, keepdims=True) + norm_eps)
    normed = (inputs * factor_one * norm_gain).astype(low_type)
    queries = jnp.dot(normed, w_query, preferred_element_type=jnp.float32).astype(low_type)
    keys_all = jnp.dot(normed, w_key, preferred_element_type=jnp.float32).astype(low_type)
    values_all = jnp.dot(normed, w_value, preferred_element_type=jnp.float32).astype(low_type)
    query_heads = queries.reshape(length, HEADS, HEAD_DIM)
    key_heads = keys_all.reshape(length, HEADS, HEAD_DIM)
    value_heads = values_all.reshape(length, HEADS, HEAD_DIM)
    buckets = bucket_index(length)
    bucket_onehot = buckets[:, :, None] == jnp.arange(BUCKETS, dtype=jnp.int32)
    bias_field = jnp.einsum(
        "qkb,bh->hqk",
        bucket_onehot.astype(jnp.float32),
        rel_bias,
        precision=lax.Precision.HIGHEST,
        preferred_element_type=jnp.float32,
    )
    scores = (
        jnp.einsum("qhe,khe->hqk", query_heads, key_heads, preferred_element_type=jnp.float32)
        * score_scale
        + bias_field
    )
    scores = jnp.where(live_mask[None, None, :], scores, masked_score)
    probs = jax.nn.softmax(scores, axis=-1)
    attn_weights = probs.astype(low_type)
    attended = jnp.einsum(
        "hqk,khe->qhe", attn_weights, value_heads, preferred_element_type=jnp.float32
    )
    attended = attended.reshape(length, model_width).astype(low_type)
    attended_all = lax.all_gather(attended, GROUP_AXES, axis=0, tiled=True)
    hidden = inputs + jnp.dot(attended, w_output, preferred_element_type=jnp.float32)
    factor_two = lax.rsqrt(jnp.mean(hidden * hidden, axis=-1, keepdims=True) + norm_eps)
    normed_two = (hidden * factor_two * ffn_gain).astype(low_type)
    logits = jnp.dot(normed_two, w_router, preferred_element_type=jnp.float32)
    router_probs = jax.nn.softmax(logits, axis=-1)
    choose = routes[:, 0][:, None] == jnp.arange(experts, dtype=jnp.int32)
    choose_int = choose.astype(jnp.int32)
    running = jnp.cumsum(choose_int * live_mask[:, None].astype(jnp.int32), axis=0)
    slot_index = jnp.sum(running * choose_int, axis=1) - 1
    kept_mask = live_mask & (slot_index < capacity)
    dispatch = (
        choose[:, :, None]
        & (slot_index[:, None, None] == jnp.arange(capacity, dtype=jnp.int32))
        & kept_mask[:, None, None]
    )
    dispatch_low = dispatch.astype(low_type)
    gate_value = jnp.sum(jnp.where(choose, router_probs, 0.0), axis=1)
    grad_top = cotangent.astype(jnp.float32)
    scaled_grad = (gate_value[:, None] * grad_top).astype(low_type)
    packed = jnp.einsum(
        "tec,td->ecd", dispatch_low, normed_two, preferred_element_type=jnp.float32
    ).astype(low_type)
    grad_packed = jnp.einsum(
        "tec,td->ecd", dispatch_low, scaled_grad, preferred_element_type=jnp.float32
    ).astype(low_type)
    outgoing = jnp.concatenate([packed, grad_packed], axis=1)
    outgoing = jnp.broadcast_to(outgoing[:, None], (experts, 2) + outgoing.shape[1:])
    outgoing = outgoing.reshape((experts * 2,) + outgoing.shape[2:])
    incoming = lax.all_to_all(outgoing, EXPERT_AXES, split_axis=0, concat_axis=0, tiled=True)
    expert_rows = incoming[:, :capacity].reshape(-1, model_width)
    grad_slots = incoming[:, capacity:].reshape(-1, model_width)

    result, d_rows = 0.0, 0.0
    expert_grads = []
    for part_in, part_out in ((w_in_own, w_out_own), (w_in_other, w_out_other)):
        inner_sum = jnp.dot(expert_rows, part_in, preferred_element_type=jnp.float32)
        active = jax.nn.gelu(inner_sum).astype(low_type)
        result = result + jnp.dot(active, part_out, preferred_element_type=jnp.float32)
        d_active = dot_last(grad_slots, part_out)
        d_inner = gelu_grad(inner_sum, d_active).astype(low_type)
        d_rows = d_rows + dot_last(d_inner, part_in)
        expert_grads.append((dot_first(expert_rows, d_inner), dot_first(active, grad_slots)))
    sent_back = jnp.concatenate(
        [
            result.astype(low_type).reshape(-1, capacity, model_width),
            d_rows.astype(low_type).reshape(-1, capacity, model_width),
        ],
        axis=1,
    )
    came_back = lax.all_to_all(sent_back, EXPERT_AXES, split_axis=0, concat_axis=0, tiled=True)
    came_back = came_back.reshape(experts, 2, 2 * capacity, model_width).astype(jnp.float32)
    came_back = (came_back[:, 0] + came_back[:, 1]).astype(low_type)
    (in_own, out_own), (in_other, out_other) = expert_grads
    grad_in = in_own + swap(in_other.astype(low_type), "dc").astype(jnp.float32)
    grad_out = out_own + swap(out_other.astype(low_type), "dc").astype(jnp.float32)

    returned = jnp.einsum(
        "tec,ecd->td", dispatch_low, came_back[:, :capacity], preferred_element_type=jnp.float32
    )
    output = (hidden + gate_value[:, None] * returned).astype(low_type)
    d_normed_two = jnp.einsum(
        "tec,ecd->td", dispatch_low, came_back[:, capacity:], preferred_element_type=jnp.float32
    )
    d_gate = jnp.sum(grad_top * returned, axis=1)
    d_router_probs = jnp.where(choose, d_gate[:, None], 0.0)
    d_logits = router_probs * (
        d_router_probs - jnp.sum(router_probs * d_router_probs, axis=1, keepdims=True)
    )
    d_logits = d_logits.astype(low_type)
    grad_router = dot_first(normed_two, d_logits)
    d_normed_two = d_normed_two + dot_last(d_logits, w_router)
    d_from_norm, grad_ffn = norm_backward(hidden, factor_two, ffn_gain, d_normed_two)
    d_hidden = grad_top + d_from_norm
    d_mixed = d_hidden.astype(low_type)
    d_attended = dot_last(d_mixed, w_output).astype(low_type).reshape(length, HEADS, HEAD_DIM)
    d_probs_attn = jnp.einsum(
        "qhe,khe->hqk", d_attended, value_heads, preferred_element_type=jnp.float32
    )
    grad_values = jnp.einsum(
        "hqk,qhe->khe", attn_weights, d_attended, preferred_element_type=jnp.float32
    )
    grad_values = grad_values.astype(low_type).reshape(length, model_width)
    d_scores = probs * (d_probs_attn - jnp.sum(probs * d_probs_attn, axis=-1, keepdims=True))
    d_scores = d_scores.astype(low_type)
    grad_queries = (
        jnp.einsum("hqk,khe->qhe", d_scores, key_heads, preferred_element_type=jnp.float32)
        * score_scale
    )
    grad_queries = grad_queries.astype(low_type).reshape(length, model_width)
    grad_keys = (
        jnp.einsum("hqk,qhe->khe", d_scores, query_heads, preferred_element_type=jnp.float32)
        * score_scale
    )
    grad_keys = grad_keys.astype(low_type).reshape(length, model_width)
    grad_bias = jnp.einsum(
        "hqk,qkb->bh", d_scores, bucket_onehot.astype(low_type), preferred_element_type=jnp.float32
    )
    d_normed = (
        dot_last(grad_queries, w_query)
        + dot_last(grad_keys, w_key)
        + dot_last(grad_values, w_value)
    )
    d_from_first, grad_norm = norm_backward(inputs, factor_one, norm_gain, d_normed)
    grad_input = (d_hidden + d_from_first).astype(low_type)

    small_sizes = (model_width, model_width, BUCKETS * HEADS, model_width * experts)
    small = jnp.concatenate(
        [grad_norm, grad_ffn, grad_bias.reshape(-1), grad_router.reshape(-1)]
    )
    small_rows = -(-small.shape[0] // (LANES * group))
    small = jnp.pad(small, (0, small_rows * group * LANES - small.shape[0]))
    small_high, small_low = split_two(small.reshape(group, small_rows, LANES))
    block = 4 * model_width // group
    factors = jnp.concatenate([grad_queries, grad_keys, grad_values, d_mixed], axis=1)
    factors = factors.T.reshape(group, block, length)
    late = jnp.concatenate([factors, small_high, small_low], axis=1)
    late = lax.all_to_all(late, GROUP_AXES, split_axis=0, concat_axis=0, tiled=True)
    small = jnp.sum(late[:, block:].astype(jnp.float32), axis=0)
    small = small[:small_rows] + small[small_rows:]

    inputs_all = tokens_all.astype(jnp.float32)
    factor_all = lax.rsqrt(jnp.mean(inputs_all * inputs_all, axis=-1, keepdims=True) + norm_eps)
    normed_all = (inputs_all * factor_all * norm_gain).astype(low_type)
    which = lax.axis_index(GROUP_AXES) // (group // 4)
    left_all = jnp.where(which == 3, attended_all, normed_all)
    late_block = late[:, :block].transpose(1, 0, 2).reshape(block, group * length)
    grad_block = jnp.dot(late_block, left_all, preferred_element_type=jnp.float32)

    part = block // eh_count
    grad_block = grad_block.reshape(eh_count, part, model_width)
    if eh_count == 2:
        place = lax.axis_index("eh")
        mine = lax.dynamic_index_in_dim(grad_block, place, 0, keepdims=False)
        theirs = lax.dynamic_index_in_dim(grad_block, 1 - place, 0, keepdims=False)
        small_high, small_low = split_two(small)
        sent = jnp.concatenate(
            [theirs.astype(low_type).reshape(-1, LANES), small_high, small_low], axis=0
        )
        got = swap(sent, "eh").astype(jnp.float32)
        edge = part * model_width // LANES
        mine = mine.reshape(-1, LANES) + got[:edge]
        small = small + (got[edge : edge + small_rows] + got[edge + small_rows :])
    else:
        mine = lax.psum_scatter(grad_block, "eh", scatter_dimension=0, tiled=True)
        mine = mine.reshape(-1, LANES)
        small = lax.psum(small, "eh")
        edge = mine.shape[0]
    small_high, small_low = split_two(small)
    share = jnp.concatenate([mine.astype(low_type), small_high, small_low], axis=0)
    rows = share.shape[0]

    if eh_count == 2:
        share = gather_pair(share, "eh")
    else:
        share = lax.all_gather(share, "eh", axis=0, tiled=False)
    share = gather_pair(share, "em").reshape(2 * eh_count * rows, LANES)
    half = eh_count * rows
    first, second = share[:half], share[half:]
    first = gather_pair(first, "dx")
    second = gather_pair(second, "ey")
    first = gather_pair(first, "ey")
    second = gather_pair(second, "dx").transpose(1, 0, 2, 3)
    whole = jnp.stack([first, second])
    whole = gather_pair(whole, "dc")
    whole = whole.reshape(2, 2, 2, 2, eh_count, rows, LANES)
    whole = whole.transpose(1, 2, 3, 0, 4, 5, 6).reshape(group, eh_count, rows, LANES)
    grads = whole[:, :, :edge].reshape(4, model_width, model_width).transpose(0, 2, 1)
    grads = grads.astype(jnp.float32)
    small = whole[:, 0, edge:].astype(jnp.float32)
    small = (small[:, :small_rows] + small[:, small_rows:]).reshape(-1)
    pieces, at = [], 0
    for size in small_sizes:
        pieces.append(small[at : at + size])
        at += size
    return (
        output,
        grad_input,
        pieces[0],
        grads[0],
        grads[1],
        grads[2],
        grads[3],
        pieces[2].reshape(BUCKETS, HEADS),
        pieces[1],
        pieces[3].reshape(model_width, experts),
        grad_in[None],
        grad_out[None],
    )


def solution(mesh):
    exp_count, dp_count = mesh.shape["exp"], mesh.shape["dp"]
    fine = Mesh(
        mesh.devices.reshape(exp_count // 4, 2, 2, dp_count // 2, 2),
        TOKEN_AXES,
    )
    exp, dp = ("eh", "em", "ey"), ("dx", "dc")
    in_specs = (
        P(TOKEN_AXES, None),
        P(),
        P(),
        P(),
        P(),
        P(),
        P(),
        P(),
        P(),
        P(exp, None, dp),
        P(exp, dp, None),
        P(TOKEN_AXES, None),
        P(TOKEN_AXES),
        P(TOKEN_AXES, None),
    )
    out_specs = (
        P(TOKEN_AXES, None),
        P(TOKEN_AXES, None),
        P(),
        P(),
        P(),
        P(),
        P(),
        P(),
        P(),
        P(),
        P(exp, None, dp),
        P(exp, dp, None),
    )
    return jax.shard_map(
        per_device, mesh=fine, in_specs=in_specs, out_specs=out_specs, check_vma=False
    )
```

```python
import functools

import jax
import jax.numpy as jnp
import numpy as np
from jax import lax
from jax.experimental import pallas as pl
from jax.experimental.pallas import tpu as pltpu
from jax.sharding import Mesh
from jax.sharding import PartitionSpec as P

HEADS = 12
HEAD_DIM = 64
BUCKETS = 32
LANES = 128

norm_eps = 1e-06
score_scale = 0.125
masked_score = -1e30
far_limits = (11, 16, 22, 32, 45, 64, 90)

EXPERT_AXES = ("eh", "em", "ey", "dx")
GROUP_AXES = ("em", "ey", "dx", "dc")
TOKEN_AXES = ("eh", "em", "ey", "dx", "dc")


def bucket_of(offset):
    distance = jnp.abs(offset)
    far_bucket = jnp.full(distance.shape, 8, jnp.int32)
    for limit_value in far_limits:
        far_bucket = far_bucket + (distance >= limit_value).astype(jnp.int32)
    near_bucket = jnp.where(distance < 8, distance, far_bucket)
    return near_bucket + 16 * (offset > 0).astype(jnp.int32)


def bucket_index(length):
    places = jnp.arange(length, dtype=jnp.int32)
    return bucket_of(places[None, :] - places[:, None])


def dot_last(left_side, right_side):
    return lax.dot_general(
        left_side, right_side, (((1,), (1,)), ((), ())), preferred_element_type=jnp.float32
    )


def dot_first(left_side, right_side):
    return lax.dot_general(
        left_side, right_side, (((0,), (0,)), ((), ())), preferred_element_type=jnp.float32
    )


def norm_backward(values, factor, gain, grad_normed):
    scaled = gain * grad_normed
    grad_gain = jnp.sum(grad_normed * values * factor, axis=0)
    grad_values = factor * scaled - values * factor * factor * factor * jnp.mean(
        scaled * values, axis=-1, keepdims=True
    )
    return (grad_values, grad_gain)


def swap(array, axis):
    return lax.ppermute(array, axis, perm=[(0, 1), (1, 0)])


def split_two(values):
    high = values.astype(jnp.bfloat16)
    low = (values - high.astype(jnp.float32)).astype(jnp.bfloat16)
    return high, low

def whole_spec():
    return pl.BlockSpec(memory_space=pltpu.VMEM)


def any_spec():
    return pl.BlockSpec(memory_space=pl.ANY)


def params(mib):
    return pltpu.CompilerParams(vmem_limit_bytes=mib * 1024 * 1024)


def cost(flops, moved):
    return pl.CostEstimate(flops=flops, bytes_accessed=moved, transcendentals=0)


def shaped(dims, kind):
    return jax.ShapeDtypeStruct(dims, kind)


gelu_scale = 0.7978845608028654
gelu_cubic = 0.044715


def expert_kernel(
    rows_ref, order_ref, in_a, out_a, in_b, out_b, back_ref, rows_out, grads_out, act_ref, inner_ref
):
    count = rows_ref.shape[0]
    half = count // 2
    lanes = lax.broadcasted_iota(jnp.int32, (count, count), 1)
    sort = jnp.where(order_ref[:, 0:1] == lanes, 1.0, 0.0).astype(jnp.bfloat16)
    unsort = jnp.where(order_ref[:, 1:2] == lanes, 1.0, 0.0).astype(jnp.bfloat16)
    ordered = jnp.dot(sort, rows_ref[...], preferred_element_type=jnp.float32)
    ordered = ordered.astype(jnp.bfloat16)
    rows, slots = ordered[:half], ordered[half:]
    rows_out[...] = rows
    grads_out[...] = slots
    result, d_rows = 0.0, 0.0
    for part, (part_in, part_out) in enumerate(((in_a, out_a), (in_b, out_b))):
        inner = jnp.dot(rows, part_in[...], preferred_element_type=jnp.float32)
        upstream = dot_last(slots, part_out[...])
        square = inner * inner
        bent = jnp.tanh(gelu_scale * (inner + gelu_cubic * (square * inner)))
        active = (inner * (0.5 * (1.0 + bent))).astype(jnp.bfloat16)
        slope = 0.5 * (1.0 + bent) + 0.5 * inner * (1.0 - bent * bent) * (
            gelu_scale * (1.0 + 3.0 * gelu_cubic * square)
        )
        d_inner = (upstream * slope).astype(jnp.bfloat16)
        act_ref[part] = active
        inner_ref[part] = d_inner
        result = result + jnp.dot(active, part_out[...], preferred_element_type=jnp.float32)
        d_rows = d_rows + dot_last(d_inner, part_in[...])
    both = jnp.concatenate([result.astype(jnp.bfloat16), d_rows.astype(jnp.bfloat16)], axis=0)
    back_ref[...] = jnp.dot(unsort, both, preferred_element_type=jnp.float32).astype(jnp.bfloat16)


def expert_rows_of(rows, capacity, part_weights):
    count, width = rows.shape
    half = count // 2
    place = np.arange(count)
    sort = place % half // capacity * 2 * capacity + place // half * capacity + place % capacity
    unsort = np.empty_like(sort)
    unsort[sort] = place
    order = jnp.asarray(np.stack([sort, unsort], axis=1), jnp.int32)
    hidden_width = part_weights[0].shape[1]
    low = jnp.bfloat16
    return pl.pallas_call(
        expert_kernel,
        out_shape=(
            shaped((count, width), low),
            shaped((half, width), low),
            shaped((half, width), low),
            shaped((2, half, hidden_width), low),
            shaped((2, half, hidden_width), low),
        ),
        in_specs=[whole_spec()] * 6,
        out_specs=(whole_spec(),) * 5,
        compiler_params=params(48),
        cost_estimate=cost(16 * half * width * hidden_width, 12 * width * width),
        name="expert_rows",
    )(rows, order, *part_weights)


def expert_grads_kernel(rows_ref, slots_ref, act_ref, inner_ref, own_in, own_out, sent_in, sent_out):
    own_in[...] = dot_first(rows_ref[...], inner_ref[0])
    sent_in[...] = dot_first(rows_ref[...], inner_ref[1]).astype(jnp.bfloat16)
    own_out[...] = dot_first(act_ref[0], slots_ref[...])
    sent_out[...] = dot_first(act_ref[1], slots_ref[...]).astype(jnp.bfloat16)


def expert_grads_of(rows, slots, active, d_inner):
    half, width = rows.shape
    hidden_width = active.shape[2]
    return pl.pallas_call(
        expert_grads_kernel,
        out_shape=(
            shaped((width, hidden_width), jnp.float32),
            shaped((hidden_width, width), jnp.float32),
            shaped((width, hidden_width), jnp.bfloat16),
            shaped((hidden_width, width), jnp.bfloat16),
        ),
        in_specs=[whole_spec()] * 4,
        out_specs=(whole_spec(),) * 4,
        compiler_params=params(48),
        cost_estimate=cost(8 * half * width * hidden_width, 12 * width * width),
        name="expert_grads",
    )(rows, slots, active, d_inner)


def block_kernel(place_ref, late_ref, left_ref, mine_ref, sent_ref, small_ref, held):
    group, rows, length = late_ref.shape
    part, width = held.shape[1], held.shape[2]
    block = 2 * part
    small_rows = small_ref.shape[0]
    right = jnp.concatenate([late_ref[i, :block] for i in range(group)], axis=1)
    total = jnp.dot(right, left_ref[...], preferred_element_type=jnp.float32)
    held[0] = total[:part]
    held[1] = total[part:]
    place = place_ref[0]
    mine, theirs = held[place], held[1 - place]
    for chunk in range(width // LANES):
        lanes = slice(chunk * LANES, (chunk + 1) * LANES)
        mine_ref[chunk * part : (chunk + 1) * part] = mine[:, lanes]
        sent_ref[chunk * part : (chunk + 1) * part] = theirs[:, lanes].astype(jnp.bfloat16)
    tail = jnp.sum(late_ref[:, block:].astype(jnp.float32), axis=0)
    small = tail[:small_rows] + tail[small_rows:]
    small_ref[...] = small
    high = small.astype(jnp.bfloat16).astype(jnp.float32)
    both = jnp.concatenate([high, small - high], axis=0)
    sent_ref[sent_ref.shape[0] - 2 * small_rows :] = both.astype(jnp.bfloat16)


def block_of(place, late, left, small_rows):
    group, rows, length = late.shape
    width = left.shape[1]
    part = (rows - 2 * small_rows) // 2
    edge = part * width // LANES
    return pl.pallas_call(
        block_kernel,
        out_shape=(
            shaped((edge, LANES), jnp.float32),
            shaped((edge + 2 * small_rows, LANES), jnp.bfloat16),
            shaped((small_rows, LANES), jnp.float32),
        ),
        in_specs=[pl.BlockSpec(memory_space=pltpu.SMEM), whole_spec(), whole_spec()],
        out_specs=(whole_spec(),) * 3,
        scratch_shapes=[pltpu.VMEM((2, part, width), jnp.float32)],
        compiler_params=params(48),
        cost_estimate=cost(4 * part * width * group * length, 2 * left.size),
        name="grad_block",
    )(place, late, left)


def share_kernel(mine_ref, small_ref, got_ref, share_ref):
    edge, small_rows = mine_ref.shape[0], small_ref.shape[0]
    share_ref[:edge] = (mine_ref[...] + got_ref[:edge].astype(jnp.float32)).astype(jnp.bfloat16)
    tail = got_ref[edge:].astype(jnp.float32)
    small = small_ref[...] + (tail[:small_rows] + tail[small_rows:])
    high = small.astype(jnp.bfloat16).astype(jnp.float32)
    share_ref[edge:] = jnp.concatenate([high, small - high], axis=0).astype(jnp.bfloat16)


def share_of(mine, small, got):
    return pl.pallas_call(
        share_kernel,
        out_shape=shaped(got.shape, jnp.bfloat16),
        in_specs=[whole_spec()] * 3,
        out_specs=whole_spec(),
        compiler_params=params(16),
        cost_estimate=cost(mine.size, 8 * mine.size),
        name="share",
    )(mine, small, got)


def assemble_kernel(part, small_rows, bits_ref, *refs):
    sources, outs, small_out = refs[:8], refs[8:12], refs[12]
    held, made, in_sems, out_sems = refs[13:]
    em, ey, dx, dc, eh = [bits_ref[i] for i in range(5)]
    edge = held.shape[2] - 2 * small_rows
    width = made.shape[1]
    copies = [[] for _ in range(4)]
    for far in range(2):
        core = dc ^ far
        for side, first in enumerate(("x", "x", "y", "y")):
            source = sources[far * 4 + side]
            for at in range(2):
                if first == "x":
                    weight, step = side, at
                else:
                    weight, step = 2 + at, side - 2
                for other in range(2):
                    to = ((dx ^ step) * 2 + core) * 2 + (eh ^ other)
                    copies[weight].append(
                        pltpu.make_async_copy(
                            source.at[at, other],
                            held.at[weight, to],
                            in_sems.at[weight, len(copies[weight])],
                        )
                    )
    for weight in range(4):
        for copy in copies[weight]:
            copy.start()
    unit = lax.broadcasted_iota(jnp.int32, (LANES, LANES), 0)
    unit = jnp.where(unit == lax.broadcasted_iota(jnp.int32, (LANES, LANES), 1), 1.0, 0.0)
    unit = unit.astype(jnp.bfloat16)
    for weight in range(4):
        for copy in copies[weight]:
            copy.wait()
        for chunk in range(width // LANES):
            columns = jnp.concatenate(
                [held[weight, i, chunk * part : (chunk + 1) * part] for i in range(8)], axis=0
            )
            made[weight, chunk * LANES : (chunk + 1) * LANES] = dot_last(unit, columns)
        truth = (em ^ (weight // 2)) * 2 + (ey ^ (weight % 2))
        for i in range(4):
            at = 2 * i
            tail = held[weight, at, edge:].astype(jnp.float32)
            small_out[truth, i] = tail[:small_rows] + tail[small_rows:]

            @pl.when(truth == i)
            def _():
                pltpu.make_async_copy(made.at[weight], outs[i], out_sems.at[weight]).start()

    for weight in range(4):
        truth = (em ^ (weight // 2)) * 2 + (ey ^ (weight % 2))
        for i in range(4):

            @pl.when(truth == i)
            def _():
                pltpu.make_async_copy(made.at[weight], outs[i], out_sems.at[weight]).wait()


def assemble(bits, sources, part, small_rows, width):
    rows = sources[0].shape[2]
    return pl.pallas_call(
        functools.partial(assemble_kernel, part, small_rows),
        out_shape=(shaped((width, width), jnp.float32),) * 4
        + (shaped((4, 4, small_rows, LANES), jnp.float32),),
        in_specs=[pl.BlockSpec(memory_space=pltpu.SMEM)] + [any_spec()] * 8,
        out_specs=(any_spec(),) * 4 + (whole_spec(),),
        scratch_shapes=[
            pltpu.VMEM((4, 8, rows, LANES), jnp.bfloat16),
            pltpu.VMEM((4, width, width), jnp.float32),
            pltpu.SemaphoreType.DMA((4, 8)),
            pltpu.SemaphoreType.DMA((4,)),
        ],
        compiler_params=params(48),
        cost_estimate=cost(8 * LANES * width * width, 24 * width * width),
        name="assemble",
    )(bits, *sources)


def gathered_grads(late, left_all, small_rows):
    width = left_all.shape[1]
    place = lax.axis_index("eh").astype(jnp.int32)
    mine, sent, small = block_of(place[None], late, left_all, small_rows)
    share = share_of(mine, small, swap(sent, "eh"))
    near = jnp.stack([share, swap(share, "eh")])
    far = swap(near, "em")
    near_x = jnp.stack([near, swap(near, "dx")])
    far_y = jnp.stack([far, swap(far, "ey")])
    near_y = swap(near_x, "ey")
    far_x = swap(far_y, "dx")
    sources = (near_x, near_y, far_y, far_x)
    sources = sources + tuple(swap(source, "dc") for source in sources)
    bits = jnp.stack([lax.axis_index(axis) for axis in ("em", "ey", "dx", "dc", "eh")])
    part = (late.shape[1] - 2 * small_rows) // 2
    *grads, small = assemble(bits.astype(jnp.int32), sources, part, small_rows, width)
    return grads, small


def gathered_grads_plain(late, left_all, small_rows):
    group, rows, length = late.shape
    width = left_all.shape[1]
    block = rows - 2 * small_rows
    small = jnp.sum(late[:, block:].astype(jnp.float32), axis=0)
    small = lax.psum(small[:small_rows] + small[small_rows:], "eh")
    late_block = late[:, :block].transpose(1, 0, 2).reshape(block, group * length)
    grad_block = jnp.dot(late_block, left_all, preferred_element_type=jnp.float32)
    mine = lax.psum_scatter(grad_block, "eh", scatter_dimension=0, tiled=True)
    grads = lax.all_gather(mine.astype(jnp.bfloat16), "eh", axis=0, tiled=True)
    grads = lax.all_gather(grads, GROUP_AXES, axis=0, tiled=True)
    small = lax.all_gather(small, GROUP_AXES, axis=0, tiled=True)
    grads = grads.reshape(4, width, width).transpose(0, 2, 1).astype(jnp.float32)
    return grads, small


def per_device(
    tokens,
    norm_gain,
    w_query,
    w_key,
    w_value,
    w_output,
    rel_bias,
    ffn_gain,
    w_router,
    w_in,
    w_out,
    routes,
    lengths,
    cotangent,
):
    low_type = jnp.bfloat16
    length, model_width = tokens.shape
    experts = w_router.shape[1]
    eh_count = lax.axis_size("eh")
    group = lax.axis_size(GROUP_AXES)
    capacity = max(2, (5 * length + 4 * experts - 1) // (4 * experts))

    w_in_own, w_out_own = w_in[0], w_out[0]
    w_in_other, w_out_other = swap(w_in_own, "dc"), swap(w_out_own, "dc")
    tokens_all = lax.all_gather(tokens, GROUP_AXES, axis=0, tiled=True)

    inputs = tokens.astype(jnp.float32)
    live_mask = jnp.arange(length, dtype=jnp.int32) < lengths[0]
    factor_one = lax.rsqrt(jnp.mean(inputs * inputs, axis=-1, keepdims=True) + norm_eps)
    normed = (inputs * factor_one * norm_gain).astype(low_type)
    queries = jnp.dot(normed, w_query, preferred_element_type=jnp.float32).astype(low_type)
    keys_all = jnp.dot(normed, w_key, preferred_element_type=jnp.float32).astype(low_type)
    values_all = jnp.dot(normed, w_value, preferred_element_type=jnp.float32).astype(low_type)
    query_heads = queries.reshape(length, HEADS, HEAD_DIM)
    key_heads = keys_all.reshape(length, HEADS, HEAD_DIM)
    value_heads = values_all.reshape(length, HEADS, HEAD_DIM)
    buckets = bucket_index(length)
    bucket_onehot = buckets[:, :, None] == jnp.arange(BUCKETS, dtype=jnp.int32)
    bias_field = jnp.einsum(
        "qkb,bh->hqk",
        bucket_onehot.astype(jnp.float32),
        rel_bias,
        precision=lax.Precision.HIGHEST,
        preferred_element_type=jnp.float32,
    )
    scores = (
        jnp.einsum("qhe,khe->hqk", query_heads, key_heads, preferred_element_type=jnp.float32)
        * score_scale
        + bias_field
    )
    scores = jnp.where(live_mask[None, None, :], scores, masked_score)
    probs = jax.nn.softmax(scores, axis=-1)
    attn_weights = probs.astype(low_type)
    attended = jnp.einsum(
        "hqk,khe->qhe", attn_weights, value_heads, preferred_element_type=jnp.float32
    )
    attended = attended.reshape(length, model_width).astype(low_type)
    attended_all = lax.all_gather(attended, GROUP_AXES, axis=0, tiled=True)
    hidden = inputs + jnp.dot(attended, w_output, preferred_element_type=jnp.float32)
    factor_two = lax.rsqrt(jnp.mean(hidden * hidden, axis=-1, keepdims=True) + norm_eps)
    normed_two = (hidden * factor_two * ffn_gain).astype(low_type)
    logits = jnp.dot(normed_two, w_router, preferred_element_type=jnp.float32)
    router_probs = jax.nn.softmax(logits, axis=-1)
    choose = routes[:, 0][:, None] == jnp.arange(experts, dtype=jnp.int32)
    choose_int = choose.astype(jnp.int32)
    running = jnp.cumsum(choose_int * live_mask[:, None].astype(jnp.int32), axis=0)
    slot_index = jnp.sum(running * choose_int, axis=1) - 1
    kept_mask = live_mask & (slot_index < capacity)
    dispatch = (
        choose[:, :, None]
        & (slot_index[:, None, None] == jnp.arange(capacity, dtype=jnp.int32))
        & kept_mask[:, None, None]
    )
    dispatch_low = dispatch.astype(low_type)
    gate_value = jnp.sum(jnp.where(choose, router_probs, 0.0), axis=1)
    grad_top = cotangent.astype(jnp.float32)
    scaled_grad = (gate_value[:, None] * grad_top).astype(low_type)
    packed = jnp.einsum(
        "tec,td->ecd", dispatch_low, normed_two, preferred_element_type=jnp.float32
    ).astype(low_type)
    grad_packed = jnp.einsum(
        "tec,td->ecd", dispatch_low, scaled_grad, preferred_element_type=jnp.float32
    ).astype(low_type)
    outgoing = jnp.concatenate([packed, grad_packed], axis=1)
    outgoing = jnp.broadcast_to(outgoing[:, None], (experts, 2) + outgoing.shape[1:])
    outgoing = outgoing.reshape((experts * 2,) + outgoing.shape[2:])
    incoming = lax.all_to_all(outgoing, EXPERT_AXES, split_axis=0, concat_axis=0, tiled=True)
    incoming = incoming.reshape(-1, model_width)
    sent_back, expert_rows, grad_slots, active, d_inner = expert_rows_of(
        incoming, capacity, (w_in_own, w_out_own, w_in_other, w_out_other)
    )
    sent_back = sent_back.reshape(2 * experts, 2 * capacity, model_width)
    in_own, out_own, in_other, out_other = expert_grads_of(
        expert_rows, grad_slots, active, d_inner
    )
    came_back = lax.all_to_all(sent_back, EXPERT_AXES, split_axis=0, concat_axis=0, tiled=True)
    came_back = came_back.reshape(experts, 2, 2 * capacity, model_width).astype(jnp.float32)
    came_back = (came_back[:, 0] + came_back[:, 1]).astype(low_type)
    came_back, in_own, out_own, in_other, out_other = lax.optimization_barrier(
        (came_back, in_own, out_own, in_other, out_other)
    )
    grad_in = in_own + swap(in_other, "dc").astype(jnp.float32)
    grad_out = out_own + swap(out_other, "dc").astype(jnp.float32)

    returned = jnp.einsum(
        "tec,ecd->td", dispatch_low, came_back[:, :capacity], preferred_element_type=jnp.float32
    )
    output = (hidden + gate_value[:, None] * returned).astype(low_type)
    d_normed_two = jnp.einsum(
        "tec,ecd->td", dispatch_low, came_back[:, capacity:], preferred_element_type=jnp.float32
    )
    d_gate = jnp.sum(grad_top * returned, axis=1)
    d_router_probs = jnp.where(choose, d_gate[:, None], 0.0)
    d_logits = router_probs * (
        d_router_probs - jnp.sum(router_probs * d_router_probs, axis=1, keepdims=True)
    )
    d_logits = d_logits.astype(low_type)
    grad_router = dot_first(normed_two, d_logits)
    d_normed_two = d_normed_two + dot_last(d_logits, w_router)
    d_from_norm, grad_ffn = norm_backward(hidden, factor_two, ffn_gain, d_normed_two)
    d_hidden = grad_top + d_from_norm
    d_mixed = d_hidden.astype(low_type)
    d_attended = dot_last(d_mixed, w_output).astype(low_type).reshape(length, HEADS, HEAD_DIM)
    d_probs_attn = jnp.einsum(
        "qhe,khe->hqk", d_attended, value_heads, preferred_element_type=jnp.float32
    )
    grad_values = jnp.einsum(
        "hqk,qhe->khe", attn_weights, d_attended, preferred_element_type=jnp.float32
    )
    grad_values = grad_values.astype(low_type).reshape(length, model_width)
    d_scores = probs * (d_probs_attn - jnp.sum(probs * d_probs_attn, axis=-1, keepdims=True))
    d_scores = d_scores.astype(low_type)
    grad_queries = (
        jnp.einsum("hqk,khe->qhe", d_scores, key_heads, preferred_element_type=jnp.float32)
        * score_scale
    )
    grad_queries = grad_queries.astype(low_type).reshape(length, model_width)
    grad_keys = (
        jnp.einsum("hqk,qhe->khe", d_scores, query_heads, preferred_element_type=jnp.float32)
        * score_scale
    )
    grad_keys = grad_keys.astype(low_type).reshape(length, model_width)
    grad_bias = jnp.einsum(
        "hqk,qkb->bh", d_scores, bucket_onehot.astype(low_type), preferred_element_type=jnp.float32
    )
    d_normed = (
        dot_last(grad_queries, w_query)
        + dot_last(grad_keys, w_key)
        + dot_last(grad_values, w_value)
    )
    d_from_first, grad_norm = norm_backward(inputs, factor_one, norm_gain, d_normed)
    grad_input = (d_hidden + d_from_first).astype(low_type)

    small_sizes = (model_width, model_width, BUCKETS * HEADS, model_width * experts)
    small = jnp.concatenate(
        [grad_norm, grad_ffn, grad_bias.reshape(-1), grad_router.reshape(-1)]
    )
    small_rows = -(-small.shape[0] // (LANES * group))
    small = jnp.pad(small, (0, small_rows * group * LANES - small.shape[0]))
    small_high, small_low = split_two(small.reshape(group, small_rows, LANES))
    block = 4 * model_width // group
    factors = jnp.concatenate([grad_queries, grad_keys, grad_values, d_mixed], axis=1)
    factors = factors.T.reshape(group, block, length)
    late = jnp.concatenate([factors, small_high, small_low], axis=1)
    late = lax.all_to_all(late, GROUP_AXES, split_axis=0, concat_axis=0, tiled=True)
    inputs_all = tokens_all.astype(jnp.float32)
    factor_all = lax.rsqrt(jnp.mean(inputs_all * inputs_all, axis=-1, keepdims=True) + norm_eps)
    normed_all = (inputs_all * factor_all * norm_gain).astype(low_type)
    which = lax.axis_index(GROUP_AXES) // (group // 4)
    left_all = jnp.where(which == 3, attended_all, normed_all)
    late, left_all = lax.optimization_barrier((late, left_all))
    if eh_count == 2:
        grads, small = gathered_grads(late, left_all, small_rows)
    else:
        grads, small = gathered_grads_plain(late, left_all, small_rows)
    small = small.reshape(-1)
    pieces, at = [], 0
    for size in small_sizes:
        pieces.append(small[at : at + size])
        at += size
    return (
        output,
        grad_input,
        pieces[0],
        grads[0],
        grads[1],
        grads[2],
        grads[3],
        pieces[2].reshape(BUCKETS, HEADS),
        pieces[1],
        pieces[3].reshape(model_width, experts),
        grad_in[None],
        grad_out[None],
    )


def solution(mesh):
    exp_count, dp_count = mesh.shape["exp"], mesh.shape["dp"]
    fine = Mesh(
        mesh.devices.reshape(exp_count // 4, 2, 2, dp_count // 2, 2),
        TOKEN_AXES,
    )
    exp, dp = ("eh", "em", "ey"), ("dx", "dc")
    in_specs = (
        P(TOKEN_AXES, None),
        P(),
        P(),
        P(),
        P(),
        P(),
        P(),
        P(),
        P(),
        P(exp, None, dp),
        P(exp, dp, None),
        P(TOKEN_AXES, None),
        P(TOKEN_AXES),
        P(TOKEN_AXES, None),
    )
    out_specs = (
        P(TOKEN_AXES, None),
        P(TOKEN_AXES, None),
        P(),
        P(),
        P(),
        P(),
        P(),
        P(),
        P(),
        P(),
        P(exp, None, dp),
        P(exp, dp, None),
    )
    return jax.shard_map(
        per_device, mesh=fine, in_specs=in_specs, out_specs=out_specs, check_vma=False
    )
```

```python
import functools

import jax
import jax.numpy as jnp
import numpy as np
from jax import lax
from jax.experimental import pallas as pl
from jax.experimental.pallas import tpu as pltpu
from jax.sharding import Mesh
from jax.sharding import PartitionSpec as P

HEADS = 12
HEAD_DIM = 64
BUCKETS = 32
LANES = 128
VMEM_MIB = 63

norm_eps = 1e-06
score_scale = 0.125
masked_score = -1e30
far_limits = (11, 16, 22, 32, 45, 64, 90)

EXPERT_AXES = ("eh", "em", "ey", "dx")
GROUP_AXES = ("em", "ey", "dx", "dc")
TOKEN_AXES = ("eh", "em", "ey", "dx", "dc")


def bucket_of(offset):
    distance = jnp.abs(offset)
    far_bucket = jnp.full(distance.shape, 8, jnp.int32)
    for limit_value in far_limits:
        far_bucket = far_bucket + (distance >= limit_value).astype(jnp.int32)
    near_bucket = jnp.where(distance < 8, distance, far_bucket)
    return near_bucket + 16 * (offset > 0).astype(jnp.int32)


def dot_last(left_side, right_side):
    return lax.dot_general(
        left_side, right_side, (((1,), (1,)), ((), ())), preferred_element_type=jnp.float32
    )


def dot_first(left_side, right_side):
    return lax.dot_general(
        left_side, right_side, (((0,), (0,)), ((), ())), preferred_element_type=jnp.float32
    )


def norm_backward(values, factor, gain, grad_normed):
    scaled = gain * grad_normed
    grad_gain = jnp.sum(grad_normed * values * factor, axis=0, keepdims=True)
    grad_values = factor * scaled - values * factor * factor * factor * jnp.mean(
        scaled * values, axis=-1, keepdims=True
    )
    return (grad_values, grad_gain)


def swap(array, axis):
    return lax.ppermute(array, axis, perm=[(0, 1), (1, 0)])


def whole_spec():
    return pl.BlockSpec(memory_space=pltpu.VMEM)


def any_spec():
    return pl.BlockSpec(memory_space=pl.ANY)


def params(mib):
    return pltpu.CompilerParams(vmem_limit_bytes=mib * 1024 * 1024)


def cost(flops, moved):
    return pl.CostEstimate(flops=flops, bytes_accessed=moved, transcendentals=0)


def shaped(dims, kind):
    return jax.ShapeDtypeStruct(dims, kind)


class Arriving:
    def __init__(self, source, held, sem):
        self.held, self.pending = held, pltpu.make_async_copy(source, held, sem)
        self.pending.start()

    def ref(self):
        if self.pending is not None:
            self.pending.wait()
            self.pending = None
        return self.held

    def __getitem__(self, index):
        return self.ref()[index]

    @property
    def shape(self):
        return self.held.shape


class Leaving:
    def __init__(self, held, target, sem):
        self.held, self.copy = held, pltpu.make_async_copy(held, target, sem)

    def __setitem__(self, index, value):
        self.held[index] = value

    def __getitem__(self, index):
        return self.held[index]

    @property
    def shape(self):
        return self.held.shape

    def send(self):
        self.copy.start()

    def finish(self):
        self.copy.wait()


class Staying:
    def __init__(self, held):
        self.held = held

    def __setitem__(self, index, value):
        self.held[index] = value

    def __getitem__(self, index):
        return self.held[index]

    @property
    def shape(self):
        return self.held.shape

    def send(self):
        pass


def staged(
    kernel,
    name,
    scalars,
    inputs,
    outputs,
    scratch,
    flops,
    moved,
    residents=(),
    kept=(),
    mib=VMEM_MIB,
):
    counts = (len(scalars), len(residents), len(inputs), len(kept), len(outputs))

    def body(*refs):
        refs = list(refs)
        take = lambda count: [refs.pop(0) for _ in range(count)]
        numbers, there, sources, staying, targets = [take(count) for count in counts]
        held_in, held_out = take(counts[2]), take(counts[4])
        sems = refs.pop(0)
        arriving = [
            Arriving(source, held, sems.at[i])
            for i, (source, held) in enumerate(zip(sources, held_in))
        ]
        leaving = [
            Leaving(held, target, sems.at[counts[2] + i])
            for i, (held, target) in enumerate(zip(held_out, targets))
        ]
        kernel(numbers, there + arriving, [Staying(ref) for ref in staying] + leaving, refs)
        for copy in leaving:
            copy.finish()

    return pl.pallas_call(
        body,
        out_shape=tuple(kept) + tuple(outputs),
        in_specs=[pl.BlockSpec(memory_space=pltpu.SMEM)] * counts[0]
        + [whole_spec()] * counts[1]
        + [any_spec()] * counts[2],
        out_specs=(whole_spec(),) * counts[3] + (any_spec(),) * counts[4],
        scratch_shapes=[pltpu.VMEM(x.shape, x.dtype) for x in inputs]
        + [pltpu.VMEM(x.shape, x.dtype) for x in outputs]
        + [pltpu.SemaphoreType.DMA((max(1, counts[2] + counts[4]),))]
        + list(scratch),
        compiler_params=params(mib),
        cost_estimate=cost(flops, moved),
        name=name,
    )(*scalars, *residents, *inputs)


def row_of(ref):
    return jnp.concatenate([ref[i : i + 1] for i in range(ref.shape[0])], axis=1)


def rms_factor(values):
    return lax.rsqrt(jnp.mean(values * values, axis=-1, keepdims=True) + norm_eps)


def pair_masks(rows):
    first = lax.broadcasted_iota(jnp.int32, (rows, LANES), 1) < HEAD_DIM
    return first


def stacked_heads(pair, first):
    zero = jnp.zeros_like(pair)
    return jnp.concatenate([jnp.where(first, pair, zero), jnp.where(first, zero, pair)], axis=0)


def offset_buckets(rows, length):
    lane = lax.broadcasted_iota(jnp.int32, (rows, 2 * length), 1)
    return bucket_of(jnp.where(lane < length, lane, lane - 2 * length))


def forward_kernel(numbers, inputs, outputs, scratch):
    (count_ref,) = numbers
    (
        tokens_ref,
        gain_ref,
        query_ref,
        key_ref,
        value_ref,
        bias_ref,
        routes_ref,
        output_ref,
        gain_two_ref,
        router_ref,
        cotangent_ref,
    ) = inputs
    (
        outgoing_ref,
        attended_ref,
        q_ref,
        k_ref,
        v_ref,
        probs_ref,
        hidden_ref,
        router_probs_ref,
        choose_ref,
        slot_ref,
    ) = outputs
    low = jnp.bfloat16
    length, width = tokens_ref.shape
    experts = router_ref.shape[0]
    capacity = outgoing_ref.shape[2] // 2
    inputs = tokens_ref[...].astype(jnp.float32)
    normed = (inputs * rms_factor(inputs) * row_of(gain_ref)).astype(low)
    for weight, out in ((query_ref, q_ref), (key_ref, k_ref), (value_ref, v_ref)):
        out[...] = jnp.dot(normed, weight[...], preferred_element_type=jnp.float32).astype(low)
        out.send()

    buckets = offset_buckets(BUCKETS, length)
    hot = buckets == lax.broadcasted_iota(jnp.int32, buckets.shape, 0)
    table = jnp.dot(
        bias_ref[...],
        jnp.where(hot, 1.0, 0.0),
        precision=lax.Precision.HIGHEST,
        preferred_element_type=jnp.float32,
    )
    live = lax.broadcasted_iota(jnp.int32, (length, length), 1) < count_ref[0]
    first = pair_masks(length)
    for pair in range(HEADS // 2):
        lanes = slice(pair * LANES, (pair + 1) * LANES)
        scores = dot_last(q_ref[:, lanes], stacked_heads(k_ref[:, lanes], first)) * score_scale
        weights = []
        for head in range(2):
            row = table[2 * pair + head : 2 * pair + head + 1]
            field = pltpu.roll(
                jnp.broadcast_to(row, (length, 2 * length)), 0, 1, stride=1, stride_axis=0
            )
            own = scores[:, head * length : (head + 1) * length] + field[:, :length]
            own = jnp.where(live, own, masked_score)
            own = jnp.exp(own - jnp.max(own, axis=1, keepdims=True))
            own = own / jnp.sum(own, axis=1, keepdims=True)
            probs_ref[pair, :, head * length : (head + 1) * length] = own
            weights.append(own.astype(low))
        both = jnp.concatenate(weights, axis=1)
        attended_ref[:, lanes] = jnp.dot(
            both, stacked_heads(v_ref[:, lanes], first), preferred_element_type=jnp.float32
        ).astype(low)

    attended_ref.send()
    probs_ref.send()
    hidden = inputs + jnp.dot(
        attended_ref[...], output_ref[...], preferred_element_type=jnp.float32
    )
    hidden_ref[...] = hidden
    hidden_ref.send()
    normed_two = (hidden * rms_factor(hidden) * row_of(gain_two_ref)).astype(low)
    logits = dot_last(normed_two, router_ref[...])
    router_probs = jnp.exp(logits - jnp.max(logits, axis=1, keepdims=True))
    router_probs = router_probs / jnp.sum(router_probs, axis=1, keepdims=True)
    router_probs_ref[...] = router_probs
    router_probs_ref.send()

    lane = lax.broadcasted_iota(jnp.int32, (length, length), 1)
    place = lax.broadcasted_iota(jnp.int32, (length, length), 0)
    routes = routes_ref[...]
    chosen = routes == lax.broadcasted_iota(jnp.int32, (experts, length), 0)
    chosen = jnp.where(chosen, 1.0, 0.0)
    alive = lax.broadcasted_iota(jnp.int32, (1, length), 1) < count_ref[0]
    before = jnp.where(place <= lane, 1.0, 0.0).astype(low)
    running = jnp.dot(
        (chosen * jnp.where(alive, 1.0, 0.0)).astype(low),
        before,
        preferred_element_type=jnp.float32,
    )
    slot = jnp.sum(running * chosen, axis=0, keepdims=True).astype(jnp.int32) - 1
    kept = alive & (slot < capacity)
    column = jnp.where(kept, routes * (2 * capacity) + slot, -2 * capacity)
    slot_ref[...] = column
    slot_ref.send()
    unit = jnp.where(place == lane, 1.0, 0.0).astype(low)
    choose = dot_last(unit, chosen.astype(low))
    choose_ref[...] = choose
    choose_ref.send()
    gate = jnp.sum(router_probs * choose, axis=1, keepdims=True)
    scaled = (gate * cotangent_ref[...].astype(jnp.float32)).astype(low)
    row = lax.broadcasted_iota(jnp.int32, (experts * 2 * capacity, length), 0)
    spread = jnp.concatenate(
        [
            jnp.where(row == column, 1.0, 0.0).astype(low),
            jnp.where(row == column + capacity, 1.0, 0.0).astype(low),
        ],
        axis=1,
    )
    packed = jnp.dot(
        spread,
        jnp.concatenate([normed_two, scaled], axis=0),
        preferred_element_type=jnp.float32,
    )
    for expert in range(experts):
        rows = packed[expert * 2 * capacity : (expert + 1) * 2 * capacity].astype(low)
        outgoing_ref[expert, 0] = rows
        outgoing_ref[expert, 1] = rows
    outgoing_ref.send()


def forward_of(count, tokens, gain, weights, bias, gain_two, router, routes, cotangent, capacity):
    length, width = tokens.shape
    experts = router.shape[0]
    low = jnp.bfloat16
    outputs = (
        shaped((experts, 2, 2 * capacity, width), low),
        shaped((length, width), low),
        shaped((length, width), low),
        shaped((length, width), low),
        shaped((length, width), low),
        shaped((HEADS // 2, length, 2 * length), jnp.float32),
        shaped((length, width), jnp.float32),
        shaped((length, experts), jnp.float32),
        shaped((length, experts), jnp.float32),
        shaped((1, length), jnp.int32),
    )
    query, key, value, output = weights
    inputs = (tokens, gain, query, key, value, bias, routes, output, gain_two, router, cotangent)
    return staged(
        forward_kernel,
        "forward",
        (count,),
        inputs,
        outputs,
        (),
        10 * length * width * width,
        10 * width * width,
    )


def backward_kernel(numbers, inputs, outputs, scratch):
    (
        came_ref,
        slot_ref,
        hidden_ref,
        router_probs_ref,
        choose_ref,
        cotangent_ref,
        gain_two_ref,
        router_ref,
        output_ref,
        v_ref,
        probs_ref,
        q_ref,
        k_ref,
        query_ref,
        key_ref,
        value_ref,
        tokens_ref,
        gain_ref,
    ) = inputs
    out_ref, grad_ref, late_ref = outputs
    turned, sums, tail = scratch
    low = jnp.bfloat16
    length, width = tokens_ref.shape
    experts = router_ref.shape[0]
    capacity = came_ref.shape[2] // 2
    group = late_ref.shape[0]
    small_rows = tail.shape[0] // group
    top = cotangent_ref[...].astype(jnp.float32)
    slots = experts * 2 * capacity
    came = came_ref[:, 0].astype(jnp.float32) + came_ref[:, 1].astype(jnp.float32)
    came = came.reshape(slots, width).astype(low)
    row = lax.broadcasted_iota(jnp.int32, (slots, length), 0)
    column = slot_ref[...]
    spread = jnp.concatenate(
        [
            jnp.where(row == column, 1.0, 0.0).astype(low),
            jnp.where(row == column + capacity, 1.0, 0.0).astype(low),
        ],
        axis=1,
    )
    back = dot_first(spread, came)
    returned, d_normed_two = back[:length], back[length:]
    hidden = hidden_ref[...]
    router_probs, choose = router_probs_ref[...], choose_ref[...]
    gate = jnp.sum(router_probs * choose, axis=1, keepdims=True)
    out_ref[...] = (hidden + gate * returned).astype(low)
    out_ref.send()
    d_gate = jnp.sum(top * returned, axis=1, keepdims=True)
    d_probs = choose * d_gate
    d_logits = router_probs * (
        d_probs - jnp.sum(router_probs * d_probs, axis=1, keepdims=True)
    )
    d_logits = d_logits.astype(low)
    factor = rms_factor(hidden)
    gain_two = row_of(gain_two_ref)
    normed_two = (hidden * factor * gain_two).astype(low)
    grad_router = dot_first(d_logits, normed_two)
    d_normed_two = d_normed_two + jnp.dot(
        d_logits, router_ref[...], preferred_element_type=jnp.float32
    )
    d_from_norm, grad_ffn = norm_backward(hidden, factor, gain_two, d_normed_two)
    d_hidden = top + d_from_norm
    d_mixed = d_hidden.astype(low)
    d_attended = dot_last(d_mixed, output_ref[...]).astype(low)
    flipped = d_mixed.T
    for head in range(HEADS):
        at = 3 * HEADS + head
        late_ref[at // 3, at % 3 * HEAD_DIM : (at % 3 + 1) * HEAD_DIM] = flipped[
            head * HEAD_DIM : (head + 1) * HEAD_DIM
        ]

    first = pair_masks(length)
    upper = lax.broadcasted_iota(jnp.int32, (LANES, length), 0) < HEAD_DIM
    lane = lax.broadcasted_iota(jnp.int32, (length, length), 1)
    place = lax.broadcasted_iota(jnp.int32, (length, length), 0)
    reverse = jnp.where(place + lane == length - 1, 1.0, 0.0).astype(low)
    for pair in range(HEADS // 2):
        lanes = slice(pair * LANES, (pair + 1) * LANES)
        upstream = d_attended[:, lanes]
        probs = probs_ref[pair]
        d_probs = dot_last(upstream, stacked_heads(v_ref[:, lanes], first))
        parts = []
        for head in range(2):
            span = slice(head * length, (head + 1) * length)
            own, grad = probs[:, span], d_probs[:, span]
            parts.append(own * (grad - jnp.sum(own * grad, axis=1, keepdims=True)))
        d_scores = jnp.concatenate(parts, axis=1).astype(low)
        d_values = dot_first(upstream, probs.astype(low))
        d_values = jnp.where(upper, d_values[:, :length], d_values[:, length:])
        d_keys = dot_first(q_ref[:, lanes], d_scores) * score_scale
        d_keys = jnp.where(upper, d_keys[:, :length], d_keys[:, length:])
        d_queries = jnp.dot(
            d_scores, stacked_heads(k_ref[:, lanes], first), preferred_element_type=jnp.float32
        )
        d_queries = (d_queries * score_scale).astype(low)
        for which, value in enumerate(
            (d_queries.T, d_keys.astype(low), d_values.astype(low))
        ):
            turned[which, lanes] = value
            for head in range(2):
                at = which * HEADS + 2 * pair + head
                late_ref[at // 3, at % 3 * HEAD_DIM : (at % 3 + 1) * HEAD_DIM] = value[
                    head * HEAD_DIM : (head + 1) * HEAD_DIM
                ]
        upside = jnp.dot(reverse, d_scores, preferred_element_type=jnp.float32)
        for head in range(2):
            own = upside[:, head * length : (head + 1) * length]
            own = jnp.concatenate([own, jnp.zeros_like(own)], axis=1)
            own = pltpu.roll(own, 0, 1, stride=1, stride_axis=0)
            at = 2 * pair + head
            sums[at % 4, at // 4 : at // 4 + 1] = jnp.sum(own, axis=0, keepdims=True)

    d_normed = 0.0
    for which, weight in enumerate((query_ref, key_ref, value_ref)):
        d_normed = d_normed + lax.dot_general(
            turned[which],
            weight[...],
            (((0,), (1,)), ((), ())),
            preferred_element_type=jnp.float32,
        )
    inputs = tokens_ref[...].astype(jnp.float32)
    d_first, grad_norm = norm_backward(
        inputs, rms_factor(inputs), row_of(gain_ref), d_normed
    )
    grad_ref[...] = (d_hidden + d_first).astype(low)
    grad_ref.send()

    shift = lax.broadcasted_iota(jnp.int32, (2 * length, LANES), 0) - (length - 1)
    bucket = bucket_of(shift)
    lane_wide = lax.broadcasted_iota(jnp.int32, (2 * length, LANES), 1)
    bias_rows = 0.0
    for quarter in range(4):
        hot = jnp.where(bucket + quarter * BUCKETS == lane_wide, 1.0, 0.0)
        bias_rows = bias_rows + jnp.dot(
            sums[quarter],
            hot,
            precision=lax.Precision.HIGHEST,
            preferred_element_type=jnp.float32,
        )
    chunks = width // LANES
    tail[...] = jnp.zeros_like(tail)
    for chunk in range(chunks):
        lanes = slice(chunk * LANES, (chunk + 1) * LANES)
        tail[chunk : chunk + 1] = grad_norm[:, lanes]
        tail[chunks + chunk : chunks + chunk + 1] = grad_ffn[:, lanes]
        for expert in range(experts):
            at = 2 * chunks + HEADS // 4 + expert * chunks + chunk
            tail[at : at + 1] = grad_router[expert : expert + 1, lanes]
    tail[2 * chunks : 2 * chunks + HEADS // 4] = bias_rows[: HEADS // 4]
    block = 4 * width // group
    for at in range(group):
        own = tail[at * small_rows : (at + 1) * small_rows]
        high = own.astype(low).astype(jnp.float32)
        late_ref[at, block:] = jnp.concatenate([high, own - high], axis=0).astype(low)
    late_ref.send()


def backward_of(came, tokens, gain, weights, gain_two, router, cotangent, saved, group):
    length, width = tokens.shape
    experts = router.shape[0]
    low = jnp.bfloat16
    small_rows = -(-small_count(width, experts) // group)
    block = 4 * width // group
    outputs = (
        shaped((length, width), low),
        shaped((length, width), low),
        shaped((group, block + 2 * small_rows, length), low),
    )
    scratch = (
        pltpu.VMEM((3, width, length), low),
        pltpu.VMEM((4, 8, 2 * length), jnp.float32),
        pltpu.VMEM((group * small_rows, LANES), jnp.float32),
    )
    query, key, value, output = weights
    q, k, v, probs, hidden, router_probs, choose, slot = saved
    inputs = (slot, hidden, router_probs, choose, cotangent, gain_two, router, output)
    inputs = inputs + (v, probs, q, k, query, key, value, tokens, gain)
    return staged(
        backward_kernel,
        "backward",
        (),
        inputs,
        outputs,
        scratch,
        10 * length * width * width,
        10 * width * width,
        residents=(came,),
        mib=62,
    )


def small_count(width, experts):
    return (2 + experts) * (width // LANES) + HEADS // 4


def pick_kernel(numbers, inputs, outputs, scratch):
    (which_ref,), (*pieces, tokens_ref) = numbers, inputs
    which = which_ref[0]
    pieces = [piece.ref() for piece in pieces]
    rows = pieces[0].shape[0]
    tokens_ref = tokens_ref.ref()
    if len(pieces) > 1:
        for part, piece in enumerate(pieces):
            outputs[0][part * rows : (part + 1) * rows] = piece[...]
        outputs[0].send()
    for out, turn in zip(outputs[-2:], (3, 2)):

        @pl.when(which == turn)
        def _():
            for part, piece in enumerate(pieces):
                out[part * rows : (part + 1) * rows] = piece[...]

        @pl.when(which != turn)
        def _():
            out[...] = tokens_ref[...]

        out.send()


def picked(which, pieces, tokens):
    outputs = (shaped(tokens.shape, tokens.dtype),) * (2 if len(pieces) == 1 else 3)
    return staged(
        pick_kernel,
        "picked",
        (which,),
        (*pieces, tokens),
        outputs,
        (),
        0,
        10 * tokens.size,
    )


def left_kernel(numbers, inputs, outputs, scratch):
    (which_ref,), (*pieces, gain_ref), (left_ref,) = numbers, inputs, outputs
    which = which_ref[0]
    scale = row_of(gain_ref)
    for number, piece in enumerate(pieces):
        held = piece.ref()
        count = held.shape[0]
        spans = [
            (at, slice(number * count + at, number * count + at + LANES))
            for at in range(0, count, LANES)
        ]

        @pl.when(which < 3)
        def _():
            for at, span in spans:
                own = held[at : at + LANES].astype(jnp.float32)
                own = (own * rms_factor(own) * scale).astype(jnp.bfloat16)
                left_ref[:, span] = own.T

        @pl.when(which == 3)
        def _():
            for at, span in spans:
                left_ref[:, span] = held[at : at + LANES].T

    left_ref.send()


def left_of(which, pieces, gain):
    count, width = pieces[0].shape
    total = count * len(pieces)
    kept = (shaped((width, total), jnp.bfloat16),)
    inputs = (*pieces, gain)
    (left,) = staged(
        left_kernel,
        "left",
        (which,),
        inputs,
        (),
        (),
        10 * total * width,
        6 * total * width,
        kept=kept,
        mib=60,
    )
    return left


gelu_scale = 0.7978845608028654
gelu_cubic = 0.044715


def expert_kernel(numbers, inputs, outputs, scratch):
    rows_ref, order_ref, in_a, out_a, in_b, out_b = inputs
    back_ref, rows_out, grads_out, act_ref, inner_ref = outputs
    count = rows_ref.shape[0]
    half = count // 2
    lanes = lax.broadcasted_iota(jnp.int32, (count, count), 1)
    sort = jnp.where(order_ref[:, 0:1] == lanes, 1.0, 0.0).astype(jnp.bfloat16)
    unsort = jnp.where(order_ref[:, 1:2] == lanes, 1.0, 0.0).astype(jnp.bfloat16)
    ordered = jnp.dot(sort, rows_ref[...], preferred_element_type=jnp.float32)
    ordered = ordered.astype(jnp.bfloat16)
    rows, slots = ordered[:half], ordered[half:]
    rows_out[...] = rows
    rows_out.send()
    grads_out[...] = slots
    grads_out.send()
    result, d_rows = 0.0, 0.0
    for part, (part_in, part_out) in enumerate(((in_a, out_a), (in_b, out_b))):
        inner = jnp.dot(rows, part_in[...], preferred_element_type=jnp.float32)
        upstream = dot_last(slots, part_out[...])
        square = inner * inner
        bent = jnp.tanh(gelu_scale * (inner + gelu_cubic * (square * inner)))
        active = (inner * (0.5 * (1.0 + bent))).astype(jnp.bfloat16)
        slope = 0.5 * (1.0 + bent) + 0.5 * inner * (1.0 - bent * bent) * (
            gelu_scale * (1.0 + 3.0 * gelu_cubic * square)
        )
        d_inner = (upstream * slope).astype(jnp.bfloat16)
        act_ref[part] = active
        inner_ref[part] = d_inner
        result = result + jnp.dot(active, part_out[...], preferred_element_type=jnp.float32)
        d_rows = d_rows + dot_last(d_inner, part_in[...])
    act_ref.send()
    inner_ref.send()
    both = jnp.concatenate([result.astype(jnp.bfloat16), d_rows.astype(jnp.bfloat16)], axis=0)
    back_ref[...] = jnp.dot(unsort, both, preferred_element_type=jnp.float32).astype(jnp.bfloat16)
    back_ref.send()


def expert_rows_of(rows, capacity, part_weights):
    count, width = rows.shape
    half = count // 2
    place = np.arange(count)
    sort = place % half // capacity * 2 * capacity + place // half * capacity + place % capacity
    unsort = np.empty_like(sort)
    unsort[sort] = place
    order = jnp.asarray(np.stack([sort, unsort], axis=1), jnp.int32)
    hidden_width = part_weights[0].shape[1]
    low = jnp.bfloat16
    outputs = (
        shaped((count, width), low),
        shaped((half, width), low),
        shaped((half, width), low),
        shaped((2, half, hidden_width), low),
        shaped((2, half, hidden_width), low),
    )
    return staged(
        expert_kernel,
        "expert_rows",
        (),
        (order, *part_weights),
        outputs,
        (),
        16 * half * width * hidden_width,
        12 * width * width,
        residents=(rows,),
        mib=62,
    )


def expert_grads_kernel(numbers, inputs, outputs, scratch):
    rows_ref, inner_ref, act_ref, slots_ref = inputs
    sent_in, sent_out, own_in, own_out = outputs
    sent_in[...] = dot_first(rows_ref[...], inner_ref[1]).astype(jnp.bfloat16)
    sent_in.send()
    sent_out[...] = dot_first(act_ref[1], slots_ref[...]).astype(jnp.bfloat16)
    sent_out.send()
    own_in[...] = dot_first(rows_ref[...], inner_ref[0])
    own_in.send()
    own_out[...] = dot_first(act_ref[0], slots_ref[...])
    own_out.send()


def expert_grads_of(rows, slots, active, d_inner):
    half, width = rows.shape
    hidden_width = active.shape[2]
    outputs = (
        shaped((width, hidden_width), jnp.bfloat16),
        shaped((hidden_width, width), jnp.bfloat16),
        shaped((width, hidden_width), jnp.float32),
        shaped((hidden_width, width), jnp.float32),
    )
    return staged(
        expert_grads_kernel,
        "expert_grads",
        (),
        (rows, d_inner, active, slots),
        outputs,
        (),
        8 * half * width * hidden_width,
        12 * width * width,
    )


def block_kernel(numbers, inputs, outputs, scratch):
    (bits_ref,), (late_ref, left_ref), (block_ref,) = numbers, inputs, outputs
    group = late_ref.shape[0]
    part = left_ref.shape[0] // 2
    block = left_ref.shape[0] * 4 // group
    edge = block - LANES
    half = part // 2
    small_rows = (block_ref.shape[1] - part - half) // 2
    odd = bits_ref[3] == 1
    which = bits_ref[0] * 2 + bits_ref[1]
    here = which * 4 + bits_ref[2] * 2 + bits_ref[3]
    right = jnp.concatenate(
        [late_ref[here ^ factor_order(i, which), :block] for i in range(group)], axis=1
    )
    right = jnp.where(odd, jnp.concatenate([right[edge:], right[:edge]], axis=0), right)
    total = dot_last(left_ref[...], right)
    first = pair_masks(half)
    tail = jnp.sum(late_ref[:, block:].astype(jnp.float32), axis=0)
    small = tail[:small_rows] + tail[small_rows:]
    high = small.astype(jnp.bfloat16).astype(jnp.float32)
    both = jnp.concatenate([high, small - high], axis=0).astype(jnp.bfloat16)
    for side in range(2):
        own = total[side * part : (side + 1) * part]
        block_ref[side, :part] = own[:, :LANES].astype(jnp.bfloat16)
        rest = own[:, LANES:]
        rest = jnp.concatenate([rest, rest], axis=1)
        upper, lower = rest[:half], rest[half:]
        even = jnp.where(first, upper, lower)
        packed = jnp.where(odd, jnp.where(first, lower, upper), even)
        block_ref[side, part : part + half] = packed.astype(jnp.bfloat16)
        block_ref[side, part + half :] = both


def block_of(bits, late, left, small_rows):
    group, rows, length = late.shape
    width = left.shape[0]
    kept = (shaped((2, 3 * width // 4 + 2 * small_rows, LANES), jnp.bfloat16),)
    (block,) = staged(
        block_kernel,
        "grad_block",
        (bits,),
        (),
        (),
        (),
        8 * width * width * length,
        2 * left.size,
        residents=(late, left),
        kept=kept,
        mib=24,
    )
    return block


def share_kernel(numbers, inputs, outputs, scratch):
    (own_ref, got_ref), (share_ref,) = inputs, outputs
    small_rows = scratch[0].shape[0]
    edge = own_ref.shape[1] - 2 * small_rows
    for side in range(2):
        own = own_ref[side, :edge].astype(jnp.float32) + got_ref[side, :edge].astype(jnp.float32)
        share_ref[side, :edge] = own.astype(jnp.bfloat16)
        own, got = own_ref[side, edge:].astype(jnp.float32), got_ref[side, edge:].astype(jnp.float32)
        small = (own[:small_rows] + own[small_rows:]) + (got[:small_rows] + got[small_rows:])
        high = small.astype(jnp.bfloat16).astype(jnp.float32)
        share_ref[side, edge:] = jnp.concatenate([high, small - high], axis=0).astype(jnp.bfloat16)


def share_of(own, got, small_rows):
    (share,) = staged(
        share_kernel,
        "share",
        (),
        (),
        (),
        (pltpu.VMEM((small_rows, LANES), jnp.float32),),
        own.size,
        6 * own.size,
        residents=(own, got),
        kept=(shaped(own.shape, own.dtype),),
        mib=8,
    )
    return share


def assemble_kernel(part, small_rows, bits_ref, *refs):
    sources, outs = refs[:16], refs[16:20]
    norm_out, ffn_out, bias_out, router_out = refs[20:24]
    held, made, tail, in_sems, out_sems = refs[24:]
    em, ey, dx, dc = [bits_ref[i] for i in range(4)]
    half = part // 2
    edge = part + half
    copies = [[] for _ in range(4)]
    for number, source in enumerate(sources):
        core, weight, step = dc ^ (number // 8), number // 2 % 4, number % 2
        copies[weight].append(
            pltpu.make_async_copy(
                source, held.at[weight, (dx ^ step) * 2 + core], in_sems.at[number]
            )
        )
    for weight in range(4):
        for copy in copies[weight]:
            copy.start()
    first = pair_masks(half)
    for weight in range(4):
        for copy in copies[weight]:
            copy.wait()
        for side in range(2):
            rows = slice(side * part, (side + 1) * part)
            upper = slice(side * part, side * part + half)
            lower = slice(side * part + half, (side + 1) * part)
            for twin in range(2):
                even, odd = 2 * twin, 2 * twin + 1
                at = 3 * twin * LANES
                made[weight, rows, at : at + LANES] = held[weight, even, side, :part].astype(
                    jnp.float32
                )
                made[weight, rows, at + 2 * LANES : at + 3 * LANES] = held[
                    weight, odd, side, :part
                ].astype(jnp.float32)
                left = held[weight, even, side, part:edge].astype(jnp.float32)
                right = held[weight, odd, side, part:edge].astype(jnp.float32)
                middle = slice(at + LANES, at + 2 * LANES)
                made[weight, upper, middle] = jnp.where(first, left, right)
                made[weight, lower, middle] = pltpu.roll(
                    jnp.where(first, right, left), HEAD_DIM, 1
                )
        truth = (em ^ (weight // 2)) * 2 + (ey ^ (weight % 2))
        for i in range(4):

            @pl.when(truth == i)
            def _():
                pltpu.make_async_copy(made.at[weight], outs[i], out_sems.at[weight]).start()

        for i in range(4):
            own = held[weight, i, 0, edge:].astype(jnp.float32)
            tail[truth, i] = own[:small_rows] + own[small_rows:]

    def small_row(at):
        at, row = divmod(at, small_rows)
        return tail[at // 4, at % 4, row : row + 1]

    chunks = made.shape[2] // LANES
    for chunk in range(chunks):
        lanes = slice(chunk * LANES, (chunk + 1) * LANES)
        norm_out[chunk : chunk + 1] = small_row(chunk)
        ffn_out[chunk : chunk + 1] = small_row(chunks + chunk)
        for expert in range(router_out.shape[0]):
            router_out[expert : expert + 1, lanes] = small_row(
                2 * chunks + HEADS // 4 + expert * chunks + chunk
            )
    for head in range(HEADS):
        at = head % 4 * BUCKETS
        bias_out[head : head + 1] = small_row(2 * chunks + head // 4)[:, at : at + BUCKETS]

    for weight in range(4):
        truth = (em ^ (weight // 2)) * 2 + (ey ^ (weight % 2))
        for i in range(4):

            @pl.when(truth == i)
            def _():
                pltpu.make_async_copy(made.at[weight], outs[i], out_sems.at[weight]).wait()


def assemble(bits, sources, small_rows, width, experts):
    return pl.pallas_call(
        functools.partial(assemble_kernel, width // 2, small_rows),
        out_shape=(shaped((width, width), jnp.float32),) * 4
        + (
            shaped((width // LANES, LANES), jnp.float32),
            shaped((width // LANES, LANES), jnp.float32),
            shaped((HEADS, BUCKETS), jnp.float32),
            shaped((experts, width), jnp.float32),
        ),
        in_specs=[pl.BlockSpec(memory_space=pltpu.SMEM)] + [whole_spec()] * 16,
        out_specs=(any_spec(),) * 4 + (whole_spec(),) * 4,
        scratch_shapes=[
            pltpu.VMEM((4, 4) + sources[0].shape, jnp.bfloat16),
            pltpu.VMEM((4, width, width), jnp.float32),
            pltpu.VMEM((4, 4, small_rows, LANES), jnp.float32),
            pltpu.SemaphoreType.DMA((16,)),
            pltpu.SemaphoreType.DMA((4,)),
        ],
        compiler_params=params(32),
        cost_estimate=cost(8 * width * width, 24 * width * width),
        name="assemble",
    )(bits, *sources)


def place_in_group():
    place = [lax.axis_index(axis) for axis in ("em", "ey", "dx", "dc")]
    return (2 * place[0] + place[1]).astype(jnp.int32), jnp.stack(place).astype(jnp.int32)


def factor_order(at, which):
    low, high = at & 1, at >> 1 & 1
    turned = jnp.where(which == 3, 2 * low + 8 * high, 8 * low + 2 * high)
    return turned + (at >> 2 & 1) * 4 + (at >> 3)


def with_other(rows, axis):
    return jnp.concatenate([rows, swap(rows, axis)], axis=0)


def gathered_grads(late, left, place, small_rows, experts, beside):
    width = left.shape[0]
    block = block_of(place, late, left, small_rows)
    block, beside = lax.optimization_barrier((block, beside))
    beside = [own + other.astype(jnp.float32) for own, other in beside]
    got, beside = lax.optimization_barrier((swap(block, "eh"), beside))
    near = share_of(block, got, small_rows)
    far, near_x, near_y = swap(near, "em"), swap(near, "dx"), swap(near, "ey")
    far_x, far_y = swap(far, "dx"), swap(far, "ey")
    near_both, far_both = swap(near_x, "ey"), swap(far_y, "dx")
    sources = (near, near_x, near_y, near_both, far, far_x, far_y, far_both)
    sources = sources + tuple(swap(source, "dc") for source in sources)
    return assemble(place, sources, small_rows, width, experts), beside


def gathered_grads_plain(late, left, place, small_rows, experts, beside):
    group, rows, length = late.shape
    width = left.shape[0]
    block = 4 * width // group
    small = jnp.sum(late[:, block:].astype(jnp.float32), axis=0)
    small = lax.psum(small[:small_rows] + small[small_rows:], "eh")
    which = place_in_group()[0]
    order = jnp.stack([factor_order(at, which) for at in range(group)])
    order = order ^ lax.axis_index(GROUP_AXES)
    late_block = jnp.take(late[:, :block], order, axis=0)
    late_block = late_block.transpose(1, 0, 2).reshape(block, group * length)
    grad_block = dot_last(late_block, left)
    mine = lax.psum_scatter(grad_block, "eh", scatter_dimension=0, tiled=True)
    grads = lax.all_gather(mine.astype(jnp.bfloat16), "eh", axis=0, tiled=True)
    grads = lax.all_gather(grads, GROUP_AXES, axis=0, tiled=True)
    small = lax.all_gather(small, GROUP_AXES, axis=0, tiled=True).reshape(-1)
    grads = grads.reshape(4, width, width).transpose(0, 2, 1).astype(jnp.float32)
    sizes = (width, width, HEADS * BUCKETS, experts * width)
    ends = np.cumsum(sizes)
    pieces = [small[end - size : end] for end, size in zip(ends, sizes)]
    pieces[2], pieces[3] = pieces[2].reshape(HEADS, BUCKETS), pieces[3].reshape(experts, width)
    return (*grads, *pieces), [own + other.astype(jnp.float32) for own, other in beside]


def per_device(
    tokens,
    norm_gain,
    w_query,
    w_key,
    w_value,
    w_output,
    rel_bias,
    ffn_gain,
    w_router,
    w_in,
    w_out,
    routes,
    lengths,
    cotangent,
):
    length, model_width = tokens.shape
    experts = w_router.shape[1]
    group = lax.axis_size(GROUP_AXES)
    capacity = max(2, (5 * length + 4 * experts - 1) // (4 * experts))
    small_rows = -(-small_count(model_width, experts) // group)
    gain_one, gain_two = norm_gain.reshape(-1, LANES), ffn_gain.reshape(-1, LANES)
    weights = (w_query, w_key, w_value, w_output)
    router = w_router.T

    w_in_own, w_out_own = w_in[0], w_out[0]
    w_in_other, w_out_other = swap(w_in_own, "dc"), swap(w_out_own, "dc")
    outgoing, attended, *saved = forward_of(
        lengths,
        tokens,
        gain_one,
        weights,
        rel_bias.T,
        gain_two,
        router,
        routes.reshape(1, length),
        cotangent,
        capacity,
    )
    which, place = place_in_group()
    outgoing, near_tokens = lax.optimization_barrier((outgoing, with_other(tokens, "em")))
    outgoing = outgoing.reshape(2 * experts, 2 * capacity, model_width)
    incoming = lax.all_to_all(outgoing, EXPERT_AXES, split_axis=0, concat_axis=0, tiled=True)
    far_tokens = swap(near_tokens, "dx")
    near_attended, own_near, given_near = picked(
        which[None], (attended, swap(attended, "dx")), near_tokens
    )
    incoming, far_tokens, near_attended, given_near = lax.optimization_barrier(
        (incoming, far_tokens, near_attended, given_near)
    )
    far_attended, got_near = swap(near_attended, "em"), swap(given_near, "ey")
    incoming = incoming.reshape(-1, model_width)
    sent_back, expert_rows, grad_slots, active, d_inner = expert_rows_of(
        incoming, capacity, (w_in_own, w_out_own, w_in_other, w_out_other)
    )
    sent_back, far_attended, got_near = lax.optimization_barrier(
        (sent_back, far_attended, got_near)
    )
    sent_back = sent_back.reshape(2 * experts, 2 * capacity, model_width)
    came_back = lax.all_to_all(sent_back, EXPERT_AXES, split_axis=0, concat_axis=0, tiled=True)
    own_far, given_far = picked(which[None], (far_attended,), far_tokens)
    expert_rows, given_far = lax.optimization_barrier((expert_rows, given_far))
    factors = [own_near, own_far, got_near, swap(given_far, "ey")]
    in_other, out_other, in_own, out_own = expert_grads_of(
        expert_rows, grad_slots, active, d_inner
    )
    came_back, factors, in_own, out_own, in_other, out_other = lax.optimization_barrier(
        (came_back, factors, in_own, out_own, in_other, out_other)
    )
    factors = factors + [swap(rows, "dc") for rows in factors]
    in_other, out_other = swap(in_other, "dc"), swap(out_other, "dc")

    output, grad_input, late = backward_of(
        came_back.reshape(experts, 2, 2 * capacity, model_width),
        tokens,
        gain_one,
        weights,
        gain_two,
        router,
        cotangent,
        saved,
        group,
    )

    late = lax.all_to_all(late, GROUP_AXES, split_axis=0, concat_axis=0, tiled=True)
    left = left_of(which[None], factors, gain_one)
    late, left = lax.optimization_barrier((late, left))
    gather = gathered_grads if lax.axis_size("eh") == 2 else gathered_grads_plain
    grads, (grad_in, grad_out) = gather(
        late, left, place, small_rows, experts, ((in_own, in_other), (out_own, out_other))
    )
    *grads, grad_norm, grad_ffn, grad_bias, grad_router = grads
    return (
        output,
        grad_input,
        grad_norm.reshape(model_width),
        *grads,
        grad_bias.T,
        grad_ffn.reshape(model_width),
        grad_router.T,
        grad_in[None],
        grad_out[None],
    )


def solution(mesh):
    exp_count, dp_count = mesh.shape["exp"], mesh.shape["dp"]
    fine = Mesh(
        mesh.devices.reshape(exp_count // 4, 2, 2, dp_count // 2, 2),
        TOKEN_AXES,
    )
    exp, dp = ("eh", "em", "ey"), ("dx", "dc")
    in_specs = (
        P(TOKEN_AXES, None),
        P(),
        P(),
        P(),
        P(),
        P(),
        P(),
        P(),
        P(),
        P(exp, None, dp),
        P(exp, dp, None),
        P(TOKEN_AXES, None),
        P(TOKEN_AXES),
        P(TOKEN_AXES, None),
    )
    out_specs = (
        P(TOKEN_AXES, None),
        P(TOKEN_AXES, None),
        P(),
        P(),
        P(),
        P(),
        P(),
        P(),
        P(),
        P(),
        P(exp, None, dp),
        P(exp, dp, None),
    )
    return jax.shard_map(
        per_device, mesh=fine, in_specs=in_specs, out_specs=out_specs, check_vma=False
    )
```

```python
import functools

import jax
import jax.numpy as jnp
import numpy as np
from jax import lax
from jax.experimental import pallas as pl
from jax.experimental.pallas import tpu as pltpu
from jax.sharding import Mesh
from jax.sharding import PartitionSpec as P

HEADS = 12
HEAD_DIM = 64
BUCKETS = 32
LANES = 128
VMEM_MIB = 63

norm_eps = 1e-06
score_scale = 0.125
masked_score = -1e30
far_limits = (11, 16, 22, 32, 45, 64, 90)

EXPERT_AXES = ("eh", "em", "ey", "dx")
GROUP_AXES = ("em", "ey", "dx", "dc")
TOKEN_AXES = ("eh", "em", "ey", "dx", "dc")


def bucket_of(offset):
    distance = jnp.abs(offset)
    far_bucket = jnp.full(distance.shape, 8, jnp.int32)
    for limit_value in far_limits:
        far_bucket = far_bucket + (distance >= limit_value).astype(jnp.int32)
    near_bucket = jnp.where(distance < 8, distance, far_bucket)
    return near_bucket + 16 * (offset > 0).astype(jnp.int32)


def dot_last(left_side, right_side):
    return lax.dot_general(
        left_side, right_side, (((1,), (1,)), ((), ())), preferred_element_type=jnp.float32
    )


def dot_first(left_side, right_side):
    return lax.dot_general(
        left_side, right_side, (((0,), (0,)), ((), ())), preferred_element_type=jnp.float32
    )


def norm_backward(values, factor, gain, grad_normed):
    scaled = gain * grad_normed
    grad_gain = jnp.sum(grad_normed * values * factor, axis=0, keepdims=True)
    grad_values = factor * scaled - values * factor * factor * factor * jnp.mean(
        scaled * values, axis=-1, keepdims=True
    )
    return (grad_values, grad_gain)


def swap(array, axis):
    return lax.ppermute(array, axis, perm=[(0, 1), (1, 0)])


def whole_spec():
    return pl.BlockSpec(memory_space=pltpu.VMEM)


def any_spec():
    return pl.BlockSpec(memory_space=pl.ANY)


def params(mib):
    return pltpu.CompilerParams(vmem_limit_bytes=mib * 1024 * 1024)


def cost(flops, moved):
    return pl.CostEstimate(flops=flops, bytes_accessed=moved, transcendentals=0)


def shaped(dims, kind):
    return jax.ShapeDtypeStruct(dims, kind)


class Arriving:
    def __init__(self, source, held, sem):
        self.held, self.pending = held, pltpu.make_async_copy(source, held, sem)
        self.pending.start()

    def ref(self):
        if self.pending is not None:
            self.pending.wait()
            self.pending = None
        return self.held

    def __getitem__(self, index):
        return self.ref()[index]

    @property
    def shape(self):
        return self.held.shape


def wait_all(*operands):
    for operand in operands:
        operand.ref()


class Leaving:
    def __init__(self, held, target, sem):
        self.held, self.copy = held, pltpu.make_async_copy(held, target, sem)

    def __setitem__(self, index, value):
        self.held[index] = value

    def __getitem__(self, index):
        return self.held[index]

    @property
    def shape(self):
        return self.held.shape

    def send(self):
        self.copy.start()

    def finish(self):
        self.copy.wait()


class Staying:
    def __init__(self, held):
        self.held = held

    def __setitem__(self, index, value):
        self.held[index] = value

    def __getitem__(self, index):
        return self.held[index]

    @property
    def shape(self):
        return self.held.shape

    def send(self):
        pass


def slot_rows(slot, capacity):
    if not mixed_tiles(capacity):
        return slot, slot + capacity
    main = capacity - 4
    tail = slot >= main
    return jnp.where(tail, slot + main, slot), jnp.where(tail, slot + main + 4, slot + main)


def mixed_tiles(capacity):
    return capacity > 4 and (capacity - 4) % 16 == 0


def staged(
    kernel,
    name,
    scalars,
    inputs,
    outputs,
    scratch,
    flops,
    moved,
    residents=(),
    kept=(),
    mib=VMEM_MIB,
):
    counts = (len(scalars), len(residents), len(inputs), len(kept), len(outputs))

    def body(*refs):
        refs = list(refs)
        take = lambda count: [refs.pop(0) for _ in range(count)]
        numbers, there, sources, staying, targets = [take(count) for count in counts]
        held_in, held_out = take(counts[2]), take(counts[4])
        sems = refs.pop(0)
        arriving = [
            Arriving(source, held, sems.at[i])
            for i, (source, held) in enumerate(zip(sources, held_in))
        ]
        leaving = [
            Leaving(held, target, sems.at[counts[2] + i])
            for i, (held, target) in enumerate(zip(held_out, targets))
        ]
        kernel(numbers, there + arriving, [Staying(ref) for ref in staying] + leaving, refs)
        for copy in leaving:
            copy.finish()

    return pl.pallas_call(
        body,
        out_shape=tuple(kept) + tuple(outputs),
        in_specs=[pl.BlockSpec(memory_space=pltpu.SMEM)] * counts[0]
        + [whole_spec()] * counts[1]
        + [any_spec()] * counts[2],
        out_specs=(whole_spec(),) * counts[3] + (any_spec(),) * counts[4],
        scratch_shapes=[pltpu.VMEM(x.shape, x.dtype) for x in inputs]
        + [pltpu.VMEM(x.shape, x.dtype) for x in outputs]
        + [pltpu.SemaphoreType.DMA((max(1, counts[2] + counts[4]),))]
        + list(scratch),
        compiler_params=params(mib),
        cost_estimate=cost(flops, moved),
        name=name,
    )(*scalars, *residents, *inputs)


def row_of(ref):
    return jnp.concatenate([ref[i : i + 1] for i in range(ref.shape[0])], axis=1)


def rms_factor(values):
    return lax.rsqrt(jnp.mean(values * values, axis=-1, keepdims=True) + norm_eps)


def pair_masks(rows):
    first = lax.broadcasted_iota(jnp.int32, (rows, LANES), 1) < HEAD_DIM
    return first


def stacked_heads(pair, first):
    zero = jnp.zeros_like(pair)
    return jnp.concatenate([jnp.where(first, pair, zero), jnp.where(first, zero, pair)], axis=0)


def offset_buckets(rows, length):
    lane = lax.broadcasted_iota(jnp.int32, (rows, 2 * length), 1)
    return bucket_of(jnp.where(lane < length, lane, lane - 2 * length))


def forward_kernel(numbers, inputs, outputs, scratch):
    (count_ref,) = numbers
    (
        tokens_ref,
        gain_ref,
        query_ref,
        key_ref,
        value_ref,
        bias_ref,
        routes_ref,
        output_ref,
        gain_two_ref,
        router_ref,
        cotangent_ref,
    ) = inputs
    (
        outgoing_ref,
        attended_ref,
        q_ref,
        k_ref,
        v_ref,
        probs_ref,
        hidden_ref,
        router_probs_ref,
        choose_ref,
        slot_ref,
    ) = outputs
    early, later = inputs[:7], inputs[7:]
    wait_all(*early)
    low = jnp.bfloat16
    length, width = tokens_ref.shape
    experts = router_ref.shape[0]
    capacity = outgoing_ref.shape[2] // 2
    inputs = tokens_ref[...].astype(jnp.float32)
    normed = (inputs * rms_factor(inputs) * row_of(gain_ref)).astype(low)
    for weight, out in ((query_ref, q_ref), (key_ref, k_ref), (value_ref, v_ref)):
        out[...] = jnp.dot(normed, weight[...], preferred_element_type=jnp.float32).astype(low)
        out.send()

    buckets = offset_buckets(BUCKETS, length)
    hot = buckets == lax.broadcasted_iota(jnp.int32, buckets.shape, 0)
    table = jnp.dot(
        bias_ref[...],
        jnp.where(hot, 1.0, 0.0),
        precision=lax.Precision.HIGHEST,
        preferred_element_type=jnp.float32,
    )
    live = lax.broadcasted_iota(jnp.int32, (length, length), 1) < count_ref[0]
    first = pair_masks(length)
    for pair in range(HEADS // 2):
        lanes = slice(pair * LANES, (pair + 1) * LANES)
        scores = dot_last(q_ref[:, lanes], stacked_heads(k_ref[:, lanes], first)) * score_scale
        weights = []
        for head in range(2):
            row = table[2 * pair + head : 2 * pair + head + 1]
            field = pltpu.roll(
                jnp.broadcast_to(row, (length, 2 * length)), 0, 1, stride=1, stride_axis=0
            )
            own = scores[:, head * length : (head + 1) * length] + field[:, :length]
            own = jnp.where(live, own, masked_score)
            own = jnp.exp(own - jnp.max(own, axis=1, keepdims=True))
            own = own / jnp.sum(own, axis=1, keepdims=True)
            probs_ref[pair, :, head * length : (head + 1) * length] = own
            weights.append(own.astype(low))
        both = jnp.concatenate(weights, axis=1)
        attended_ref[:, lanes] = jnp.dot(
            both, stacked_heads(v_ref[:, lanes], first), preferred_element_type=jnp.float32
        ).astype(low)

    attended_ref.send()
    probs_ref.send()
    wait_all(*later)
    hidden = inputs + jnp.dot(
        attended_ref[...], output_ref[...], preferred_element_type=jnp.float32
    )
    hidden_ref[...] = hidden
    hidden_ref.send()
    normed_two = (hidden * rms_factor(hidden) * row_of(gain_two_ref)).astype(low)
    logits = dot_last(normed_two, router_ref[...])
    router_probs = jnp.exp(logits - jnp.max(logits, axis=1, keepdims=True))
    router_probs = router_probs / jnp.sum(router_probs, axis=1, keepdims=True)
    router_probs_ref[...] = router_probs
    router_probs_ref.send()

    lane = lax.broadcasted_iota(jnp.int32, (length, length), 1)
    place = lax.broadcasted_iota(jnp.int32, (length, length), 0)
    routes = routes_ref[...]
    chosen = routes == lax.broadcasted_iota(jnp.int32, (experts, length), 0)
    chosen = jnp.where(chosen, 1.0, 0.0)
    alive = lax.broadcasted_iota(jnp.int32, (1, length), 1) < count_ref[0]
    before = jnp.where(place <= lane, 1.0, 0.0).astype(low)
    running = jnp.dot(
        (chosen * jnp.where(alive, 1.0, 0.0)).astype(low),
        before,
        preferred_element_type=jnp.float32,
    )
    slot = jnp.sum(running * chosen, axis=0, keepdims=True).astype(jnp.int32) - 1
    kept = alive & (slot < capacity)
    columns = [
        jnp.where(kept, routes * (2 * capacity) + row, -1) for row in slot_rows(slot, capacity)
    ]
    slot_ref[...] = jnp.concatenate(columns, axis=0)
    slot_ref.send()
    unit = jnp.where(place == lane, 1.0, 0.0).astype(low)
    choose = dot_last(unit, chosen.astype(low))
    choose_ref[...] = choose
    choose_ref.send()
    gate = jnp.sum(router_probs * choose, axis=1, keepdims=True)
    scaled = (gate * cotangent_ref[...].astype(jnp.float32)).astype(low)
    row = lax.broadcasted_iota(jnp.int32, (experts * 2 * capacity, length), 0)
    spread = jnp.concatenate(
        [
            jnp.where(row == columns[0], 1.0, 0.0).astype(low),
            jnp.where(row == columns[1], 1.0, 0.0).astype(low),
        ],
        axis=1,
    )
    packed = jnp.dot(
        spread,
        jnp.concatenate([normed_two, scaled], axis=0),
        preferred_element_type=jnp.float32,
    )
    for expert in range(experts):
        rows = packed[expert * 2 * capacity : (expert + 1) * 2 * capacity].astype(low)
        outgoing_ref[expert, 0] = rows
        outgoing_ref[expert, 1] = rows
    outgoing_ref.send()


def forward_of(count, tokens, gain, weights, bias, gain_two, router, routes, cotangent, capacity):
    length, width = tokens.shape
    experts = router.shape[0]
    low = jnp.bfloat16
    outputs = (
        shaped((experts, 2, 2 * capacity, width), low),
        shaped((length, width), low),
        shaped((length, width), low),
        shaped((length, width), low),
        shaped((length, width), low),
        shaped((HEADS // 2, length, 2 * length), jnp.float32),
        shaped((length, width), jnp.float32),
        shaped((length, experts), jnp.float32),
        shaped((length, experts), jnp.float32),
        shaped((2, length), jnp.int32),
    )
    query, key, value, output = weights
    inputs = (tokens, gain, query, key, value, bias, routes, output, gain_two, router, cotangent)
    return staged(
        forward_kernel,
        "forward",
        (count,),
        inputs,
        outputs,
        (),
        10 * length * width * width,
        10 * width * width,
    )


def backward_kernel(numbers, inputs, outputs, scratch):
    (
        came_ref,
        slot_ref,
        hidden_ref,
        router_probs_ref,
        choose_ref,
        cotangent_ref,
        gain_two_ref,
        router_ref,
        output_ref,
        v_ref,
        probs_ref,
        q_ref,
        k_ref,
    ) = inputs
    late_ref, turned, hidden_grad_ref, out_ref = outputs
    sums, tail = scratch
    wait_all(*inputs[1:])
    low = jnp.bfloat16
    length, width = hidden_ref.shape
    experts = router_ref.shape[0]
    capacity = came_ref.shape[2] // 2
    group = late_ref.shape[0]
    small_rows = tail.shape[0] // group
    top = cotangent_ref[...].astype(jnp.float32)
    slots = experts * 2 * capacity
    came = came_ref[:, 0].astype(jnp.float32) + came_ref[:, 1].astype(jnp.float32)
    came = came.reshape(slots, width).astype(low)
    row = lax.broadcasted_iota(jnp.int32, (slots, length), 0)
    spread = jnp.concatenate(
        [
            jnp.where(row == slot_ref[0:1], 1.0, 0.0).astype(low),
            jnp.where(row == slot_ref[1:2], 1.0, 0.0).astype(low),
        ],
        axis=1,
    )
    back = dot_first(spread, came)
    returned, d_normed_two = back[:length], back[length:]
    hidden = hidden_ref[...]
    router_probs, choose = router_probs_ref[...], choose_ref[...]
    gate = jnp.sum(router_probs * choose, axis=1, keepdims=True)
    out_ref[...] = (hidden + gate * returned).astype(low)
    out_ref.send()
    d_gate = jnp.sum(top * returned, axis=1, keepdims=True)
    d_probs = choose * d_gate
    d_logits = router_probs * (
        d_probs - jnp.sum(router_probs * d_probs, axis=1, keepdims=True)
    )
    d_logits = d_logits.astype(low)
    factor = rms_factor(hidden)
    gain_two = row_of(gain_two_ref)
    normed_two = (hidden * factor * gain_two).astype(low)
    grad_router = dot_first(d_logits, normed_two)
    d_normed_two = d_normed_two + jnp.dot(
        d_logits, router_ref[...], preferred_element_type=jnp.float32
    )
    d_from_norm, grad_ffn = norm_backward(hidden, factor, gain_two, d_normed_two)
    d_hidden = top + d_from_norm
    hidden_grad_ref[...] = d_hidden
    hidden_grad_ref.send()
    d_mixed = d_hidden.astype(low)
    d_attended = dot_last(d_mixed, output_ref[...]).astype(low)
    flipped = d_mixed.T
    for head in range(HEADS):
        at = 3 * HEADS + head
        late_ref[at // 3, at % 3 * HEAD_DIM : (at % 3 + 1) * HEAD_DIM] = flipped[
            head * HEAD_DIM : (head + 1) * HEAD_DIM
        ]

    first = pair_masks(length)
    upper = lax.broadcasted_iota(jnp.int32, (LANES, length), 0) < HEAD_DIM
    lane = lax.broadcasted_iota(jnp.int32, (length, length), 1)
    place = lax.broadcasted_iota(jnp.int32, (length, length), 0)
    reverse = jnp.where(place + lane == length - 1, 1.0, 0.0).astype(low)
    for pair in range(HEADS // 2):
        lanes = slice(pair * LANES, (pair + 1) * LANES)
        upstream = d_attended[:, lanes]
        probs = probs_ref[pair]
        d_probs = dot_last(upstream, stacked_heads(v_ref[:, lanes], first))
        parts = []
        for head in range(2):
            span = slice(head * length, (head + 1) * length)
            own, grad = probs[:, span], d_probs[:, span]
            parts.append(own * (grad - jnp.sum(own * grad, axis=1, keepdims=True)))
        d_scores = jnp.concatenate(parts, axis=1).astype(low)
        d_values = dot_first(upstream, probs.astype(low))
        d_values = jnp.where(upper, d_values[:, :length], d_values[:, length:])
        d_keys = dot_first(q_ref[:, lanes], d_scores) * score_scale
        d_keys = jnp.where(upper, d_keys[:, :length], d_keys[:, length:])
        d_queries = jnp.dot(
            d_scores, stacked_heads(k_ref[:, lanes], first), preferred_element_type=jnp.float32
        )
        d_queries = (d_queries * score_scale).astype(low)
        for which, value in enumerate(
            (d_queries.T, d_keys.astype(low), d_values.astype(low))
        ):
            turned[which, lanes] = value
            for head in range(2):
                at = which * HEADS + 2 * pair + head
                late_ref[at // 3, at % 3 * HEAD_DIM : (at % 3 + 1) * HEAD_DIM] = value[
                    head * HEAD_DIM : (head + 1) * HEAD_DIM
                ]
        upside = jnp.dot(reverse, d_scores, preferred_element_type=jnp.float32)
        for head in range(2):
            own = upside[:, head * length : (head + 1) * length]
            own = jnp.concatenate([own, jnp.zeros_like(own)], axis=1)
            own = pltpu.roll(own, 0, 1, stride=1, stride_axis=0)
            at = 2 * pair + head
            sums[at % 4, at // 4 : at // 4 + 1] = jnp.sum(own, axis=0, keepdims=True)

    turned.send()

    shift = lax.broadcasted_iota(jnp.int32, (2 * length, LANES), 0) - (length - 1)
    bucket = bucket_of(shift)
    lane_wide = lax.broadcasted_iota(jnp.int32, (2 * length, LANES), 1)
    bias_rows = 0.0
    for quarter in range(4):
        hot = jnp.where(bucket + quarter * BUCKETS == lane_wide, 1.0, 0.0)
        bias_rows = bias_rows + jnp.dot(
            sums[quarter],
            hot,
            precision=lax.Precision.HIGHEST,
            preferred_element_type=jnp.float32,
        )
    chunks = width // LANES
    tail[...] = jnp.zeros_like(tail)
    for chunk in range(chunks):
        lanes = slice(chunk * LANES, (chunk + 1) * LANES)
        tail[chunk : chunk + 1] = grad_ffn[:, lanes]
        for expert in range(experts):
            at = chunks + HEADS // 4 + expert * chunks + chunk
            tail[at : at + 1] = grad_router[expert : expert + 1, lanes]
    tail[chunks : chunks + HEADS // 4] = bias_rows[: HEADS // 4]
    block = 4 * width // group
    for at in range(group):
        own = tail[at * small_rows : (at + 1) * small_rows]
        high = own.astype(low).astype(jnp.float32)
        late_ref[at, block:] = jnp.concatenate([high, own - high], axis=0).astype(low)
    late_ref.send()


def backward_of(came, weight, gain_two, router, cotangent, saved, group):
    length, width = cotangent.shape
    experts = router.shape[0]
    low = jnp.bfloat16
    small_rows = -(-small_count(width, experts) // group)
    block = 4 * width // group
    outputs = (
        shaped((group, block + 2 * small_rows, length), low),
        shaped((3, width, length), low),
        shaped((length, width), jnp.float32),
        shaped((length, width), low),
    )
    scratch = (
        pltpu.VMEM((4, 8, 2 * length), jnp.float32),
        pltpu.VMEM((group * small_rows, LANES), jnp.float32),
    )
    q, k, v, probs, hidden, router_probs, choose, slot = saved
    inputs = (slot, hidden, router_probs, choose, cotangent, gain_two, router, weight)
    return staged(
        backward_kernel,
        "backward",
        (),
        (*inputs, v, probs, q, k),
        outputs,
        scratch,
        4 * length * width * width,
        10 * width * width,
        residents=(came,),
        mib=62,
    )


def first_norm_kernel(numbers, inputs, outputs, scratch):
    turned, hidden_grad_ref, query_ref, key_ref, value_ref, tokens_ref, gain_ref = inputs
    gain_out, grad_ref = outputs
    wait_all(*inputs)
    d_normed = 0.0
    for which, weight in enumerate((query_ref, key_ref, value_ref)):
        d_normed = d_normed + lax.dot_general(
            turned[which],
            weight[...],
            (((0,), (1,)), ((), ())),
            preferred_element_type=jnp.float32,
        )
    inputs = tokens_ref[...].astype(jnp.float32)
    d_first, grad_norm = norm_backward(
        inputs, rms_factor(inputs), row_of(gain_ref), d_normed
    )
    grad_ref[...] = (hidden_grad_ref[...] + d_first).astype(jnp.bfloat16)
    grad_ref.send()
    gain_out[...] = jnp.zeros(gain_out.shape, jnp.float32)
    for chunk in range(gain_ref.shape[0]):
        gain_out[chunk : chunk + 1] = grad_norm[:, chunk * LANES : (chunk + 1) * LANES]
    gain_out.send()


def first_norm_of(turned, hidden_grad, weights, tokens, gain):
    length, width = tokens.shape
    low = jnp.bfloat16
    rows = -(-gain.shape[0] // 8) * 8
    return staged(
        first_norm_kernel,
        "first_norm",
        (),
        (turned, hidden_grad, *weights, tokens, gain),
        (shaped((length, width), low),),
        (),
        6 * length * width * width,
        8 * width * width,
        kept=(shaped((rows, LANES), jnp.float32),),
        mib=59,
    )


def small_count(width, experts):
    return (1 + experts) * (width // LANES) + HEADS // 4


def pick_kernel(numbers, inputs, outputs, scratch):
    (which_ref,), (*pieces, tokens_ref) = numbers, inputs
    which = which_ref[0]
    pieces = [piece.ref() for piece in pieces]
    rows = pieces[0].shape[0]
    tokens_ref = tokens_ref.ref()
    if len(pieces) > 1:
        for part, piece in enumerate(pieces):
            outputs[0][part * rows : (part + 1) * rows] = piece[...]
        outputs[0].send()
    for out, turn in zip(outputs[-2:], (3, 1)):

        @pl.when(which == turn)
        def _():
            for part, piece in enumerate(pieces):
                out[part * rows : (part + 1) * rows] = piece[...]

        @pl.when(which != turn)
        def _():
            out[...] = tokens_ref[...]

        out.send()


def picked(which, pieces, tokens):
    outputs = (shaped(tokens.shape, tokens.dtype),) * (2 if len(pieces) == 1 else 3)
    return staged(
        pick_kernel,
        "picked",
        (which,),
        (*pieces, tokens),
        outputs,
        (),
        0,
        10 * tokens.size,
    )


def left_kernel(numbers, inputs, outputs, scratch):
    (which_ref,), (*pieces, gain_ref), (left_ref,) = numbers, inputs, outputs
    which = which_ref[0]
    scale = row_of(gain_ref)
    wait_all(*pieces)
    count = pieces[0].shape[0]
    spans = [
        (piece, at, slice(number * count + at, number * count + at + LANES))
        for number, piece in enumerate(pieces)
        for at in range(0, count, LANES)
    ]

    @pl.when(which < 3)
    def _():
        for piece, at, span in spans:
            own = piece[at : at + LANES].astype(jnp.float32)
            own = (own * rms_factor(own) * scale).astype(jnp.bfloat16)
            left_ref[:, span] = own.T

    @pl.when(which == 3)
    def _():
        for piece, at, span in spans:
            left_ref[:, span] = piece[at : at + LANES].T

    left_ref.send()


def left_of(which, pieces, gain):
    count, width = pieces[0].shape
    total = count * len(pieces)
    kept = (shaped((width, total), jnp.bfloat16),)
    inputs = (*pieces, gain)
    (left,) = staged(
        left_kernel,
        "left",
        (which,),
        inputs,
        (),
        (),
        10 * total * width,
        6 * total * width,
        kept=kept,
        mib=59,
    )
    return left


gelu_scale = 0.7978845608028654
gelu_cubic = 0.044715


def expert_pass(rows, slots, weights, act_ref, inner_ref):
    result, d_rows = 0.0, 0.0
    for part, (part_in, part_out) in enumerate(weights):
        inner = jnp.dot(rows, part_in[...], preferred_element_type=jnp.float32)
        upstream = dot_last(slots, part_out[...])
        square = inner * inner
        bent = jnp.tanh(gelu_scale * (inner + gelu_cubic * (square * inner)))
        active = (inner * (0.5 * (1.0 + bent))).astype(jnp.bfloat16)
        slope = 0.5 * (1.0 + bent) + 0.5 * inner * (1.0 - bent * bent) * (
            gelu_scale * (1.0 + 3.0 * gelu_cubic * square)
        )
        d_inner = (upstream * slope).astype(jnp.bfloat16)
        act_ref[part] = active
        inner_ref[part] = d_inner
        result = result + jnp.dot(active, part_out[...], preferred_element_type=jnp.float32)
        d_rows = d_rows + dot_last(d_inner, part_in[...])
    act_ref.send()
    inner_ref.send()
    return result, d_rows


def expert_kernel(numbers, inputs, outputs, scratch):
    blocks_ref, in_a, out_a, in_b, out_b = inputs
    back_ref, rows_out, slots_out, act_ref, inner_ref = outputs
    low = jnp.bfloat16
    blocks, height, width = blocks_ref.shape
    main = height // 2 - 4
    count = blocks * main
    mixed = blocks_ref[:, 2 * main :].astype(jnp.float32).reshape(blocks * 8, width)
    place = lax.broadcasted_iota(jnp.int32, mixed.shape, 0) & 7
    ahead = place < 4
    second = pltpu.roll(mixed, blocks * 8 - 4, 0)
    zero = jnp.zeros_like(mixed)
    first_main = blocks_ref[:, :main].reshape(count, width)
    second_main = blocks_ref[:, main : 2 * main].reshape(count, width)
    rows = jnp.concatenate([first_main, jnp.where(ahead, mixed, zero).astype(low)], axis=0)
    slots = jnp.concatenate([second_main, jnp.where(ahead, second, zero).astype(low)], axis=0)
    rows_out[...] = rows
    rows_out.send()
    slots_out[...] = slots
    slots_out.send()
    weights = ((in_a, out_a), (in_b, out_b))
    wait_all(in_a, out_a, in_b, out_b)
    result, d_rows = expert_pass(rows, slots, weights, act_ref, inner_ref)
    back_ref[:, :main] = result[:count].reshape(blocks, main, width).astype(low)
    back_ref[:, main : 2 * main] = d_rows[:count].reshape(blocks, main, width).astype(low)
    mixed = jnp.where(ahead, result[count:], pltpu.roll(d_rows[count:], 4, 0))
    back_ref[:, 2 * main :] = mixed.reshape(blocks, 8, width).astype(low)
    back_ref.send()


def expert_sorting_kernel(numbers, inputs, outputs, scratch):
    rows_ref, order_ref, in_a, out_a, in_b, out_b = inputs
    back_ref, rows_out, slots_out, act_ref, inner_ref = outputs
    count = rows_ref.shape[0]
    half = count // 2
    lanes = lax.broadcasted_iota(jnp.int32, (count, count), 1)
    sort = jnp.where(order_ref[:, 0:1] == lanes, 1.0, 0.0).astype(jnp.bfloat16)
    unsort = jnp.where(order_ref[:, 1:2] == lanes, 1.0, 0.0).astype(jnp.bfloat16)
    ordered = jnp.dot(sort, rows_ref[...], preferred_element_type=jnp.float32)
    ordered = ordered.astype(jnp.bfloat16)
    rows, slots = ordered[:half], ordered[half:]
    rows_out[...] = rows
    rows_out.send()
    slots_out[...] = slots
    slots_out.send()
    weights = ((in_a, out_a), (in_b, out_b))
    result, d_rows = expert_pass(rows, slots, weights, act_ref, inner_ref)
    both = jnp.concatenate([result.astype(jnp.bfloat16), d_rows.astype(jnp.bfloat16)], axis=0)
    back_ref[...] = jnp.dot(unsort, both, preferred_element_type=jnp.float32).astype(jnp.bfloat16)
    back_ref.send()


def expert_rows_of(blocks, part_weights):
    number, height, width = blocks.shape
    capacity = height // 2
    hidden_width = part_weights[0].shape[1]
    low = jnp.bfloat16
    mixed = mixed_tiles(capacity)
    half = number * (capacity + 4 if mixed else capacity)
    back = shaped(blocks.shape if mixed else (number * height, width), low)
    outputs = (
        back,
        shaped((half, width), low),
        shaped((half, width), low),
        shaped((2, half, hidden_width), low),
        shaped((2, half, hidden_width), low),
    )
    flops, moved = 16 * half * width * hidden_width, 12 * width * width
    if mixed:
        return staged(
            expert_kernel,
            "expert_rows",
            (),
            part_weights,
            outputs,
            (),
            flops,
            moved,
            residents=(blocks,),
            mib=62,
        )
    place = np.arange(2 * half)
    sort = place % half // capacity * height + place // half * capacity + place % capacity
    unsort = np.empty_like(sort)
    unsort[sort] = place
    order = jnp.asarray(np.stack([sort, unsort], axis=1), jnp.int32)
    back, *rest = staged(
        expert_sorting_kernel,
        "expert_rows",
        (),
        (blocks.reshape(-1, width), order, *part_weights),
        outputs,
        (),
        flops,
        moved,
    )
    return back.reshape(blocks.shape), *rest


def sent_grads_kernel(numbers, inputs, outputs, scratch):
    rows_ref, inner_ref, act_ref, slots_ref = inputs
    sent_in, sent_out = outputs
    wait_all(*inputs)
    sent_in[...] = dot_first(rows_ref[...], inner_ref[1]).astype(jnp.bfloat16)
    sent_in.send()
    sent_out[...] = dot_first(act_ref[1], slots_ref[...]).astype(jnp.bfloat16)
    sent_out.send()


def sent_grads_of(rows, slots, active, d_inner):
    half, width = rows.shape
    hidden_width = active.shape[2]
    outputs = (
        shaped((width, hidden_width), jnp.bfloat16),
        shaped((hidden_width, width), jnp.bfloat16),
    )
    return staged(
        sent_grads_kernel,
        "sent_grads",
        (),
        (rows, d_inner, active, slots),
        outputs,
        (),
        4 * half * width * hidden_width,
        8 * width * width,
    )


def own_grads_kernel(numbers, inputs, outputs, scratch):
    rows_ref, inner_ref, act_ref, slots_ref, got_in, got_out = inputs
    own_in, own_out = outputs
    wait_all(*inputs)
    own_in[...] = dot_first(rows_ref[...], inner_ref[0]) + got_in[...].astype(jnp.float32)
    own_in.send()
    own_out[...] = dot_first(act_ref[0], slots_ref[...]) + got_out[...].astype(jnp.float32)
    own_out.send()


def own_grads_of(rows, slots, active, d_inner, got_in, got_out):
    half, width = rows.shape
    hidden_width = active.shape[2]
    outputs = (
        shaped((width, hidden_width), jnp.float32),
        shaped((hidden_width, width), jnp.float32),
    )
    return staged(
        own_grads_kernel,
        "own_grads",
        (),
        (rows, d_inner, active, slots, got_in, got_out),
        outputs,
        (),
        0,
        0,
    )


def in_parts(values):
    high = values.astype(jnp.bfloat16).astype(jnp.float32)
    return jnp.concatenate([high, values - high], axis=0).astype(jnp.bfloat16)


def from_parts(parts):
    parts = parts.astype(jnp.float32)
    rows = parts.shape[0] // 2
    return parts[:rows] + parts[rows:]


def block_kernel(numbers, inputs, outputs, scratch):
    (bits_ref,), (late_ref, left_ref, gain_ref), (block_ref,) = numbers, inputs, outputs
    group = late_ref.shape[0]
    part = left_ref.shape[0] // 2
    block = left_ref.shape[0] * 4 // group
    edge = block - LANES
    half = part // 2
    gain_edge = block_ref.shape[1] - 2 * gain_ref.shape[0]
    odd = bits_ref[3] == 1
    here = bits_ref[0] * 8 + bits_ref[1] * 4 + bits_ref[2] * 2 + bits_ref[3]
    right = jnp.concatenate(
        [late_ref[here ^ factor_order(i), :block] for i in range(group)], axis=1
    )
    right = jnp.where(odd, jnp.concatenate([right[edge:], right[:edge]], axis=0), right)
    total = dot_last(left_ref[...], right)
    first = pair_masks(half)
    small = in_parts(from_parts(jnp.sum(late_ref[:, block:].astype(jnp.float32), axis=0)))
    gain = in_parts(gain_ref[...])
    for side in range(2):
        own = total[side * part : (side + 1) * part]
        block_ref[side, :part] = own[:, :LANES].astype(jnp.bfloat16)
        rest = own[:, LANES:]
        rest = jnp.concatenate([rest, rest], axis=1)
        upper, lower = rest[:half], rest[half:]
        even = jnp.where(first, upper, lower)
        packed = jnp.where(odd, jnp.where(first, lower, upper), even)
        block_ref[side, part : part + half] = packed.astype(jnp.bfloat16)
        block_ref[side, part + half : gain_edge] = small
        block_ref[side, gain_edge:] = gain


def block_of(bits, late, left, gain, small_rows):
    group, rows, length = late.shape
    width = left.shape[0]
    height = 3 * width // 4 + 2 * (small_rows + gain.shape[0])
    (block,) = staged(
        block_kernel,
        "grad_block",
        (bits,),
        (),
        (),
        (),
        8 * width * width * length,
        2 * left.size,
        residents=(late, left, gain),
        kept=(shaped((2, height, LANES), jnp.bfloat16),),
        mib=24,
    )
    return block


def share_kernel(edge, small_rows, numbers, inputs, outputs, scratch):
    (own_ref, got_ref), (share_ref,) = inputs, outputs
    gain_edge = edge + 2 * small_rows
    for side in range(2):
        own = own_ref[side, :edge].astype(jnp.float32) + got_ref[side, :edge].astype(jnp.float32)
        share_ref[side, :edge] = own.astype(jnp.bfloat16)
        for rows in (slice(edge, gain_edge), slice(gain_edge, None)):
            share_ref[side, rows] = in_parts(
                from_parts(own_ref[side, rows]) + from_parts(got_ref[side, rows])
            )


def share_of(own, got, edge, small_rows):
    (share,) = staged(
        functools.partial(share_kernel, edge, small_rows),
        "share",
        (),
        (),
        (),
        (),
        own.size,
        6 * own.size,
        residents=(own, got),
        kept=(shaped(own.shape, own.dtype),),
        mib=8,
    )
    return share


def assemble_kernel(weights, small_rows, bits_ref, sources, outs, made, out_sems, put_small):
    em, ey, dx, dc = [bits_ref[i] for i in range(4)]
    part = made.shape[1] // 2
    half = part // 2
    edge = part + half
    first = pair_masks(half)
    for number, weight in enumerate(weights):
        for here in range(4):

            @pl.when(dx * 2 + dc == here)
            def _():
                own = [sources[4 * number + 2 * ((i ^ here) & 1) + ((i ^ here) >> 1)] for i in range(4)]
                for side in range(2):
                    rows = slice(side * part, (side + 1) * part)
                    upper = slice(side * part, side * part + half)
                    lower = slice(side * part + half, (side + 1) * part)
                    for twin in range(2):
                        even, odd = own[2 * twin], own[2 * twin + 1]
                        at = 3 * twin * LANES
                        made[number, rows, at : at + LANES] = even[side, :part].astype(jnp.float32)
                        made[number, rows, at + 2 * LANES : at + 3 * LANES] = odd[
                            side, :part
                        ].astype(jnp.float32)
                        left = even[side, part:edge].astype(jnp.float32)
                        right = odd[side, part:edge].astype(jnp.float32)
                        middle = slice(at + LANES, at + 2 * LANES)
                        made[number, upper, middle] = jnp.where(first, left, right)
                        made[number, lower, middle] = pltpu.roll(
                            jnp.where(first, right, left), HEAD_DIM, 1
                        )
                for i in range(4):
                    tail = own[i][0, edge:].astype(jnp.float32)
                    gain = tail[2 * small_rows :]
                    gain_rows = gain.shape[0] // 2
                    put_small(
                        number,
                        i,
                        jnp.concatenate(
                            [
                                tail[:small_rows] + tail[small_rows : 2 * small_rows],
                                gain[:gain_rows] + gain[gain_rows:],
                            ],
                            axis=0,
                        ),
                    )

        truth = (em ^ (weight // 2)) * 2 + (ey ^ (weight % 2))
        for i in range(4):

            @pl.when(truth == i)
            def _():
                pltpu.make_async_copy(made.at[number], outs[i], out_sems.at[number]).start()

    for number, weight in enumerate(weights):
        truth = (em ^ (weight // 2)) * 2 + (ey ^ (weight % 2))
        for i in range(4):

            @pl.when(truth == i)
            def _():
                pltpu.make_async_copy(made.at[number], outs[i], out_sems.at[number]).wait()


def first_half_kernel(small_rows, bits_ref, *refs):
    sources, outs, small_out, made, out_sems = refs[:8], refs[8:12], refs[12], refs[13], refs[14]

    def put_small(number, i, rows):
        small_out[number, i] = rows

    assemble_kernel((0, 2), small_rows, bits_ref, sources, outs, made, out_sems, put_small)


def second_half_kernel(small_rows, bits_ref, *refs):
    sources, small_ref, outs = refs[:8], refs[8], refs[13:17]
    norm_out, ffn_out, bias_out, router_out = refs[17:21]
    made, tail, out_sems = refs[21:]
    em, ey = bits_ref[0], bits_ref[1]
    for number in range(2):
        tail[(em ^ number) * 2 + ey] = small_ref[number]

    def put_small(number, i, rows):
        tail[(em ^ number) * 2 + (ey ^ 1), i] = rows

    assemble_kernel((1, 3), small_rows, bits_ref, sources, outs, made, out_sems, put_small)

    def small_row(at):
        at, row = divmod(at, small_rows)
        return tail[at // 4, at % 4, row : row + 1]

    chunks = made.shape[2] // LANES
    total = 0.0
    for at in range(16):
        total = total + tail[at // 4, at % 4, small_rows:]
    norm_out[...] = total[:chunks]
    for chunk in range(chunks):
        lanes = slice(chunk * LANES, (chunk + 1) * LANES)
        ffn_out[chunk : chunk + 1] = small_row(chunk)
        for expert in range(router_out.shape[0]):
            router_out[expert : expert + 1, lanes] = small_row(
                chunks + HEADS // 4 + expert * chunks + chunk
            )
    for head in range(HEADS):
        at = head % 4 * BUCKETS
        bias_out[head : head + 1] = small_row(chunks + head // 4)[:, at : at + BUCKETS]


def first_half(bits, sources, small_rows, width):
    gain_rows = (sources[0].shape[1] - 3 * width // 4 - 2 * small_rows) // 2
    *grads, small = pl.pallas_call(
        functools.partial(first_half_kernel, small_rows),
        out_shape=(shaped((width, width), jnp.float32),) * 4
        + (shaped((2, 4, small_rows + gain_rows, LANES), jnp.float32),),
        in_specs=[pl.BlockSpec(memory_space=pltpu.SMEM)] + [whole_spec()] * 8,
        out_specs=(any_spec(),) * 4 + (whole_spec(),),
        scratch_shapes=[
            pltpu.VMEM((2, width, width), jnp.float32),
            pltpu.SemaphoreType.DMA((2,)),
        ],
        compiler_params=params(16),
        cost_estimate=cost(8 * width * width, 12 * width * width),
        name="first_half",
    )(bits, *sources)
    return grads, small


def second_half(bits, sources, small, grads, small_rows, width, experts):
    return pl.pallas_call(
        functools.partial(second_half_kernel, small_rows),
        out_shape=(shaped((width, width), jnp.float32),) * 4
        + (
            shaped((width // LANES, LANES), jnp.float32),
            shaped((width // LANES, LANES), jnp.float32),
            shaped((HEADS, BUCKETS), jnp.float32),
            shaped((experts, width), jnp.float32),
        ),
        in_specs=[pl.BlockSpec(memory_space=pltpu.SMEM)]
        + [whole_spec()] * 9
        + [any_spec()] * 4,
        out_specs=(any_spec(),) * 4 + (whole_spec(),) * 4,
        input_output_aliases={10 + i: i for i in range(4)},
        scratch_shapes=[
            pltpu.VMEM((2, width, width), jnp.float32),
            pltpu.VMEM((4, 4) + small.shape[2:], jnp.float32),
            pltpu.SemaphoreType.DMA((2,)),
        ],
        compiler_params=params(16),
        cost_estimate=cost(8 * width * width, 12 * width * width),
        name="second_half",
    )(bits, *sources, small, *grads)


def place_in_group():
    place = [lax.axis_index(axis) for axis in ("em", "ey", "dx", "dc")]
    return (2 * place[0] + place[1]).astype(jnp.int32), jnp.stack(place).astype(jnp.int32)


def factor_order(at):
    return (at & 1) * 2 + (at >> 1 & 1) * 4 + (at >> 2 & 1) * 8 + (at >> 3)


def with_other(rows, axis):
    return jnp.concatenate([rows, swap(rows, axis)], axis=0)


def gathered_grads(late, left, gain_rows, place, small_rows, experts, beside):
    width = left.shape[0]
    block = block_of(place, late, left, gain_rows, small_rows)
    block, beside = lax.optimization_barrier((block, beside))
    beside = own_grads_of(*beside)
    got, beside = lax.optimization_barrier((swap(block, "eh"), beside))
    near = share_of(block, got, 3 * width // 4, small_rows)
    far, near_x, near_y = swap(near, "em"), swap(near, "dx"), swap(near, "ey")
    far_x, far_y = swap(far, "dx"), swap(far, "ey")
    near_both, far_both = swap(near_x, "ey"), swap(far_y, "dx")

    def both_cores(*sources):
        return sources + tuple(swap(source, "dc") for source in sources)

    sources = both_cores(near, near_x) + both_cores(far, far_x)
    grads, small = first_half(place, sources, small_rows, width)
    sources = both_cores(near_y, near_both) + both_cores(far_y, far_both)
    grads = second_half(place, sources, small, grads, small_rows, width, experts)
    return grads, beside


def gathered_grads_plain(late, left, gain_rows, place, small_rows, experts, beside):
    group, rows, length = late.shape
    width = left.shape[0]
    block = 4 * width // group
    small = jnp.sum(late[:, block:].astype(jnp.float32), axis=0)
    small = lax.psum(small[:small_rows] + small[small_rows:], "eh")
    order = jnp.asarray([factor_order(at) for at in range(group)], jnp.int32)
    order = order ^ lax.axis_index(GROUP_AXES)
    late_block = jnp.take(late[:, :block], order, axis=0)
    late_block = late_block.transpose(1, 0, 2).reshape(block, group * length)
    grad_block = dot_last(late_block, left)
    mine = lax.psum_scatter(grad_block, "eh", scatter_dimension=0, tiled=True)
    grads = lax.all_gather(mine.astype(jnp.bfloat16), "eh", axis=0, tiled=True)
    grads = lax.all_gather(grads, GROUP_AXES, axis=0, tiled=True)
    small = lax.all_gather(small, GROUP_AXES, axis=0, tiled=True).reshape(-1)
    grads = grads.reshape(4, width, width).transpose(0, 2, 1).astype(jnp.float32)
    sizes = (width, HEADS * BUCKETS, experts * width)
    ends = np.cumsum(sizes)
    pieces = [small[end - size : end] for end, size in zip(ends, sizes)]
    pieces[1], pieces[2] = pieces[1].reshape(HEADS, BUCKETS), pieces[2].reshape(experts, width)
    grad_norm = lax.psum(gain_rows, TOKEN_AXES)[: width // LANES]
    return (*grads, grad_norm, *pieces), own_grads_of(*beside)


def per_device(
    tokens,
    norm_gain,
    w_query,
    w_key,
    w_value,
    w_output,
    rel_bias,
    ffn_gain,
    w_router,
    w_in,
    w_out,
    routes,
    lengths,
    cotangent,
):
    length, model_width = tokens.shape
    experts = w_router.shape[1]
    group = lax.axis_size(GROUP_AXES)
    capacity = max(2, (5 * length + 4 * experts - 1) // (4 * experts))
    small_rows = -(-small_count(model_width, experts) // group)
    gain_one, gain_two = norm_gain.reshape(-1, LANES), ffn_gain.reshape(-1, LANES)
    weights = (w_query, w_key, w_value, w_output)
    router = w_router.T

    w_in_own, w_out_own = w_in[0], w_out[0]
    w_in_other, w_out_other = swap(w_in_own, "dc"), swap(w_out_own, "dc")
    outgoing, attended, *saved = forward_of(
        lengths,
        tokens,
        gain_one,
        weights,
        rel_bias.T,
        gain_two,
        router,
        routes.reshape(1, length),
        cotangent,
        capacity,
    )
    which, place = place_in_group()
    outgoing, near_tokens = lax.optimization_barrier((outgoing, with_other(tokens, "dx")))
    outgoing = outgoing.reshape(2 * experts, 2 * capacity, model_width)
    incoming = lax.all_to_all(outgoing, EXPERT_AXES, split_axis=0, concat_axis=0, tiled=True)
    far_tokens = swap(near_tokens, "ey")
    near_attended, own_near, given_near = picked(
        which[None], (attended, swap(attended, "dx")), near_tokens
    )
    far_attended, got_near = swap(near_attended, "ey"), swap(given_near, "em")
    incoming, far_tokens, _ = lax.optimization_barrier((incoming, far_tokens, given_near))
    sent_back, expert_rows, grad_slots, active, d_inner = expert_rows_of(
        incoming, (w_in_own, w_out_own, w_in_other, w_out_other)
    )
    sent_back, far_attended, got_near = lax.optimization_barrier(
        (sent_back, far_attended, got_near)
    )
    came_back = lax.all_to_all(sent_back, EXPERT_AXES, split_axis=0, concat_axis=0, tiled=True)
    own_far, given_far = picked(which[None], (far_attended,), far_tokens)
    in_other, out_other = sent_grads_of(expert_rows, grad_slots, active, d_inner)
    factors = [own_near, own_far, got_near]
    factors = factors + [swap(rows, "dc") for rows in factors]
    came_back, factors, given_far, in_other, out_other = lax.optimization_barrier(
        (came_back, factors, given_far, in_other, out_other)
    )
    got_far = swap(given_far, "em")
    beside = (expert_rows, grad_slots, active, d_inner, swap(in_other, "dc"), swap(out_other, "dc"))

    late, turned, hidden_grad, output = backward_of(
        came_back.reshape(experts, 2, 2 * capacity, model_width),
        w_output,
        gain_two,
        router,
        cotangent,
        saved,
        group,
    )
    late, got_far = lax.optimization_barrier((late, got_far))
    factors = factors[:3] + [got_far] + factors[3:] + [swap(got_far, "dc")]
    late = lax.all_to_all(late, GROUP_AXES, split_axis=0, concat_axis=0, tiled=True)
    left = left_of(which[None], factors, gain_one)
    gain_rows, grad_input = first_norm_of(turned, hidden_grad, weights[:3], tokens, gain_one)
    late, left, gain_rows = lax.optimization_barrier((late, left, gain_rows))
    gather = gathered_grads if lax.axis_size("eh") == 2 else gathered_grads_plain
    grads, (grad_in, grad_out) = gather(
        late, left, gain_rows, place, small_rows, experts, beside
    )
    *grads, grad_norm, grad_ffn, grad_bias, grad_router = grads
    return (
        output,
        grad_input,
        grad_norm.reshape(model_width),
        *grads,
        grad_bias.T,
        grad_ffn.reshape(model_width),
        grad_router.T,
        grad_in[None],
        grad_out[None],
    )


def solution(mesh):
    exp_count, dp_count = mesh.shape["exp"], mesh.shape["dp"]
    fine = Mesh(
        mesh.devices.reshape(exp_count // 4, 2, 2, dp_count // 2, 2),
        TOKEN_AXES,
    )
    exp, dp = ("eh", "em", "ey"), ("dx", "dc")
    in_specs = (
        P(TOKEN_AXES, None),
        P(),
        P(),
        P(),
        P(),
        P(),
        P(),
        P(),
        P(),
        P(exp, None, dp),
        P(exp, dp, None),
        P(TOKEN_AXES, None),
        P(TOKEN_AXES),
        P(TOKEN_AXES, None),
    )
    out_specs = (
        P(TOKEN_AXES, None),
        P(TOKEN_AXES, None),
        P(),
        P(),
        P(),
        P(),
        P(),
        P(),
        P(),
        P(),
        P(exp, None, dp),
        P(exp, dp, None),
    )
    return jax.shard_map(
        per_device, mesh=fine, in_specs=in_specs, out_specs=out_specs, check_vma=False
    )
```

```python
import functools

import jax
import jax.numpy as jnp
import numpy as np
from jax import lax
from jax.experimental import pallas as pl
from jax.experimental.pallas import tpu as pltpu
from jax.sharding import Mesh
from jax.sharding import PartitionSpec as P

HEADS = 12
HEAD_DIM = 64
BUCKETS = 32
LANES = 128
VMEM_MIB = 63

norm_eps = 1e-06
score_scale = 0.125
masked_score = -1e30
far_limits = (11, 16, 22, 32, 45, 64, 90)

EXPERT_AXES = ("eh", "em", "ey", "dx")
GROUP_AXES = ("em", "ey", "dx", "dc")
TOKEN_AXES = ("eh", "em", "ey", "dx", "dc")


def bucket_of(offset):
    distance = jnp.abs(offset)
    far_bucket = jnp.full(distance.shape, 8, jnp.int32)
    for limit_value in far_limits:
        far_bucket = far_bucket + (distance >= limit_value).astype(jnp.int32)
    near_bucket = jnp.where(distance < 8, distance, far_bucket)
    return near_bucket + 16 * (offset > 0).astype(jnp.int32)


def dot_last(left_side, right_side):
    return lax.dot_general(
        left_side, right_side, (((1,), (1,)), ((), ())), preferred_element_type=jnp.float32
    )


def dot_first(left_side, right_side):
    return lax.dot_general(
        left_side, right_side, (((0,), (0,)), ((), ())), preferred_element_type=jnp.float32
    )


def norm_backward(values, factor, gain, grad_normed):
    scaled = gain * grad_normed
    grad_gain = jnp.sum(grad_normed * values * factor, axis=0, keepdims=True)
    grad_values = factor * scaled - values * factor * factor * factor * jnp.mean(
        scaled * values, axis=-1, keepdims=True
    )
    return (grad_values, grad_gain)


def swap(array, axis):
    return lax.ppermute(array, axis, perm=[(0, 1), (1, 0)])


def whole_spec():
    return pl.BlockSpec(memory_space=pltpu.VMEM)


def any_spec():
    return pl.BlockSpec(memory_space=pl.ANY)


def params(mib):
    return pltpu.CompilerParams(vmem_limit_bytes=mib * 1024 * 1024)


def cost(flops, moved):
    return pl.CostEstimate(flops=flops, bytes_accessed=moved, transcendentals=0)


def shaped(dims, kind):
    return jax.ShapeDtypeStruct(dims, kind)


class Arriving:
    def __init__(self, source, held, sem):
        self.held, self.pending = held, pltpu.make_async_copy(source, held, sem)
        self.pending.start()

    def ref(self):
        if self.pending is not None:
            self.pending.wait()
            self.pending = None
        return self.held

    def __getitem__(self, index):
        return self.ref()[index]

    @property
    def shape(self):
        return self.held.shape


def wait_all(*operands):
    for operand in operands:
        operand.ref()


class Leaving:
    def __init__(self, held, target, sem):
        self.held, self.copy = held, pltpu.make_async_copy(held, target, sem)

    def __setitem__(self, index, value):
        self.held[index] = value

    def __getitem__(self, index):
        return self.held[index]

    @property
    def shape(self):
        return self.held.shape

    def send(self):
        self.copy.start()

    def finish(self):
        self.copy.wait()


class Staying:
    def __init__(self, held):
        self.held = held

    def __setitem__(self, index, value):
        self.held[index] = value

    def __getitem__(self, index):
        return self.held[index]

    @property
    def shape(self):
        return self.held.shape

    def send(self):
        pass


def slot_rows(slot, capacity):
    if not mixed_tiles(capacity):
        return slot, slot + capacity
    main = capacity - 4
    tail = slot >= main
    return jnp.where(tail, slot + main, slot), jnp.where(tail, slot + main + 4, slot + main)


def mixed_tiles(capacity):
    return capacity > 4 and (capacity - 4) % 16 == 0


def staged(
    kernel,
    name,
    scalars,
    inputs,
    outputs,
    scratch,
    flops,
    moved,
    residents=(),
    kept=(),
    mib=VMEM_MIB,
):
    counts = (len(scalars), len(residents), len(inputs), len(kept), len(outputs))

    def body(*refs):
        refs = list(refs)
        take = lambda count: [refs.pop(0) for _ in range(count)]
        numbers, there, sources, staying, targets = [take(count) for count in counts]
        held_in, held_out = take(counts[2]), take(counts[4])
        sems = refs.pop(0)
        arriving = [
            Arriving(source, held, sems.at[i])
            for i, (source, held) in enumerate(zip(sources, held_in))
        ]
        leaving = [
            Leaving(held, target, sems.at[counts[2] + i])
            for i, (held, target) in enumerate(zip(held_out, targets))
        ]
        kernel(numbers, there + arriving, [Staying(ref) for ref in staying] + leaving, refs)
        for copy in leaving:
            copy.finish()

    return pl.pallas_call(
        body,
        out_shape=tuple(kept) + tuple(outputs),
        in_specs=[pl.BlockSpec(memory_space=pltpu.SMEM)] * counts[0]
        + [whole_spec()] * counts[1]
        + [any_spec()] * counts[2],
        out_specs=(whole_spec(),) * counts[3] + (any_spec(),) * counts[4],
        scratch_shapes=[pltpu.VMEM(x.shape, x.dtype) for x in inputs]
        + [pltpu.VMEM(x.shape, x.dtype) for x in outputs]
        + [pltpu.SemaphoreType.DMA((max(1, counts[2] + counts[4]),))]
        + list(scratch),
        compiler_params=params(mib),
        cost_estimate=cost(flops, moved),
        name=name,
    )(*scalars, *residents, *inputs)


def row_of(ref):
    return jnp.concatenate([ref[i : i + 1] for i in range(ref.shape[0])], axis=1)


def rms_factor(values):
    return lax.rsqrt(jnp.mean(values * values, axis=-1, keepdims=True) + norm_eps)


def pair_masks(rows):
    first = lax.broadcasted_iota(jnp.int32, (rows, LANES), 1) < HEAD_DIM
    return first


def stacked_heads(pair, first):
    zero = jnp.zeros_like(pair)
    return jnp.concatenate([jnp.where(first, pair, zero), jnp.where(first, zero, pair)], axis=0)


def offset_buckets(rows, length):
    lane = lax.broadcasted_iota(jnp.int32, (rows, 2 * length), 1)
    return bucket_of(jnp.where(lane < length, lane, lane - 2 * length))


def forward_kernel(numbers, inputs, outputs, scratch):
    (count_ref,) = numbers
    (
        tokens_ref,
        gain_ref,
        query_ref,
        key_ref,
        value_ref,
        bias_ref,
        routes_ref,
        output_ref,
        gain_two_ref,
        router_ref,
        cotangent_ref,
    ) = inputs
    (
        outgoing_ref,
        attended_ref,
        q_ref,
        k_ref,
        v_ref,
        probs_ref,
        hidden_ref,
        router_probs_ref,
        choose_ref,
        slot_ref,
    ) = outputs
    early, later = inputs[:7], inputs[7:]
    wait_all(*early)
    low = jnp.bfloat16
    length, width = tokens_ref.shape
    experts = router_ref.shape[0]
    capacity = outgoing_ref.shape[2] // 2
    inputs = tokens_ref[...].astype(jnp.float32)
    normed = (inputs * rms_factor(inputs) * row_of(gain_ref)).astype(low)
    for weight, out in ((query_ref, q_ref), (key_ref, k_ref), (value_ref, v_ref)):
        out[...] = jnp.dot(normed, weight[...], preferred_element_type=jnp.float32).astype(low)
        out.send()

    buckets = offset_buckets(BUCKETS, length)
    hot = buckets == lax.broadcasted_iota(jnp.int32, buckets.shape, 0)
    table = jnp.dot(
        bias_ref[...],
        jnp.where(hot, 1.0, 0.0),
        precision=lax.Precision.HIGHEST,
        preferred_element_type=jnp.float32,
    )
    live = lax.broadcasted_iota(jnp.int32, (length, length), 1) < count_ref[0]
    first = pair_masks(length)
    for pair in range(HEADS // 2):
        lanes = slice(pair * LANES, (pair + 1) * LANES)
        scores = dot_last(q_ref[:, lanes], stacked_heads(k_ref[:, lanes], first)) * score_scale
        weights = []
        for head in range(2):
            row = table[2 * pair + head : 2 * pair + head + 1]
            field = pltpu.roll(
                jnp.broadcast_to(row, (length, 2 * length)), 0, 1, stride=1, stride_axis=0
            )
            own = scores[:, head * length : (head + 1) * length] + field[:, :length]
            own = jnp.where(live, own, masked_score)
            own = jnp.exp(own - jnp.max(own, axis=1, keepdims=True))
            own = own / jnp.sum(own, axis=1, keepdims=True)
            probs_ref[pair, :, head * length : (head + 1) * length] = own
            weights.append(own.astype(low))
        both = jnp.concatenate(weights, axis=1)
        attended_ref[:, lanes] = jnp.dot(
            both, stacked_heads(v_ref[:, lanes], first), preferred_element_type=jnp.float32
        ).astype(low)

    attended_ref.send()
    probs_ref.send()
    wait_all(*later)
    hidden = inputs + jnp.dot(
        attended_ref[...], output_ref[...], preferred_element_type=jnp.float32
    )
    hidden_ref[...] = hidden
    hidden_ref.send()
    normed_two = (hidden * rms_factor(hidden) * row_of(gain_two_ref)).astype(low)
    logits = dot_last(normed_two, router_ref[...])
    router_probs = jnp.exp(logits - jnp.max(logits, axis=1, keepdims=True))
    router_probs = router_probs / jnp.sum(router_probs, axis=1, keepdims=True)
    router_probs_ref[...] = router_probs
    router_probs_ref.send()

    lane = lax.broadcasted_iota(jnp.int32, (length, length), 1)
    place = lax.broadcasted_iota(jnp.int32, (length, length), 0)
    routes = routes_ref[...]
    chosen = routes == lax.broadcasted_iota(jnp.int32, (experts, length), 0)
    chosen = jnp.where(chosen, 1.0, 0.0)
    alive = lax.broadcasted_iota(jnp.int32, (1, length), 1) < count_ref[0]
    before = jnp.where(place <= lane, 1.0, 0.0).astype(low)
    running = jnp.dot(
        (chosen * jnp.where(alive, 1.0, 0.0)).astype(low),
        before,
        preferred_element_type=jnp.float32,
    )
    slot = jnp.sum(running * chosen, axis=0, keepdims=True).astype(jnp.int32) - 1
    kept = alive & (slot < capacity)
    columns = [
        jnp.where(kept, routes * (2 * capacity) + row, -1) for row in slot_rows(slot, capacity)
    ]
    slot_ref[...] = jnp.concatenate(columns, axis=0)
    slot_ref.send()
    unit = jnp.where(place == lane, 1.0, 0.0).astype(low)
    choose = dot_last(unit, chosen.astype(low))
    choose_ref[...] = choose
    choose_ref.send()
    gate = jnp.sum(router_probs * choose, axis=1, keepdims=True)
    scaled = (gate * cotangent_ref[...].astype(jnp.float32)).astype(low)
    row = lax.broadcasted_iota(jnp.int32, (experts * 2 * capacity, length), 0)
    spread = jnp.concatenate(
        [
            jnp.where(row == columns[0], 1.0, 0.0).astype(low),
            jnp.where(row == columns[1], 1.0, 0.0).astype(low),
        ],
        axis=1,
    )
    packed = jnp.dot(
        spread,
        jnp.concatenate([normed_two, scaled], axis=0),
        preferred_element_type=jnp.float32,
    )
    for expert in range(experts):
        rows = packed[expert * 2 * capacity : (expert + 1) * 2 * capacity].astype(low)
        outgoing_ref[expert, 0] = rows
        outgoing_ref[expert, 1] = rows
    outgoing_ref.send()


def forward_of(count, tokens, gain, weights, bias, gain_two, router, routes, cotangent, capacity):
    length, width = tokens.shape
    experts = router.shape[0]
    low = jnp.bfloat16
    outputs = (
        shaped((experts, 2, 2 * capacity, width), low),
        shaped((length, width), low),
        shaped((length, width), low),
        shaped((length, width), low),
        shaped((length, width), low),
        shaped((HEADS // 2, length, 2 * length), jnp.float32),
        shaped((length, width), jnp.float32),
        shaped((length, experts), jnp.float32),
        shaped((length, experts), jnp.float32),
        shaped((2, length), jnp.int32),
    )
    query, key, value, output = weights
    inputs = (tokens, gain, query, key, value, bias, routes, output, gain_two, router, cotangent)
    return staged(
        forward_kernel,
        "forward",
        (count,),
        inputs,
        outputs,
        (),
        10 * length * width * width,
        10 * width * width,
    )


def backward_kernel(numbers, inputs, outputs, scratch):
    (
        came_ref,
        slot_ref,
        hidden_ref,
        router_probs_ref,
        choose_ref,
        cotangent_ref,
        gain_two_ref,
        router_ref,
        output_ref,
        v_ref,
        probs_ref,
        q_ref,
        k_ref,
    ) = inputs
    late_ref, turned, hidden_grad_ref, out_ref = outputs
    sums, tail = scratch
    wait_all(*inputs[1:])
    low = jnp.bfloat16
    length, width = hidden_ref.shape
    experts = router_ref.shape[0]
    capacity = came_ref.shape[2] // 2
    group = late_ref.shape[0]
    small_rows = tail.shape[0] // group
    top = cotangent_ref[...].astype(jnp.float32)
    slots = experts * 2 * capacity
    came = came_ref[:, 0].astype(jnp.float32) + came_ref[:, 1].astype(jnp.float32)
    came = came.reshape(slots, width).astype(low)
    row = lax.broadcasted_iota(jnp.int32, (slots, length), 0)
    spread = jnp.concatenate(
        [
            jnp.where(row == slot_ref[0:1], 1.0, 0.0).astype(low),
            jnp.where(row == slot_ref[1:2], 1.0, 0.0).astype(low),
        ],
        axis=1,
    )
    back = dot_first(spread, came)
    returned, d_normed_two = back[:length], back[length:]
    hidden = hidden_ref[...]
    router_probs, choose = router_probs_ref[...], choose_ref[...]
    gate = jnp.sum(router_probs * choose, axis=1, keepdims=True)
    out_ref[...] = (hidden + gate * returned).astype(low)
    out_ref.send()
    d_gate = jnp.sum(top * returned, axis=1, keepdims=True)
    d_probs = choose * d_gate
    d_logits = router_probs * (
        d_probs - jnp.sum(router_probs * d_probs, axis=1, keepdims=True)
    )
    d_logits = d_logits.astype(low)
    factor = rms_factor(hidden)
    gain_two = row_of(gain_two_ref)
    normed_two = (hidden * factor * gain_two).astype(low)
    grad_router = dot_first(d_logits, normed_two)
    d_normed_two = d_normed_two + jnp.dot(
        d_logits, router_ref[...], preferred_element_type=jnp.float32
    )
    d_from_norm, grad_ffn = norm_backward(hidden, factor, gain_two, d_normed_two)
    d_hidden = top + d_from_norm
    hidden_grad_ref[...] = d_hidden
    hidden_grad_ref.send()
    d_mixed = d_hidden.astype(low)
    d_attended = dot_last(d_mixed, output_ref[...]).astype(low)
    flipped = d_mixed.T
    for head in range(HEADS):
        at = 3 * HEADS + head
        late_ref[at // 3, at % 3 * HEAD_DIM : (at % 3 + 1) * HEAD_DIM] = flipped[
            head * HEAD_DIM : (head + 1) * HEAD_DIM
        ]

    first = pair_masks(length)
    upper = lax.broadcasted_iota(jnp.int32, (LANES, length), 0) < HEAD_DIM
    lane = lax.broadcasted_iota(jnp.int32, (length, length), 1)
    place = lax.broadcasted_iota(jnp.int32, (length, length), 0)
    reverse = jnp.where(place + lane == length - 1, 1.0, 0.0).astype(low)
    for pair in range(HEADS // 2):
        lanes = slice(pair * LANES, (pair + 1) * LANES)
        upstream = d_attended[:, lanes]
        probs = probs_ref[pair]
        d_probs = dot_last(upstream, stacked_heads(v_ref[:, lanes], first))
        parts = []
        for head in range(2):
            span = slice(head * length, (head + 1) * length)
            own, grad = probs[:, span], d_probs[:, span]
            parts.append(own * (grad - jnp.sum(own * grad, axis=1, keepdims=True)))
        d_scores = jnp.concatenate(parts, axis=1).astype(low)
        d_values = dot_first(upstream, probs.astype(low))
        d_values = jnp.where(upper, d_values[:, :length], d_values[:, length:])
        d_keys = dot_first(q_ref[:, lanes], d_scores) * score_scale
        d_keys = jnp.where(upper, d_keys[:, :length], d_keys[:, length:])
        d_queries = jnp.dot(
            d_scores, stacked_heads(k_ref[:, lanes], first), preferred_element_type=jnp.float32
        )
        d_queries = (d_queries * score_scale).astype(low)
        for which, value in enumerate(
            (d_queries.T, d_keys.astype(low), d_values.astype(low))
        ):
            turned[which, lanes] = value
            for head in range(2):
                at = which * HEADS + 2 * pair + head
                late_ref[at // 3, at % 3 * HEAD_DIM : (at % 3 + 1) * HEAD_DIM] = value[
                    head * HEAD_DIM : (head + 1) * HEAD_DIM
                ]
        upside = jnp.dot(reverse, d_scores, preferred_element_type=jnp.float32)
        for head in range(2):
            own = upside[:, head * length : (head + 1) * length]
            own = jnp.concatenate([own, jnp.zeros_like(own)], axis=1)
            own = pltpu.roll(own, 0, 1, stride=1, stride_axis=0)
            at = 2 * pair + head
            sums[at % 4, at // 4 : at // 4 + 1] = jnp.sum(own, axis=0, keepdims=True)

    turned.send()

    shift = lax.broadcasted_iota(jnp.int32, (2 * length, LANES), 0) - (length - 1)
    bucket = bucket_of(shift)
    lane_wide = lax.broadcasted_iota(jnp.int32, (2 * length, LANES), 1)
    bias_rows = 0.0
    for quarter in range(4):
        hot = jnp.where(bucket + quarter * BUCKETS == lane_wide, 1.0, 0.0)
        bias_rows = bias_rows + jnp.dot(
            sums[quarter],
            hot,
            precision=lax.Precision.HIGHEST,
            preferred_element_type=jnp.float32,
        )
    chunks = width // LANES
    tail[...] = jnp.zeros_like(tail)
    for chunk in range(chunks):
        lanes = slice(chunk * LANES, (chunk + 1) * LANES)
        tail[chunk : chunk + 1] = grad_ffn[:, lanes]
        for expert in range(experts):
            at = chunks + HEADS // 4 + expert * chunks + chunk
            tail[at : at + 1] = grad_router[expert : expert + 1, lanes]
    tail[chunks : chunks + HEADS // 4] = bias_rows[: HEADS // 4]
    block = 4 * width // group
    for at in range(group):
        own = tail[at * small_rows : (at + 1) * small_rows]
        high = own.astype(low).astype(jnp.float32)
        late_ref[at, block:] = jnp.concatenate([high, own - high], axis=0).astype(low)
    late_ref.send()


def backward_of(came, weight, gain_two, router, cotangent, saved, group):
    length, width = cotangent.shape
    experts = router.shape[0]
    low = jnp.bfloat16
    small_rows = -(-small_count(width, experts) // group)
    block = 4 * width // group
    outputs = (
        shaped((group, block + 2 * small_rows, length), low),
        shaped((3, width, length), low),
        shaped((length, width), jnp.float32),
        shaped((length, width), low),
    )
    scratch = (
        pltpu.VMEM((4, 8, 2 * length), jnp.float32),
        pltpu.VMEM((group * small_rows, LANES), jnp.float32),
    )
    q, k, v, probs, hidden, router_probs, choose, slot = saved
    inputs = (slot, hidden, router_probs, choose, cotangent, gain_two, router, weight)
    return staged(
        backward_kernel,
        "backward",
        (),
        (*inputs, v, probs, q, k),
        outputs,
        scratch,
        4 * length * width * width,
        10 * width * width,
        residents=(came,),
        mib=62,
    )


def first_norm_kernel(numbers, inputs, outputs, scratch):
    turned, hidden_grad_ref, query_ref, key_ref, value_ref, tokens_ref, gain_ref = inputs
    gain_out, grad_ref = outputs
    wait_all(*inputs)
    d_normed = 0.0
    for which, weight in enumerate((query_ref, key_ref, value_ref)):
        d_normed = d_normed + lax.dot_general(
            turned[which],
            weight[...],
            (((0,), (1,)), ((), ())),
            preferred_element_type=jnp.float32,
        )
    inputs = tokens_ref[...].astype(jnp.float32)
    d_first, grad_norm = norm_backward(
        inputs, rms_factor(inputs), row_of(gain_ref), d_normed
    )
    grad_ref[...] = (hidden_grad_ref[...] + d_first).astype(jnp.bfloat16)
    grad_ref.send()
    gain_out[...] = jnp.zeros(gain_out.shape, jnp.float32)
    for chunk in range(gain_ref.shape[0]):
        gain_out[chunk : chunk + 1] = grad_norm[:, chunk * LANES : (chunk + 1) * LANES]
    gain_out.send()


def first_norm_of(turned, hidden_grad, weights, tokens, gain):
    length, width = tokens.shape
    low = jnp.bfloat16
    rows = -(-gain.shape[0] // 8) * 8
    return staged(
        first_norm_kernel,
        "first_norm",
        (),
        (turned, hidden_grad, *weights, tokens, gain),
        (shaped((length, width), low),),
        (),
        6 * length * width * width,
        8 * width * width,
        kept=(shaped((rows, LANES), jnp.float32),),
        mib=56,
    )


def small_count(width, experts):
    return (1 + experts) * (width // LANES) + HEADS // 4


def pick_kernel(numbers, inputs, outputs, scratch):
    (which_ref,), (*pieces, tokens_ref) = numbers, inputs
    which = which_ref[0]
    pieces = [piece.ref() for piece in pieces]
    rows = pieces[0].shape[0]
    tokens_ref = tokens_ref.ref()
    if len(pieces) > 1:
        for part, piece in enumerate(pieces):
            outputs[0][part * rows : (part + 1) * rows] = piece[...]
        outputs[0].send()
    for out, turn in zip(outputs[-2:], (3, 1)):

        @pl.when(which == turn)
        def _():
            for part, piece in enumerate(pieces):
                out[part * rows : (part + 1) * rows] = piece[...]

        @pl.when(which != turn)
        def _():
            out[...] = tokens_ref[...]

        out.send()


def picked(which, pieces, tokens):
    outputs = (shaped(tokens.shape, tokens.dtype),) * (2 if len(pieces) == 1 else 3)
    return staged(
        pick_kernel,
        "picked",
        (which,),
        (*pieces, tokens),
        outputs,
        (),
        0,
        10 * tokens.size,
    )


def left_kernel(numbers, inputs, outputs, scratch):
    (which_ref,), (*pieces, gain_ref), (left_ref,) = numbers, inputs, outputs
    which = which_ref[0]
    scale = row_of(gain_ref)
    wait_all(*pieces)
    count = pieces[0].shape[0]
    spans = [
        (piece, at, slice(number * count + at, number * count + at + LANES))
        for number, piece in enumerate(pieces)
        for at in range(0, count, LANES)
    ]

    @pl.when(which < 3)
    def _():
        for piece, at, span in spans:
            own = piece[at : at + LANES].astype(jnp.float32)
            own = (own * rms_factor(own) * scale).astype(jnp.bfloat16)
            left_ref[:, span] = own.T

    @pl.when(which == 3)
    def _():
        for piece, at, span in spans:
            left_ref[:, span] = piece[at : at + LANES].T

    left_ref.send()


def left_of(which, pieces, gain):
    count, width = pieces[0].shape
    total = count * len(pieces)
    kept = (shaped((width, total), jnp.bfloat16),)
    inputs = (*pieces, gain)
    (left,) = staged(
        left_kernel,
        "left",
        (which,),
        inputs,
        (),
        (),
        10 * total * width,
        6 * total * width,
        kept=kept,
        mib=44,
    )
    return left


gelu_scale = 0.7978845608028654
gelu_cubic = 0.044715


def hidden_pass(rows, slots, part_in, part_out):
    inner = jnp.dot(rows, part_in[...], preferred_element_type=jnp.float32)
    upstream = dot_last(slots, part_out[...])
    square = inner * inner
    bent = jnp.tanh(gelu_scale * (inner + gelu_cubic * (square * inner)))
    active = (inner * (0.5 * (1.0 + bent))).astype(jnp.bfloat16)
    slope = 0.5 * (1.0 + bent) + 0.5 * inner * (1.0 - bent * bent) * (
        gelu_scale * (1.0 + 3.0 * gelu_cubic * square)
    )
    return active, (upstream * slope).astype(jnp.bfloat16)


def expert_pass(rows, slots, weights):
    result, d_rows = 0.0, 0.0
    for part_in, part_out in weights:
        active, d_inner = hidden_pass(rows, slots, part_in, part_out)
        result = result + jnp.dot(active, part_out[...], preferred_element_type=jnp.float32)
        d_rows = d_rows + dot_last(d_inner, part_in[...])
    return result, d_rows


def four_of_eight(shape):
    return lax.broadcasted_iota(jnp.int32, shape, 0) & 7 < 4


def sorted_rows(blocks_ref):
    number, height, width = blocks_ref.shape
    main = height // 2 - 4
    mixed = blocks_ref[:, 2 * main :].astype(jnp.float32).reshape(number * 8, width)
    ahead = four_of_eight(mixed.shape)
    second = pltpu.roll(mixed, number * 8 - 4, 0)
    zero = jnp.zeros_like(mixed)
    sorted_kinds = []
    for whole, rest in (
        (blocks_ref[:, :main], mixed),
        (blocks_ref[:, main : 2 * main], second),
    ):
        rest = jnp.where(ahead, rest, zero).astype(jnp.bfloat16)
        sorted_kinds.append(jnp.concatenate([whole.reshape(number * main, width), rest], axis=0))
    return sorted_kinds


def expert_kernel(numbers, inputs, outputs, scratch):
    blocks_ref, in_a, out_a, in_b, out_b = inputs
    (back_ref,) = outputs
    low = jnp.bfloat16
    blocks, height, width = blocks_ref.shape
    main = height // 2 - 4
    count = blocks * main
    rows, slots = sorted_rows(blocks_ref)
    wait_all(in_a, out_a, in_b, out_b)
    result, d_rows = expert_pass(rows, slots, ((in_a, out_a), (in_b, out_b)))
    back_ref[:, :main] = result[:count].reshape(blocks, main, width).astype(low)
    back_ref[:, main : 2 * main] = d_rows[:count].reshape(blocks, main, width).astype(low)
    mixed = result[count:]
    mixed = jnp.where(four_of_eight(mixed.shape), mixed, pltpu.roll(d_rows[count:], 4, 0))
    back_ref[:, 2 * main :] = mixed.reshape(blocks, 8, width).astype(low)
    back_ref.send()


def sorting(number, height):
    half, capacity = number * height // 2, height // 2
    place = np.arange(2 * half)
    sort = place % half // capacity * height + place // half * capacity + place % capacity
    unsort = np.empty_like(sort)
    unsort[sort] = place
    return jnp.asarray(np.stack([sort, unsort], axis=1), jnp.int32)


def rows_by_product(rows_ref, order_ref):
    count = rows_ref.shape[0]
    lanes = lax.broadcasted_iota(jnp.int32, (count, count), 1)
    sort = jnp.where(order_ref[:, 0:1] == lanes, 1.0, 0.0).astype(jnp.bfloat16)
    ordered = jnp.dot(sort, rows_ref[...], preferred_element_type=jnp.float32)
    ordered = ordered.astype(jnp.bfloat16)
    return ordered[: count // 2], ordered[count // 2 :]


def expert_sorting_kernel(numbers, inputs, outputs, scratch):
    rows_ref, order_ref, in_a, out_a, in_b, out_b = inputs
    (back_ref,) = outputs
    count = rows_ref.shape[0]
    rows, slots = rows_by_product(rows_ref, order_ref)
    result, d_rows = expert_pass(rows, slots, ((in_a, out_a), (in_b, out_b)))
    lanes = lax.broadcasted_iota(jnp.int32, (count, count), 1)
    unsort = jnp.where(order_ref[:, 1:2] == lanes, 1.0, 0.0).astype(jnp.bfloat16)
    both = jnp.concatenate([result.astype(jnp.bfloat16), d_rows.astype(jnp.bfloat16)], axis=0)
    back_ref[...] = jnp.dot(unsort, both, preferred_element_type=jnp.float32).astype(jnp.bfloat16)
    back_ref.send()


def expert_rows_of(blocks, part_weights):
    number, height, width = blocks.shape
    hidden_width = part_weights[0].shape[1]
    flops, moved = 8 * number * height * width * hidden_width, 12 * width * width
    if mixed_tiles(height // 2):
        (back,) = staged(
            expert_kernel,
            "expert_rows",
            (),
            part_weights,
            (shaped(blocks.shape, blocks.dtype),),
            (),
            flops,
            moved,
            residents=(blocks,),
            mib=62,
        )
        return back
    (back,) = staged(
        expert_sorting_kernel,
        "expert_rows",
        (),
        (blocks.reshape(-1, width), sorting(number, height), *part_weights),
        (shaped((number * height, width), blocks.dtype),),
        (),
        flops,
        moved,
    )
    return back.reshape(blocks.shape)


def grads_kernel(mixed, numbers, inputs, outputs, scratch):
    wait_all(*inputs)
    if mixed:
        blocks_ref, part_in, part_out, *got = inputs
        rows, slots = sorted_rows(blocks_ref)
    else:
        rows_ref, order_ref, part_in, part_out, *got = inputs
        rows, slots = rows_by_product(rows_ref, order_ref)
    active, d_inner = hidden_pass(rows, slots, part_in, part_out)
    for number, (left, right) in enumerate(((rows, d_inner), (active, slots))):
        grad = dot_first(left, right)
        if got:
            outputs[number][...] = grad + got[number][...].astype(jnp.float32)
        else:
            outputs[number][...] = grad.astype(jnp.bfloat16)
        outputs[number].send()


def expert_grads_of(blocks, part_in, part_out, *got):
    number, height, width = blocks.shape
    hidden_width = part_in.shape[1]
    mixed = mixed_tiles(height // 2)
    kind = jnp.float32 if got else jnp.bfloat16
    outputs = (shaped((width, hidden_width), kind), shaped((hidden_width, width), kind))
    rows = (blocks,) if mixed else (blocks.reshape(-1, width), sorting(number, height))
    return staged(
        functools.partial(grads_kernel, mixed),
        "own_grads" if got else "sent_grads",
        (),
        (*rows, part_in, part_out, *got),
        outputs,
        (),
        0 if got else 4 * number * height * width * hidden_width,
        0 if got else 8 * width * width,
    )


def in_parts(values):
    high = values.astype(jnp.bfloat16).astype(jnp.float32)
    return jnp.concatenate([high, values - high], axis=0).astype(jnp.bfloat16)


def from_parts(parts):
    parts = parts.astype(jnp.float32)
    rows = parts.shape[0] // 2
    return parts[:rows] + parts[rows:]


def block_kernel(numbers, inputs, outputs, scratch):
    (bits_ref,), (late_ref, left_ref, gain_ref), (block_ref,) = numbers, inputs, outputs
    group = late_ref.shape[0]
    part = left_ref.shape[0] // 2
    block = left_ref.shape[0] * 4 // group
    edge = block - LANES
    half = part // 2
    gain_edge = block_ref.shape[1] - 2 * gain_ref.shape[0]
    odd = bits_ref[3] == 1
    here = bits_ref[0] * 8 + bits_ref[1] * 4 + bits_ref[2] * 2 + bits_ref[3]
    right = jnp.concatenate(
        [late_ref[here ^ factor_order(i), :block] for i in range(group)], axis=1
    )
    right = jnp.where(odd, jnp.concatenate([right[edge:], right[:edge]], axis=0), right)
    total = dot_last(left_ref[...], right)
    first = pair_masks(half)
    small = in_parts(from_parts(jnp.sum(late_ref[:, block:].astype(jnp.float32), axis=0)))
    gain = in_parts(gain_ref[...])
    for side in range(2):
        own = total[side * part : (side + 1) * part]
        block_ref[side, :part] = own[:, :LANES].astype(jnp.bfloat16)
        rest = own[:, LANES:]
        rest = jnp.concatenate([rest, rest], axis=1)
        upper, lower = rest[:half], rest[half:]
        even = jnp.where(first, upper, lower)
        packed = jnp.where(odd, jnp.where(first, lower, upper), even)
        block_ref[side, part : part + half] = packed.astype(jnp.bfloat16)
        block_ref[side, part + half : gain_edge] = small
        block_ref[side, gain_edge:] = gain


def block_of(bits, late, left, gain, small_rows):
    group, rows, length = late.shape
    width = left.shape[0]
    height = 3 * width // 4 + 2 * (small_rows + gain.shape[0])
    (block,) = staged(
        block_kernel,
        "grad_block",
        (bits,),
        (),
        (),
        (),
        8 * width * width * length,
        2 * left.size,
        residents=(late, left, gain),
        kept=(shaped((2, height, LANES), jnp.bfloat16),),
        mib=24,
    )
    return block


def share_kernel(edge, small_rows, numbers, inputs, outputs, scratch):
    (own_ref, got_ref), (share_ref,) = inputs, outputs
    gain_edge = edge + 2 * small_rows
    for side in range(2):
        own = own_ref[side, :edge].astype(jnp.float32) + got_ref[side, :edge].astype(jnp.float32)
        share_ref[side, :edge] = own.astype(jnp.bfloat16)
        for rows in (slice(edge, gain_edge), slice(gain_edge, None)):
            share_ref[side, rows] = in_parts(
                from_parts(own_ref[side, rows]) + from_parts(got_ref[side, rows])
            )


def share_of(own, got, edge, small_rows):
    (share,) = staged(
        functools.partial(share_kernel, edge, small_rows),
        "share",
        (),
        (),
        (),
        (),
        own.size,
        6 * own.size,
        residents=(own, got),
        kept=(shaped(own.shape, own.dtype),),
        mib=8,
    )
    return share


def assemble_kernel(weights, small_rows, bits_ref, sources, outs, made, out_sems, put_small):
    em, ey, dx, dc = [bits_ref[i] for i in range(4)]
    part = made.shape[1] // 2
    half = part // 2
    edge = part + half
    first = pair_masks(half)
    def copy_of(number, side, target):
        rows = pl.ds(side * part, part)
        return pltpu.make_async_copy(
            made.at[number, rows], target.at[rows], out_sems.at[2 * number + side]
        )

    for number, weight in enumerate(weights):
        truth = (em ^ (weight // 2)) * 2 + (ey ^ (weight % 2))
        for side in range(2):
            for here in range(4):

                @pl.when(dx * 2 + dc == here)
                def _():
                    own = [
                        sources[4 * number + 2 * ((i ^ here) & 1) + ((i ^ here) >> 1)]
                        for i in range(4)
                    ]
                    rows = slice(side * part, (side + 1) * part)
                    upper = slice(side * part, side * part + half)
                    lower = slice(side * part + half, (side + 1) * part)
                    for twin in range(2):
                        even, odd = own[2 * twin], own[2 * twin + 1]
                        at = 3 * twin * LANES
                        made[number, rows, at : at + LANES] = even[side, :part].astype(jnp.float32)
                        made[number, rows, at + 2 * LANES : at + 3 * LANES] = odd[
                            side, :part
                        ].astype(jnp.float32)
                        left = even[side, part:edge].astype(jnp.float32)
                        right = odd[side, part:edge].astype(jnp.float32)
                        middle = slice(at + LANES, at + 2 * LANES)
                        made[number, upper, middle] = jnp.where(first, left, right)
                        made[number, lower, middle] = pltpu.roll(
                            jnp.where(first, right, left), HEAD_DIM, 1
                        )
                    for i in range(4 if side == 0 else 0):
                        tail = own[i][0, edge:].astype(jnp.float32)
                        gain = tail[2 * small_rows :]
                        gain_rows = gain.shape[0] // 2
                        put_small(
                            number,
                            i,
                            jnp.concatenate(
                                [
                                    tail[:small_rows] + tail[small_rows : 2 * small_rows],
                                    gain[:gain_rows] + gain[gain_rows:],
                                ],
                                axis=0,
                            ),
                        )

            for i in range(4):

                @pl.when(truth == i)
                def _():
                    copy_of(number, side, outs[i]).start()

    for number, weight in enumerate(weights):
        truth = (em ^ (weight // 2)) * 2 + (ey ^ (weight % 2))
        for i in range(4):

            @pl.when(truth == i)
            def _():
                for side in range(2):
                    copy_of(number, side, outs[i]).wait()


def first_half_kernel(small_rows, bits_ref, *refs):
    sources, outs, small_out, made, out_sems = refs[:8], refs[8:12], refs[12], refs[13], refs[14]

    def put_small(number, i, rows):
        small_out[number, i] = rows

    assemble_kernel((0, 2), small_rows, bits_ref, sources, outs, made, out_sems, put_small)


def second_half_kernel(small_rows, bits_ref, *refs):
    sources, small_ref, outs = refs[:8], refs[8], refs[13:17]
    norm_out, ffn_out, bias_out, router_out = refs[17:21]
    made, tail, out_sems = refs[21:]
    em, ey = bits_ref[0], bits_ref[1]
    for number in range(2):
        tail[(em ^ number) * 2 + ey] = small_ref[number]

    def put_small(number, i, rows):
        tail[(em ^ number) * 2 + (ey ^ 1), i] = rows

    assemble_kernel((1, 3), small_rows, bits_ref, sources, outs, made, out_sems, put_small)

    def small_row(at):
        at, row = divmod(at, small_rows)
        return tail[at // 4, at % 4, row : row + 1]

    chunks = made.shape[2] // LANES
    total = 0.0
    for at in range(16):
        total = total + tail[at // 4, at % 4, small_rows:]
    norm_out[...] = total[:chunks]
    for chunk in range(chunks):
        lanes = slice(chunk * LANES, (chunk + 1) * LANES)
        ffn_out[chunk : chunk + 1] = small_row(chunk)
        for expert in range(router_out.shape[0]):
            router_out[expert : expert + 1, lanes] = small_row(
                chunks + HEADS // 4 + expert * chunks + chunk
            )
    for head in range(HEADS):
        at = head % 4 * BUCKETS
        bias_out[head : head + 1] = small_row(chunks + head // 4)[:, at : at + BUCKETS]


def first_half(bits, sources, small_rows, width):
    gain_rows = (sources[0].shape[1] - 3 * width // 4 - 2 * small_rows) // 2
    *grads, small = pl.pallas_call(
        functools.partial(first_half_kernel, small_rows),
        out_shape=(shaped((width, width), jnp.float32),) * 4
        + (shaped((2, 4, small_rows + gain_rows, LANES), jnp.float32),),
        in_specs=[pl.BlockSpec(memory_space=pltpu.SMEM)] + [whole_spec()] * 8,
        out_specs=(any_spec(),) * 4 + (whole_spec(),),
        scratch_shapes=[
            pltpu.VMEM((2, width, width), jnp.float32),
            pltpu.SemaphoreType.DMA((4,)),
        ],
        compiler_params=params(16),
        cost_estimate=cost(8 * width * width, 12 * width * width),
        name="first_half",
    )(bits, *sources)
    return grads, small


def second_half(bits, sources, small, grads, small_rows, width, experts):
    return pl.pallas_call(
        functools.partial(second_half_kernel, small_rows),
        out_shape=(shaped((width, width), jnp.float32),) * 4
        + (
            shaped((width // LANES, LANES), jnp.float32),
            shaped((width // LANES, LANES), jnp.float32),
            shaped((HEADS, BUCKETS), jnp.float32),
            shaped((experts, width), jnp.float32),
        ),
        in_specs=[pl.BlockSpec(memory_space=pltpu.SMEM)]
        + [whole_spec()] * 9
        + [any_spec()] * 4,
        out_specs=(any_spec(),) * 4 + (whole_spec(),) * 4,
        input_output_aliases={10 + i: i for i in range(4)},
        scratch_shapes=[
            pltpu.VMEM((2, width, width), jnp.float32),
            pltpu.VMEM((4, 4) + small.shape[2:], jnp.float32),
            pltpu.SemaphoreType.DMA((4,)),
        ],
        compiler_params=params(16),
        cost_estimate=cost(8 * width * width, 12 * width * width),
        name="second_half",
    )(bits, *sources, small, *grads)


def place_in_group():
    place = [lax.axis_index(axis) for axis in ("em", "ey", "dx", "dc")]
    return (2 * place[0] + place[1]).astype(jnp.int32), jnp.stack(place).astype(jnp.int32)


def factor_order(at):
    return (at & 1) * 2 + (at >> 1 & 1) * 4 + (at >> 2 & 1) * 8 + (at >> 3)


def with_other(rows, axis):
    return jnp.concatenate([rows, swap(rows, axis)], axis=0)


def gathered_grads(late, left, gain_rows, place, small_rows, experts, beside):
    width = left.shape[0]
    block = block_of(place, late, left, gain_rows, small_rows)
    block, beside = lax.optimization_barrier((block, beside))
    beside = expert_grads_of(*beside)
    got, beside = lax.optimization_barrier((swap(block, "eh"), beside))
    near = share_of(block, got, 3 * width // 4, small_rows)
    far, near_x, near_y = swap(near, "em"), swap(near, "dx"), swap(near, "ey")
    far_x, far_y = swap(far, "dx"), swap(far, "ey")
    near_both, far_both = swap(near_x, "ey"), swap(far_y, "dx")

    def both_cores(*sources):
        return sources + tuple(swap(source, "dc") for source in sources)

    sources = both_cores(near, near_x) + both_cores(far, far_x)
    grads, small = first_half(place, sources, small_rows, width)
    sources = both_cores(near_y, near_both) + both_cores(far_y, far_both)
    grads = second_half(place, sources, small, grads, small_rows, width, experts)
    return grads, beside


def gathered_grads_plain(late, left, gain_rows, place, small_rows, experts, beside):
    group, rows, length = late.shape
    width = left.shape[0]
    block = 4 * width // group
    small = jnp.sum(late[:, block:].astype(jnp.float32), axis=0)
    small = lax.psum(small[:small_rows] + small[small_rows:], "eh")
    order = jnp.asarray([factor_order(at) for at in range(group)], jnp.int32)
    order = order ^ lax.axis_index(GROUP_AXES)
    late_block = jnp.take(late[:, :block], order, axis=0)
    late_block = late_block.transpose(1, 0, 2).reshape(block, group * length)
    grad_block = dot_last(late_block, left)
    mine = lax.psum_scatter(grad_block, "eh", scatter_dimension=0, tiled=True)
    grads = lax.all_gather(mine.astype(jnp.bfloat16), "eh", axis=0, tiled=True)
    grads = lax.all_gather(grads, GROUP_AXES, axis=0, tiled=True)
    small = lax.all_gather(small, GROUP_AXES, axis=0, tiled=True).reshape(-1)
    grads = grads.reshape(4, width, width).transpose(0, 2, 1).astype(jnp.float32)
    sizes = (width, HEADS * BUCKETS, experts * width)
    ends = np.cumsum(sizes)
    pieces = [small[end - size : end] for end, size in zip(ends, sizes)]
    pieces[1], pieces[2] = pieces[1].reshape(HEADS, BUCKETS), pieces[2].reshape(experts, width)
    grad_norm = lax.psum(gain_rows, TOKEN_AXES)[: width // LANES]
    return (*grads, grad_norm, *pieces), expert_grads_of(*beside)


def per_device(
    tokens,
    norm_gain,
    w_query,
    w_key,
    w_value,
    w_output,
    rel_bias,
    ffn_gain,
    w_router,
    w_in,
    w_out,
    routes,
    lengths,
    cotangent,
):
    length, model_width = tokens.shape
    experts = w_router.shape[1]
    group = lax.axis_size(GROUP_AXES)
    capacity = max(2, (5 * length + 4 * experts - 1) // (4 * experts))
    small_rows = -(-small_count(model_width, experts) // group)
    gain_one, gain_two = norm_gain.reshape(-1, LANES), ffn_gain.reshape(-1, LANES)
    weights = (w_query, w_key, w_value, w_output)
    router = w_router.T

    w_in_own, w_out_own = w_in[0], w_out[0]
    w_in_other, w_out_other = swap(w_in_own, "dc"), swap(w_out_own, "dc")
    outgoing, attended, *saved = forward_of(
        lengths,
        tokens,
        gain_one,
        weights,
        rel_bias.T,
        gain_two,
        router,
        routes.reshape(1, length),
        cotangent,
        capacity,
    )
    which, place = place_in_group()
    outgoing, near_tokens = lax.optimization_barrier((outgoing, with_other(tokens, "dx")))
    outgoing = outgoing.reshape(2 * experts, 2 * capacity, model_width)
    incoming = lax.all_to_all(outgoing, EXPERT_AXES, split_axis=0, concat_axis=0, tiled=True)
    far_tokens = swap(near_tokens, "ey")
    near_attended, own_near, given_near = picked(
        which[None], (attended, swap(attended, "dx")), near_tokens
    )
    far_attended, got_near = swap(near_attended, "ey"), swap(given_near, "em")
    incoming, far_tokens, _ = lax.optimization_barrier((incoming, far_tokens, given_near))
    sent_back = expert_rows_of(incoming, (w_in_own, w_out_own, w_in_other, w_out_other))
    sent_back, far_attended, got_near = lax.optimization_barrier(
        (sent_back, far_attended, got_near)
    )
    came_back = lax.all_to_all(sent_back, EXPERT_AXES, split_axis=0, concat_axis=0, tiled=True)
    own_far, given_far = picked(which[None], (far_attended,), far_tokens)
    incoming, _ = lax.optimization_barrier((incoming, sent_back))
    in_other, out_other = expert_grads_of(incoming, w_in_other, w_out_other)
    factors = [own_near, own_far, got_near]
    factors = factors + [swap(rows, "dc") for rows in factors]
    came_back, factors, given_far, in_other, out_other = lax.optimization_barrier(
        (came_back, factors, given_far, in_other, out_other)
    )
    got_far = swap(given_far, "em")
    beside = (incoming, w_in_own, w_out_own, swap(in_other, "dc"), swap(out_other, "dc"))

    late, turned, hidden_grad, output = backward_of(
        came_back.reshape(experts, 2, 2 * capacity, model_width),
        w_output,
        gain_two,
        router,
        cotangent,
        saved,
        group,
    )
    late, got_far = lax.optimization_barrier((late, got_far))
    factors = factors[:3] + [got_far] + factors[3:] + [swap(got_far, "dc")]
    late = lax.all_to_all(late, GROUP_AXES, split_axis=0, concat_axis=0, tiled=True)
    left = left_of(which[None], factors, gain_one)
    gain_rows, grad_input = first_norm_of(turned, hidden_grad, weights[:3], tokens, gain_one)
    late, left, gain_rows, beside = lax.optimization_barrier((late, left, gain_rows, beside))
    gather = gathered_grads if lax.axis_size("eh") == 2 else gathered_grads_plain
    grads, (grad_in, grad_out) = gather(
        late, left, gain_rows, place, small_rows, experts, beside
    )
    *grads, grad_norm, grad_ffn, grad_bias, grad_router = grads
    return (
        output,
        grad_input,
        grad_norm.reshape(model_width),
        *grads,
        grad_bias.T,
        grad_ffn.reshape(model_width),
        grad_router.T,
        grad_in[None],
        grad_out[None],
    )


def solution(mesh):
    exp_count, dp_count = mesh.shape["exp"], mesh.shape["dp"]
    fine = Mesh(
        mesh.devices.reshape(exp_count // 4, 2, 2, dp_count // 2, 2),
        TOKEN_AXES,
    )
    exp, dp = ("eh", "em", "ey"), ("dx", "dc")
    in_specs = (
        P(TOKEN_AXES, None),
        P(),
        P(),
        P(),
        P(),
        P(),
        P(),
        P(),
        P(),
        P(exp, None, dp),
        P(exp, dp, None),
        P(TOKEN_AXES, None),
        P(TOKEN_AXES),
        P(TOKEN_AXES, None),
    )
    out_specs = (
        P(TOKEN_AXES, None),
        P(TOKEN_AXES, None),
        P(),
        P(),
        P(),
        P(),
        P(),
        P(),
        P(),
        P(),
        P(exp, None, dp),
        P(exp, dp, None),
    )
    return jax.shard_map(
        per_device, mesh=fine, in_specs=in_specs, out_specs=out_specs, check_vma=False
    )
```

```python
import functools

import jax
import jax.numpy as jnp
import numpy as np
from jax import lax
from jax.experimental import pallas as pl
from jax.experimental.pallas import tpu as pltpu
from jax.sharding import Mesh
from jax.sharding import PartitionSpec as P

HEADS = 12
HEAD_DIM = 64
BUCKETS = 32
LANES = 128
VMEM_MIB = 63

norm_eps = 1e-06
score_scale = 0.125
masked_score = -1e30
far_limits = (11, 16, 22, 32, 45, 64, 90)

EXPERT_AXES = ("eh", "em", "ey", "dx")
GROUP_AXES = ("em", "ey", "dx", "dc")
TOKEN_AXES = ("eh", "em", "ey", "dx", "dc")


def bucket_of(offset):
    distance = jnp.abs(offset)
    far_bucket = jnp.full(distance.shape, 8, jnp.int32)
    for limit_value in far_limits:
        far_bucket = far_bucket + (distance >= limit_value).astype(jnp.int32)
    near_bucket = jnp.where(distance < 8, distance, far_bucket)
    return near_bucket + 16 * (offset > 0).astype(jnp.int32)


def dot_last(left_side, right_side):
    return lax.dot_general(
        left_side, right_side, (((1,), (1,)), ((), ())), preferred_element_type=jnp.float32
    )


def dot_first(left_side, right_side):
    return lax.dot_general(
        left_side, right_side, (((0,), (0,)), ((), ())), preferred_element_type=jnp.float32
    )


def norm_backward(values, factor, gain, grad_normed):
    scaled = gain * grad_normed
    grad_gain = jnp.sum(grad_normed * values * factor, axis=0, keepdims=True)
    grad_values = factor * scaled - values * factor * factor * factor * jnp.mean(
        scaled * values, axis=-1, keepdims=True
    )
    return (grad_values, grad_gain)


def swap(array, axis):
    return lax.ppermute(array, axis, perm=[(0, 1), (1, 0)])


def whole_spec():
    return pl.BlockSpec(memory_space=pltpu.VMEM)


def any_spec():
    return pl.BlockSpec(memory_space=pl.ANY)


def params(mib):
    return pltpu.CompilerParams(vmem_limit_bytes=mib * 1024 * 1024)


def cost(flops, moved):
    return pl.CostEstimate(flops=flops, bytes_accessed=moved, transcendentals=0)


def shaped(dims, kind):
    return jax.ShapeDtypeStruct(dims, kind)


class Arriving:
    def __init__(self, source, held, sem):
        self.held, self.pending = held, pltpu.make_async_copy(source, held, sem)
        self.pending.start()

    def ref(self):
        if self.pending is not None:
            self.pending.wait()
            self.pending = None
        return self.held

    def __getitem__(self, index):
        return self.ref()[index]

    @property
    def shape(self):
        return self.held.shape


def wait_all(*operands):
    for operand in operands:
        operand.ref()


class Leaving:
    def __init__(self, held, target, sem):
        self.held, self.copy = held, pltpu.make_async_copy(held, target, sem)

    def __setitem__(self, index, value):
        self.held[index] = value

    def __getitem__(self, index):
        return self.held[index]

    @property
    def shape(self):
        return self.held.shape

    def send(self):
        self.copy.start()

    def finish(self):
        self.copy.wait()


class Staying:
    def __init__(self, held):
        self.held = held

    def __setitem__(self, index, value):
        self.held[index] = value

    def __getitem__(self, index):
        return self.held[index]

    @property
    def shape(self):
        return self.held.shape

    def send(self):
        pass


def slot_rows(slot, capacity):
    if not mixed_tiles(capacity):
        return slot, slot + capacity
    main = capacity - 4
    tail = slot >= main
    return jnp.where(tail, slot + main, slot), jnp.where(tail, slot + main + 4, slot + main)


def mixed_tiles(capacity):
    return capacity > 4 and (capacity - 4) % 16 == 0


def staged(
    kernel,
    name,
    scalars,
    inputs,
    outputs,
    scratch,
    flops,
    moved,
    residents=(),
    kept=(),
    mib=VMEM_MIB,
):
    counts = (len(scalars), len(residents), len(inputs), len(kept), len(outputs))

    def body(*refs):
        refs = list(refs)
        take = lambda count: [refs.pop(0) for _ in range(count)]
        numbers, there, sources, staying, targets = [take(count) for count in counts]
        held_in, held_out = take(counts[2]), take(counts[4])
        sems = refs.pop(0)
        arriving = [
            Arriving(source, held, sems.at[i])
            for i, (source, held) in enumerate(zip(sources, held_in))
        ]
        leaving = [
            Leaving(held, target, sems.at[counts[2] + i])
            for i, (held, target) in enumerate(zip(held_out, targets))
        ]
        kernel(numbers, there + arriving, [Staying(ref) for ref in staying] + leaving, refs)
        for copy in leaving:
            copy.finish()

    return pl.pallas_call(
        body,
        out_shape=tuple(kept) + tuple(outputs),
        in_specs=[pl.BlockSpec(memory_space=pltpu.SMEM)] * counts[0]
        + [whole_spec()] * counts[1]
        + [any_spec()] * counts[2],
        out_specs=(whole_spec(),) * counts[3] + (any_spec(),) * counts[4],
        scratch_shapes=[pltpu.VMEM(x.shape, x.dtype) for x in inputs]
        + [pltpu.VMEM(x.shape, x.dtype) for x in outputs]
        + [pltpu.SemaphoreType.DMA((max(1, counts[2] + counts[4]),))]
        + list(scratch),
        compiler_params=params(mib),
        cost_estimate=cost(flops, moved),
        name=name,
    )(*scalars, *residents, *inputs)


def row_of(ref):
    return jnp.concatenate([ref[i : i + 1] for i in range(ref.shape[0])], axis=1)


def rms_factor(values):
    return lax.rsqrt(jnp.mean(values * values, axis=-1, keepdims=True) + norm_eps)


def pair_masks(rows):
    first = lax.broadcasted_iota(jnp.int32, (rows, LANES), 1) < HEAD_DIM
    return first


def stacked_heads(pair, first):
    zero = jnp.zeros_like(pair)
    return jnp.concatenate([jnp.where(first, pair, zero), jnp.where(first, zero, pair)], axis=0)


def offset_buckets(rows, length):
    lane = lax.broadcasted_iota(jnp.int32, (rows, 2 * length), 1)
    return bucket_of(jnp.where(lane < length, lane, lane - 2 * length))


def forward_kernel(numbers, inputs, outputs, scratch):
    (count_ref,) = numbers
    (
        tokens_ref,
        gain_ref,
        query_ref,
        key_ref,
        value_ref,
        bias_ref,
        routes_ref,
        output_ref,
        gain_two_ref,
        router_ref,
        cotangent_ref,
    ) = inputs
    (
        outgoing_ref,
        attended_ref,
        q_ref,
        k_ref,
        v_ref,
        probs_ref,
        hidden_ref,
        router_probs_ref,
        choose_ref,
        slot_ref,
    ) = outputs
    early, later = inputs[:7], inputs[7:]
    wait_all(*early)
    low = jnp.bfloat16
    length, width = tokens_ref.shape
    experts = router_ref.shape[0]
    capacity = outgoing_ref.shape[2] // 2
    inputs = tokens_ref[...].astype(jnp.float32)
    normed = (inputs * rms_factor(inputs) * row_of(gain_ref)).astype(low)
    for weight, out in ((query_ref, q_ref), (key_ref, k_ref), (value_ref, v_ref)):
        out[...] = jnp.dot(normed, weight[...], preferred_element_type=jnp.float32).astype(low)
        out.send()

    buckets = offset_buckets(BUCKETS, length)
    hot = buckets == lax.broadcasted_iota(jnp.int32, buckets.shape, 0)
    table = jnp.dot(
        bias_ref[...],
        jnp.where(hot, 1.0, 0.0),
        precision=lax.Precision.HIGHEST,
        preferred_element_type=jnp.float32,
    )
    live = lax.broadcasted_iota(jnp.int32, (length, length), 1) < count_ref[0]
    first = pair_masks(length)
    for pair in range(HEADS // 2):
        lanes = slice(pair * LANES, (pair + 1) * LANES)
        scores = dot_last(q_ref[:, lanes], stacked_heads(k_ref[:, lanes], first)) * score_scale
        weights = []
        for head in range(2):
            row = table[2 * pair + head : 2 * pair + head + 1]
            field = pltpu.roll(
                jnp.broadcast_to(row, (length, 2 * length)), 0, 1, stride=1, stride_axis=0
            )
            own = scores[:, head * length : (head + 1) * length] + field[:, :length]
            own = jnp.where(live, own, masked_score)
            own = jnp.exp(own - jnp.max(own, axis=1, keepdims=True))
            own = own / jnp.sum(own, axis=1, keepdims=True)
            probs_ref[pair, :, head * length : (head + 1) * length] = own
            weights.append(own.astype(low))
        both = jnp.concatenate(weights, axis=1)
        attended_ref[:, lanes] = jnp.dot(
            both, stacked_heads(v_ref[:, lanes], first), preferred_element_type=jnp.float32
        ).astype(low)

    attended_ref.send()
    probs_ref.send()
    wait_all(*later)
    hidden = inputs + jnp.dot(
        attended_ref[...], output_ref[...], preferred_element_type=jnp.float32
    )
    hidden_ref[...] = hidden
    hidden_ref.send()
    normed_two = (hidden * rms_factor(hidden) * row_of(gain_two_ref)).astype(low)
    logits = dot_last(normed_two, router_ref[...])
    router_probs = jnp.exp(logits - jnp.max(logits, axis=1, keepdims=True))
    router_probs = router_probs / jnp.sum(router_probs, axis=1, keepdims=True)
    router_probs_ref[...] = router_probs
    router_probs_ref.send()

    lane = lax.broadcasted_iota(jnp.int32, (length, length), 1)
    place = lax.broadcasted_iota(jnp.int32, (length, length), 0)
    routes = routes_ref[...]
    chosen = routes == lax.broadcasted_iota(jnp.int32, (experts, length), 0)
    chosen = jnp.where(chosen, 1.0, 0.0)
    alive = lax.broadcasted_iota(jnp.int32, (1, length), 1) < count_ref[0]
    before = jnp.where(place <= lane, 1.0, 0.0).astype(low)
    running = jnp.dot(
        (chosen * jnp.where(alive, 1.0, 0.0)).astype(low),
        before,
        preferred_element_type=jnp.float32,
    )
    slot = jnp.sum(running * chosen, axis=0, keepdims=True).astype(jnp.int32) - 1
    kept = alive & (slot < capacity)
    columns = [
        jnp.where(kept, routes * (2 * capacity) + row, -1) for row in slot_rows(slot, capacity)
    ]
    slot_ref[...] = jnp.concatenate(columns, axis=0)
    slot_ref.send()
    unit = jnp.where(place == lane, 1.0, 0.0).astype(low)
    choose = dot_last(unit, chosen.astype(low))
    choose_ref[...] = choose
    choose_ref.send()
    gate = jnp.sum(router_probs * choose, axis=1, keepdims=True)
    scaled = (gate * cotangent_ref[...].astype(jnp.float32)).astype(low)
    row = lax.broadcasted_iota(jnp.int32, (experts * 2 * capacity, length), 0)
    spread = jnp.concatenate(
        [
            jnp.where(row == columns[0], 1.0, 0.0).astype(low),
            jnp.where(row == columns[1], 1.0, 0.0).astype(low),
        ],
        axis=1,
    )
    packed = jnp.dot(
        spread,
        jnp.concatenate([normed_two, scaled], axis=0),
        preferred_element_type=jnp.float32,
    )
    for expert in range(experts):
        rows = packed[expert * 2 * capacity : (expert + 1) * 2 * capacity].astype(low)
        outgoing_ref[expert, 0] = rows
        outgoing_ref[expert, 1] = rows
    outgoing_ref.send()


def forward_of(count, tokens, gain, weights, bias, gain_two, router, routes, cotangent, capacity):
    length, width = tokens.shape
    experts = router.shape[0]
    low = jnp.bfloat16
    outputs = (
        shaped((experts, 2, 2 * capacity, width), low),
        shaped((length, width), low),
        shaped((length, width), low),
        shaped((length, width), low),
        shaped((length, width), low),
        shaped((HEADS // 2, length, 2 * length), jnp.float32),
        shaped((length, width), jnp.float32),
        shaped((length, experts), jnp.float32),
        shaped((length, experts), jnp.float32),
        shaped((2, length), jnp.int32),
    )
    query, key, value, output = weights
    inputs = (tokens, gain, query, key, value, bias, routes, output, gain_two, router, cotangent)
    return staged(
        forward_kernel,
        "forward",
        (count,),
        inputs,
        outputs,
        (),
        10 * length * width * width,
        10 * width * width,
    )


def backward_kernel(numbers, inputs, outputs, scratch):
    (
        came_ref,
        slot_ref,
        hidden_ref,
        router_probs_ref,
        choose_ref,
        cotangent_ref,
        gain_two_ref,
        router_ref,
        output_ref,
        v_ref,
        probs_ref,
        q_ref,
        k_ref,
    ) = inputs
    late_ref, hidden_grad_ref, out_ref = outputs
    sums, tail = scratch
    early, later = inputs[1:9], inputs[9:]
    wait_all(*early)
    low = jnp.bfloat16
    length, width = hidden_ref.shape
    experts = router_ref.shape[0]
    capacity = came_ref.shape[2] // 2
    group = late_ref.shape[0]
    small_rows = tail.shape[0] // group
    top = cotangent_ref[...].astype(jnp.float32)
    slots = experts * 2 * capacity
    came = came_ref[:, 0].astype(jnp.float32) + came_ref[:, 1].astype(jnp.float32)
    came = came.reshape(slots, width).astype(low)
    row = lax.broadcasted_iota(jnp.int32, (slots, length), 0)
    spread = jnp.concatenate(
        [
            jnp.where(row == slot_ref[0:1], 1.0, 0.0).astype(low),
            jnp.where(row == slot_ref[1:2], 1.0, 0.0).astype(low),
        ],
        axis=1,
    )
    back = dot_first(spread, came)
    returned, d_normed_two = back[:length], back[length:]
    hidden = hidden_ref[...]
    router_probs, choose = router_probs_ref[...], choose_ref[...]
    gate = jnp.sum(router_probs * choose, axis=1, keepdims=True)
    out_ref[...] = (hidden + gate * returned).astype(low)
    out_ref.send()
    d_gate = jnp.sum(top * returned, axis=1, keepdims=True)
    d_probs = choose * d_gate
    d_logits = router_probs * (
        d_probs - jnp.sum(router_probs * d_probs, axis=1, keepdims=True)
    )
    d_logits = d_logits.astype(low)
    factor = rms_factor(hidden)
    gain_two = row_of(gain_two_ref)
    normed_two = (hidden * factor * gain_two).astype(low)
    grad_router = dot_first(d_logits, normed_two)
    d_normed_two = d_normed_two + jnp.dot(
        d_logits, router_ref[...], preferred_element_type=jnp.float32
    )
    d_from_norm, grad_ffn = norm_backward(hidden, factor, gain_two, d_normed_two)
    d_hidden = top + d_from_norm
    hidden_grad_ref[...] = d_hidden
    hidden_grad_ref.send()
    d_mixed = d_hidden.astype(low)
    d_attended = dot_last(d_mixed, output_ref[...]).astype(low)
    flipped = d_mixed.T
    for head in range(HEADS):
        at = 3 * HEADS + head
        late_ref[at // 3, at % 3 * HEAD_DIM : (at % 3 + 1) * HEAD_DIM] = flipped[
            head * HEAD_DIM : (head + 1) * HEAD_DIM
        ]

    wait_all(*later)
    first = pair_masks(length)
    upper = lax.broadcasted_iota(jnp.int32, (LANES, length), 0) < HEAD_DIM
    lane = lax.broadcasted_iota(jnp.int32, (length, length), 1)
    place = lax.broadcasted_iota(jnp.int32, (length, length), 0)
    reverse = jnp.where(place + lane == length - 1, 1.0, 0.0).astype(low)
    for pair in range(HEADS // 2):
        lanes = slice(pair * LANES, (pair + 1) * LANES)
        upstream = d_attended[:, lanes]
        probs = probs_ref[pair]
        d_probs = dot_last(upstream, stacked_heads(v_ref[:, lanes], first))
        parts = []
        for head in range(2):
            span = slice(head * length, (head + 1) * length)
            own, grad = probs[:, span], d_probs[:, span]
            parts.append(own * (grad - jnp.sum(own * grad, axis=1, keepdims=True)))
        d_scores = jnp.concatenate(parts, axis=1).astype(low)
        d_values = dot_first(upstream, probs.astype(low))
        d_values = jnp.where(upper, d_values[:, :length], d_values[:, length:])
        d_keys = dot_first(q_ref[:, lanes], d_scores) * score_scale
        d_keys = jnp.where(upper, d_keys[:, :length], d_keys[:, length:])
        d_queries = jnp.dot(
            d_scores, stacked_heads(k_ref[:, lanes], first), preferred_element_type=jnp.float32
        )
        d_queries = (d_queries * score_scale).astype(low)
        for which, value in enumerate(
            (d_queries.T, d_keys.astype(low), d_values.astype(low))
        ):
            for head in range(2):
                at = which * HEADS + 2 * pair + head
                late_ref[at // 3, at % 3 * HEAD_DIM : (at % 3 + 1) * HEAD_DIM] = value[
                    head * HEAD_DIM : (head + 1) * HEAD_DIM
                ]
        upside = jnp.dot(reverse, d_scores, preferred_element_type=jnp.float32)
        for head in range(2):
            own = upside[:, head * length : (head + 1) * length]
            own = jnp.concatenate([own, jnp.zeros_like(own)], axis=1)
            own = pltpu.roll(own, 0, 1, stride=1, stride_axis=0)
            at = 2 * pair + head
            sums[at % 4, at // 4 : at // 4 + 1] = jnp.sum(own, axis=0, keepdims=True)

    shift = lax.broadcasted_iota(jnp.int32, (2 * length, LANES), 0) - (length - 1)
    bucket = bucket_of(shift)
    lane_wide = lax.broadcasted_iota(jnp.int32, (2 * length, LANES), 1)
    bias_rows = 0.0
    for quarter in range(4):
        hot = jnp.where(bucket + quarter * BUCKETS == lane_wide, 1.0, 0.0)
        bias_rows = bias_rows + jnp.dot(
            sums[quarter],
            hot,
            precision=lax.Precision.HIGHEST,
            preferred_element_type=jnp.float32,
        )
    chunks = width // LANES
    tail[...] = jnp.zeros_like(tail)
    for chunk in range(chunks):
        lanes = slice(chunk * LANES, (chunk + 1) * LANES)
        tail[chunk : chunk + 1] = grad_ffn[:, lanes]
        for expert in range(experts):
            at = chunks + HEADS // 4 + expert * chunks + chunk
            tail[at : at + 1] = grad_router[expert : expert + 1, lanes]
    tail[chunks : chunks + HEADS // 4] = bias_rows[: HEADS // 4]
    block = 4 * width // group
    for at in range(group):
        own = tail[at * small_rows : (at + 1) * small_rows]
        high = own.astype(low).astype(jnp.float32)
        late_ref[at, block:] = jnp.concatenate([high, own - high], axis=0).astype(low)
    late_ref.send()


def backward_of(came, weight, gain_two, router, cotangent, saved, group):
    length, width = cotangent.shape
    experts = router.shape[0]
    low = jnp.bfloat16
    small_rows = -(-small_count(width, experts) // group)
    block = 4 * width // group
    outputs = (
        shaped((group, block + 2 * small_rows, length), low),
        shaped((length, width), jnp.float32),
        shaped((length, width), low),
    )
    scratch = (
        pltpu.VMEM((4, 8, 2 * length), jnp.float32),
        pltpu.VMEM((group * small_rows, LANES), jnp.float32),
    )
    q, k, v, probs, hidden, router_probs, choose, slot = saved
    inputs = (slot, hidden, router_probs, choose, cotangent, gain_two, router, weight)
    return staged(
        backward_kernel,
        "backward",
        (),
        (*inputs, v, probs, q, k),
        outputs,
        scratch,
        4 * length * width * width,
        10 * width * width,
        residents=(came,),
        mib=62,
    )


def first_norm_kernel(numbers, inputs, outputs, scratch):
    late_ref, hidden_grad_ref, query_ref, key_ref, value_ref, tokens_ref, gain_ref = inputs
    gain_out, grad_ref = outputs
    wait_all(*inputs)
    d_normed = 0.0
    each = late_ref.shape[0] // 4
    block = query_ref.shape[0] // each
    for which, weight in enumerate((query_ref, key_ref, value_ref)):
        turned = [late_ref[i, :block] for i in range(which * each, (which + 1) * each)]
        d_normed = d_normed + lax.dot_general(
            jnp.concatenate(turned, axis=0),
            weight[...],
            (((0,), (1,)), ((), ())),
            preferred_element_type=jnp.float32,
        )
    inputs = tokens_ref[...].astype(jnp.float32)
    d_first, grad_norm = norm_backward(
        inputs, rms_factor(inputs), row_of(gain_ref), d_normed
    )
    grad_ref[...] = (hidden_grad_ref[...] + d_first).astype(jnp.bfloat16)
    grad_ref.send()
    gain_out[...] = jnp.zeros(gain_out.shape, jnp.float32)
    for chunk in range(gain_ref.shape[0]):
        gain_out[chunk : chunk + 1] = grad_norm[:, chunk * LANES : (chunk + 1) * LANES]
    gain_out.send()


def first_norm_of(late, hidden_grad, weights, tokens, gain):
    length, width = tokens.shape
    low = jnp.bfloat16
    rows = -(-gain.shape[0] // 8) * 8
    return staged(
        first_norm_kernel,
        "first_norm",
        (),
        (late, hidden_grad, *weights, tokens, gain),
        (shaped((length, width), low),),
        (),
        6 * length * width * width,
        8 * width * width,
        kept=(shaped((rows, LANES), jnp.float32),),
        mib=56,
    )


def small_count(width, experts):
    return (1 + experts) * (width // LANES) + HEADS // 4


def pick_kernel(numbers, inputs, outputs, scratch):
    (which_ref,), (*pieces, tokens_ref) = numbers, inputs
    which = which_ref[0]
    pieces = [piece.ref() for piece in pieces]
    rows = pieces[0].shape[0]
    tokens_ref = tokens_ref.ref()
    if len(pieces) > 1:
        for part, piece in enumerate(pieces):
            outputs[0][part * rows : (part + 1) * rows] = piece[...]
        outputs[0].send()
    for out, turn in zip(outputs[-2:], (3, 1)):

        @pl.when(which == turn)
        def _():
            for part, piece in enumerate(pieces):
                out[part * rows : (part + 1) * rows] = piece[...]

        @pl.when(which != turn)
        def _():
            out[...] = tokens_ref[...]

        out.send()


def picked(which, pieces, tokens):
    outputs = (shaped(tokens.shape, tokens.dtype),) * (2 if len(pieces) == 1 else 3)
    return staged(
        pick_kernel,
        "picked",
        (which,),
        (*pieces, tokens),
        outputs,
        (),
        0,
        10 * tokens.size,
    )


def left_kernel(numbers, inputs, outputs, scratch):
    (which_ref,), (*pieces, gain_ref), (left_ref,) = numbers, inputs, outputs
    which = which_ref[0]
    scale = row_of(gain_ref)
    wait_all(*pieces)
    count = pieces[0].shape[0]
    spans = [
        (piece, at, slice(number * count + at, number * count + at + LANES))
        for number, piece in enumerate(pieces)
        for at in range(0, count, LANES)
    ]

    @pl.when(which < 3)
    def _():
        for piece, at, span in spans:
            own = piece[at : at + LANES].astype(jnp.float32)
            own = (own * rms_factor(own) * scale).astype(jnp.bfloat16)
            left_ref[:, span] = own.T

    @pl.when(which == 3)
    def _():
        for piece, at, span in spans:
            left_ref[:, span] = piece[at : at + LANES].T

    left_ref.send()


def left_of(which, pieces, gain):
    count, width = pieces[0].shape
    total = count * len(pieces)
    kept = (shaped((width, total), jnp.bfloat16),)
    inputs = (*pieces, gain)
    (left,) = staged(
        left_kernel,
        "left",
        (which,),
        inputs,
        (),
        (),
        10 * total * width,
        6 * total * width,
        kept=kept,
        mib=44,
    )
    return left


gelu_scale = 0.7978845608028654
gelu_cubic = 0.044715


def hidden_pass(rows, slots, part_in, part_out):
    inner = jnp.dot(rows, part_in[...], preferred_element_type=jnp.float32)
    upstream = dot_last(slots, part_out[...])
    square = inner * inner
    bent = jnp.tanh(gelu_scale * (inner + gelu_cubic * (square * inner)))
    active = (inner * (0.5 * (1.0 + bent))).astype(jnp.bfloat16)
    slope = 0.5 * (1.0 + bent) + 0.5 * inner * (1.0 - bent * bent) * (
        gelu_scale * (1.0 + 3.0 * gelu_cubic * square)
    )
    return active, (upstream * slope).astype(jnp.bfloat16)


def expert_pass(rows, slots, weights):
    result, d_rows = 0.0, 0.0
    for part_in, part_out in weights:
        active, d_inner = hidden_pass(rows, slots, part_in, part_out)
        result = result + jnp.dot(active, part_out[...], preferred_element_type=jnp.float32)
        d_rows = d_rows + dot_last(d_inner, part_in[...])
    return result, d_rows


def four_of_eight(shape):
    return lax.broadcasted_iota(jnp.int32, shape, 0) & 7 < 4


def sorted_rows(blocks_ref):
    number, height, width = blocks_ref.shape
    main = height // 2 - 4
    mixed = blocks_ref[:, 2 * main :].astype(jnp.float32).reshape(number * 8, width)
    ahead = four_of_eight(mixed.shape)
    second = pltpu.roll(mixed, number * 8 - 4, 0)
    zero = jnp.zeros_like(mixed)
    sorted_kinds = []
    for whole, rest in (
        (blocks_ref[:, :main], mixed),
        (blocks_ref[:, main : 2 * main], second),
    ):
        rest = jnp.where(ahead, rest, zero).astype(jnp.bfloat16)
        sorted_kinds.append(jnp.concatenate([whole.reshape(number * main, width), rest], axis=0))
    return sorted_kinds


def expert_kernel(numbers, inputs, outputs, scratch):
    blocks_ref, in_a, out_a, in_b, out_b = inputs
    (back_ref,) = outputs
    low = jnp.bfloat16
    blocks, height, width = blocks_ref.shape
    main = height // 2 - 4
    count = blocks * main
    rows, slots = sorted_rows(blocks_ref)
    result, d_rows = 0.0, 0.0
    for part_in, part_out in ((in_a, out_a), (in_b, out_b)):
        wait_all(part_in, part_out)
        part_result, part_rows = expert_pass(rows, slots, ((part_in, part_out),))
        result, d_rows = result + part_result, d_rows + part_rows
    back_ref[:, :main] = result[:count].reshape(blocks, main, width).astype(low)
    back_ref[:, main : 2 * main] = d_rows[:count].reshape(blocks, main, width).astype(low)
    mixed = result[count:]
    mixed = jnp.where(four_of_eight(mixed.shape), mixed, pltpu.roll(d_rows[count:], 4, 0))
    back_ref[:, 2 * main :] = mixed.reshape(blocks, 8, width).astype(low)
    back_ref.send()


def sorting(number, height):
    half, capacity = number * height // 2, height // 2
    place = np.arange(2 * half)
    sort = place % half // capacity * height + place // half * capacity + place % capacity
    unsort = np.empty_like(sort)
    unsort[sort] = place
    return jnp.asarray(np.stack([sort, unsort], axis=1), jnp.int32)


def rows_by_product(rows_ref, order_ref):
    count = rows_ref.shape[0]
    lanes = lax.broadcasted_iota(jnp.int32, (count, count), 1)
    sort = jnp.where(order_ref[:, 0:1] == lanes, 1.0, 0.0).astype(jnp.bfloat16)
    ordered = jnp.dot(sort, rows_ref[...], preferred_element_type=jnp.float32)
    ordered = ordered.astype(jnp.bfloat16)
    return ordered[: count // 2], ordered[count // 2 :]


def expert_sorting_kernel(numbers, inputs, outputs, scratch):
    rows_ref, order_ref, in_a, out_a, in_b, out_b = inputs
    (back_ref,) = outputs
    count = rows_ref.shape[0]
    rows, slots = rows_by_product(rows_ref, order_ref)
    result, d_rows = expert_pass(rows, slots, ((in_a, out_a), (in_b, out_b)))
    lanes = lax.broadcasted_iota(jnp.int32, (count, count), 1)
    unsort = jnp.where(order_ref[:, 1:2] == lanes, 1.0, 0.0).astype(jnp.bfloat16)
    both = jnp.concatenate([result.astype(jnp.bfloat16), d_rows.astype(jnp.bfloat16)], axis=0)
    back_ref[...] = jnp.dot(unsort, both, preferred_element_type=jnp.float32).astype(jnp.bfloat16)
    back_ref.send()


def expert_rows_of(blocks, part_weights):
    number, height, width = blocks.shape
    hidden_width = part_weights[0].shape[1]
    flops, moved = 8 * number * height * width * hidden_width, 12 * width * width
    if mixed_tiles(height // 2):
        (back,) = staged(
            expert_kernel,
            "expert_rows",
            (),
            part_weights,
            (shaped(blocks.shape, blocks.dtype),),
            (),
            flops,
            moved,
            residents=(blocks,),
            mib=62,
        )
        return back
    (back,) = staged(
        expert_sorting_kernel,
        "expert_rows",
        (),
        (blocks.reshape(-1, width), sorting(number, height), *part_weights),
        (shaped((number * height, width), blocks.dtype),),
        (),
        flops,
        moved,
    )
    return back.reshape(blocks.shape)


def grads_kernel(mixed, numbers, inputs, outputs, scratch):
    wait_all(*inputs)
    if mixed:
        blocks_ref, part_in, part_out, *got = inputs
        rows, slots = sorted_rows(blocks_ref)
    else:
        rows_ref, order_ref, part_in, part_out, *got = inputs
        rows, slots = rows_by_product(rows_ref, order_ref)
    active, d_inner = hidden_pass(rows, slots, part_in, part_out)
    for number, (left, right) in enumerate(((rows, d_inner), (active, slots))):
        grad = dot_first(left, right)
        if got:
            outputs[number][...] = grad + got[number][...].astype(jnp.float32)
        else:
            outputs[number][...] = grad.astype(jnp.bfloat16)
        outputs[number].send()


def expert_grads_of(blocks, part_in, part_out, *got):
    number, height, width = blocks.shape
    hidden_width = part_in.shape[1]
    mixed = mixed_tiles(height // 2)
    kind = jnp.float32 if got else jnp.bfloat16
    outputs = (shaped((width, hidden_width), kind), shaped((hidden_width, width), kind))
    rows = (blocks,) if mixed else (blocks.reshape(-1, width), sorting(number, height))
    return staged(
        functools.partial(grads_kernel, mixed),
        "own_grads" if got else "sent_grads",
        (),
        (*rows, part_in, part_out, *got),
        outputs,
        (),
        0 if got else 4 * number * height * width * hidden_width,
        0 if got else 8 * width * width,
    )


def in_parts(values):
    high = values.astype(jnp.bfloat16).astype(jnp.float32)
    return jnp.concatenate([high, values - high], axis=0).astype(jnp.bfloat16)


def from_parts(parts):
    parts = parts.astype(jnp.float32)
    rows = parts.shape[0] // 2
    return parts[:rows] + parts[rows:]


def block_kernel(numbers, inputs, outputs, scratch):
    (bits_ref,), (late_ref, left_ref, gain_ref), (block_ref,) = numbers, inputs, outputs
    group = late_ref.shape[0]
    part = left_ref.shape[0] // 2
    block = left_ref.shape[0] * 4 // group
    edge = block - LANES
    half = part // 2
    gain_edge = block_ref.shape[1] - 2 * gain_ref.shape[0]
    odd = bits_ref[3] == 1
    here = bits_ref[0] * 8 + bits_ref[1] * 4 + bits_ref[2] * 2 + bits_ref[3]
    right = jnp.concatenate(
        [late_ref[here ^ factor_order(i), :block] for i in range(group)], axis=1
    )
    right = jnp.where(odd, jnp.concatenate([right[edge:], right[:edge]], axis=0), right)
    total = dot_last(left_ref[...], right)
    first = pair_masks(half)
    small = in_parts(from_parts(jnp.sum(late_ref[:, block:].astype(jnp.float32), axis=0)))
    gain = in_parts(gain_ref[...])
    for side in range(2):
        own = total[side * part : (side + 1) * part]
        block_ref[side, :part] = own[:, :LANES].astype(jnp.bfloat16)
        rest = own[:, LANES:]
        rest = jnp.concatenate([rest, rest], axis=1)
        upper, lower = rest[:half], rest[half:]
        even = jnp.where(first, upper, lower)
        packed = jnp.where(odd, jnp.where(first, lower, upper), even)
        block_ref[side, part : part + half] = packed.astype(jnp.bfloat16)
        block_ref[side, part + half : gain_edge] = small
        block_ref[side, gain_edge:] = gain


def block_of(bits, late, left, gain, small_rows):
    group, rows, length = late.shape
    width = left.shape[0]
    height = 3 * width // 4 + 2 * (small_rows + gain.shape[0])
    (block,) = staged(
        block_kernel,
        "grad_block",
        (bits,),
        (),
        (),
        (),
        8 * width * width * length,
        2 * left.size,
        residents=(late, left, gain),
        kept=(shaped((2, height, LANES), jnp.bfloat16),),
        mib=24,
    )
    return block


def share_kernel(edge, small_rows, numbers, inputs, outputs, scratch):
    (own_ref, got_ref), (share_ref,) = inputs, outputs
    gain_edge = edge + 2 * small_rows
    for side in range(2):
        own = own_ref[side, :edge].astype(jnp.float32) + got_ref[side, :edge].astype(jnp.float32)
        share_ref[side, :edge] = own.astype(jnp.bfloat16)
        for rows in (slice(edge, gain_edge), slice(gain_edge, None)):
            share_ref[side, rows] = in_parts(
                from_parts(own_ref[side, rows]) + from_parts(got_ref[side, rows])
            )


def share_of(own, got, edge, small_rows):
    (share,) = staged(
        functools.partial(share_kernel, edge, small_rows),
        "share",
        (),
        (),
        (),
        (),
        own.size,
        6 * own.size,
        residents=(own, got),
        kept=(shaped(own.shape, own.dtype),),
        mib=8,
    )
    return share


def assemble_kernel(weights, small_rows, bits_ref, sources, outs, made, out_sems, put_small):
    em, ey, dx, dc = [bits_ref[i] for i in range(4)]
    part = made.shape[1] // 2
    half = part // 2
    edge = part + half
    first = pair_masks(half)
    def copy_of(number, side, target):
        rows = pl.ds(side * part, part)
        return pltpu.make_async_copy(
            made.at[number, rows], target.at[rows], out_sems.at[2 * number + side]
        )

    for number, weight in enumerate(weights):
        truth = (em ^ (weight // 2)) * 2 + (ey ^ (weight % 2))
        for side in range(2):
            for here in range(4):

                @pl.when(dx * 2 + dc == here)
                def _():
                    own = [
                        sources[4 * number + 2 * ((i ^ here) & 1) + ((i ^ here) >> 1)]
                        for i in range(4)
                    ]
                    rows = slice(side * part, (side + 1) * part)
                    upper = slice(side * part, side * part + half)
                    lower = slice(side * part + half, (side + 1) * part)
                    for twin in range(2):
                        even, odd = own[2 * twin], own[2 * twin + 1]
                        at = 3 * twin * LANES
                        made[number, rows, at : at + LANES] = even[side, :part].astype(jnp.float32)
                        made[number, rows, at + 2 * LANES : at + 3 * LANES] = odd[
                            side, :part
                        ].astype(jnp.float32)
                        left = even[side, part:edge].astype(jnp.float32)
                        right = odd[side, part:edge].astype(jnp.float32)
                        middle = slice(at + LANES, at + 2 * LANES)
                        made[number, upper, middle] = jnp.where(first, left, right)
                        made[number, lower, middle] = pltpu.roll(
                            jnp.where(first, right, left), HEAD_DIM, 1
                        )
                    for i in range(4 if side == 0 else 0):
                        tail = own[i][0, edge:].astype(jnp.float32)
                        gain = tail[2 * small_rows :]
                        gain_rows = gain.shape[0] // 2
                        put_small(
                            number,
                            i,
                            jnp.concatenate(
                                [
                                    tail[:small_rows] + tail[small_rows : 2 * small_rows],
                                    gain[:gain_rows] + gain[gain_rows:],
                                ],
                                axis=0,
                            ),
                        )

            for i in range(4):

                @pl.when(truth == i)
                def _():
                    copy_of(number, side, outs[i]).start()

    for number, weight in enumerate(weights):
        truth = (em ^ (weight // 2)) * 2 + (ey ^ (weight % 2))
        for i in range(4):

            @pl.when(truth == i)
            def _():
                for side in range(2):
                    copy_of(number, side, outs[i]).wait()


def first_half_kernel(small_rows, bits_ref, *refs):
    sources, outs, small_out, made, out_sems = refs[:8], refs[8:12], refs[12], refs[13], refs[14]

    def put_small(number, i, rows):
        small_out[number, i] = rows

    assemble_kernel((0, 2), small_rows, bits_ref, sources, outs, made, out_sems, put_small)


def second_half_kernel(small_rows, bits_ref, *refs):
    sources, small_ref, outs = refs[:8], refs[8], refs[13:17]
    norm_out, ffn_out, bias_out, router_out = refs[17:21]
    made, tail, out_sems = refs[21:]
    em, ey = bits_ref[0], bits_ref[1]
    for number in range(2):
        tail[(em ^ number) * 2 + ey] = small_ref[number]

    def put_small(number, i, rows):
        tail[(em ^ number) * 2 + (ey ^ 1), i] = rows

    assemble_kernel((1, 3), small_rows, bits_ref, sources, outs, made, out_sems, put_small)

    def small_row(at):
        at, row = divmod(at, small_rows)
        return tail[at // 4, at % 4, row : row + 1]

    chunks = made.shape[2] // LANES
    total = 0.0
    for at in range(16):
        total = total + tail[at // 4, at % 4, small_rows:]
    norm_out[...] = total[:chunks]
    for chunk in range(chunks):
        lanes = slice(chunk * LANES, (chunk + 1) * LANES)
        ffn_out[chunk : chunk + 1] = small_row(chunk)
        for expert in range(router_out.shape[0]):
            router_out[expert : expert + 1, lanes] = small_row(
                chunks + HEADS // 4 + expert * chunks + chunk
            )
    for head in range(HEADS):
        at = head % 4 * BUCKETS
        bias_out[head : head + 1] = small_row(chunks + head // 4)[:, at : at + BUCKETS]


def first_half(bits, sources, small_rows, width):
    gain_rows = (sources[0].shape[1] - 3 * width // 4 - 2 * small_rows) // 2
    *grads, small = pl.pallas_call(
        functools.partial(first_half_kernel, small_rows),
        out_shape=(shaped((width, width), jnp.float32),) * 4
        + (shaped((2, 4, small_rows + gain_rows, LANES), jnp.float32),),
        in_specs=[pl.BlockSpec(memory_space=pltpu.SMEM)] + [whole_spec()] * 8,
        out_specs=(any_spec(),) * 4 + (whole_spec(),),
        scratch_shapes=[
            pltpu.VMEM((2, width, width), jnp.float32),
            pltpu.SemaphoreType.DMA((4,)),
        ],
        compiler_params=params(16),
        cost_estimate=cost(8 * width * width, 12 * width * width),
        name="first_half",
    )(bits, *sources)
    return grads, small


def second_half(bits, sources, small, grads, small_rows, width, experts):
    return pl.pallas_call(
        functools.partial(second_half_kernel, small_rows),
        out_shape=(shaped((width, width), jnp.float32),) * 4
        + (
            shaped((width // LANES, LANES), jnp.float32),
            shaped((width // LANES, LANES), jnp.float32),
            shaped((HEADS, BUCKETS), jnp.float32),
            shaped((experts, width), jnp.float32),
        ),
        in_specs=[pl.BlockSpec(memory_space=pltpu.SMEM)]
        + [whole_spec()] * 9
        + [any_spec()] * 4,
        out_specs=(any_spec(),) * 4 + (whole_spec(),) * 4,
        input_output_aliases={10 + i: i for i in range(4)},
        scratch_shapes=[
            pltpu.VMEM((2, width, width), jnp.float32),
            pltpu.VMEM((4, 4) + small.shape[2:], jnp.float32),
            pltpu.SemaphoreType.DMA((4,)),
        ],
        compiler_params=params(16),
        cost_estimate=cost(8 * width * width, 12 * width * width),
        name="second_half",
    )(bits, *sources, small, *grads)


def place_in_group():
    place = [lax.axis_index(axis) for axis in ("em", "ey", "dx", "dc")]
    return (2 * place[0] + place[1]).astype(jnp.int32), jnp.stack(place).astype(jnp.int32)


def factor_order(at):
    return (at & 1) * 2 + (at >> 1 & 1) * 4 + (at >> 2 & 1) * 8 + (at >> 3)


def with_other(rows, axis):
    return jnp.concatenate([rows, swap(rows, axis)], axis=0)


def gathered_grads(late, left, gain_rows, place, small_rows, experts, beside):
    width = left.shape[0]
    block = block_of(place, late, left, gain_rows, small_rows)
    block, beside = lax.optimization_barrier((block, beside))
    beside = expert_grads_of(*beside)
    got, beside = lax.optimization_barrier((swap(block, "eh"), beside))
    near = share_of(block, got, 3 * width // 4, small_rows)
    far, near_x, near_y = swap(near, "em"), swap(near, "dx"), swap(near, "ey")
    far_x, far_y = swap(far, "dx"), swap(far, "ey")
    near_both, far_both = swap(near_x, "ey"), swap(far_y, "dx")

    def both_cores(*sources):
        return sources + tuple(swap(source, "dc") for source in sources)

    sources = both_cores(near, near_x) + both_cores(far, far_x)
    grads, small = first_half(place, sources, small_rows, width)
    sources = both_cores(near_y, near_both) + both_cores(far_y, far_both)
    grads = second_half(place, sources, small, grads, small_rows, width, experts)
    return grads, beside


def gathered_grads_plain(late, left, gain_rows, place, small_rows, experts, beside):
    group, rows, length = late.shape
    width = left.shape[0]
    block = 4 * width // group
    small = jnp.sum(late[:, block:].astype(jnp.float32), axis=0)
    small = lax.psum(small[:small_rows] + small[small_rows:], "eh")
    order = jnp.asarray([factor_order(at) for at in range(group)], jnp.int32)
    order = order ^ lax.axis_index(GROUP_AXES)
    late_block = jnp.take(late[:, :block], order, axis=0)
    late_block = late_block.transpose(1, 0, 2).reshape(block, group * length)
    grad_block = dot_last(late_block, left)
    mine = lax.psum_scatter(grad_block, "eh", scatter_dimension=0, tiled=True)
    grads = lax.all_gather(mine.astype(jnp.bfloat16), "eh", axis=0, tiled=True)
    grads = lax.all_gather(grads, GROUP_AXES, axis=0, tiled=True)
    small = lax.all_gather(small, GROUP_AXES, axis=0, tiled=True).reshape(-1)
    grads = grads.reshape(4, width, width).transpose(0, 2, 1).astype(jnp.float32)
    sizes = (width, HEADS * BUCKETS, experts * width)
    ends = np.cumsum(sizes)
    pieces = [small[end - size : end] for end, size in zip(ends, sizes)]
    pieces[1], pieces[2] = pieces[1].reshape(HEADS, BUCKETS), pieces[2].reshape(experts, width)
    grad_norm = lax.psum(gain_rows, TOKEN_AXES)[: width // LANES]
    return (*grads, grad_norm, *pieces), expert_grads_of(*beside)


def per_device(
    tokens,
    norm_gain,
    w_query,
    w_key,
    w_value,
    w_output,
    rel_bias,
    ffn_gain,
    w_router,
    w_in,
    w_out,
    routes,
    lengths,
    cotangent,
):
    length, model_width = tokens.shape
    experts = w_router.shape[1]
    group = lax.axis_size(GROUP_AXES)
    capacity = max(2, (5 * length + 4 * experts - 1) // (4 * experts))
    small_rows = -(-small_count(model_width, experts) // group)
    gain_one, gain_two = norm_gain.reshape(-1, LANES), ffn_gain.reshape(-1, LANES)
    weights = (w_query, w_key, w_value, w_output)
    router = w_router.T

    w_in_own, w_out_own = w_in[0], w_out[0]
    w_in_other, w_out_other = swap(w_in_own, "dc"), swap(w_out_own, "dc")
    outgoing, attended, *saved = forward_of(
        lengths,
        tokens,
        gain_one,
        weights,
        rel_bias.T,
        gain_two,
        router,
        routes.reshape(1, length),
        cotangent,
        capacity,
    )
    which, place = place_in_group()
    outgoing, near_tokens = lax.optimization_barrier((outgoing, with_other(tokens, "dx")))
    outgoing = outgoing.reshape(2 * experts, 2 * capacity, model_width)
    incoming = lax.all_to_all(outgoing, EXPERT_AXES, split_axis=0, concat_axis=0, tiled=True)
    far_tokens = swap(near_tokens, "ey")
    near_attended, own_near, given_near = picked(
        which[None], (attended, swap(attended, "dx")), near_tokens
    )
    far_attended, got_near = swap(near_attended, "ey"), swap(given_near, "em")
    incoming, far_tokens, _ = lax.optimization_barrier((incoming, far_tokens, given_near))
    sent_back = expert_rows_of(incoming, (w_in_own, w_out_own, w_in_other, w_out_other))
    sent_back, far_attended, got_near = lax.optimization_barrier(
        (sent_back, far_attended, got_near)
    )
    came_back = lax.all_to_all(sent_back, EXPERT_AXES, split_axis=0, concat_axis=0, tiled=True)
    own_far, given_far = picked(which[None], (far_attended,), far_tokens)
    incoming, _ = lax.optimization_barrier((incoming, sent_back))
    in_other, out_other = expert_grads_of(incoming, w_in_other, w_out_other)
    factors = [own_near, own_far, got_near]
    factors = factors + [swap(rows, "dc") for rows in factors]
    came_back, factors, given_far, in_other, out_other = lax.optimization_barrier(
        (came_back, factors, given_far, in_other, out_other)
    )
    got_far = swap(given_far, "em")
    beside = (incoming, w_in_own, w_out_own, swap(in_other, "dc"), swap(out_other, "dc"))

    late, hidden_grad, output = backward_of(
        came_back.reshape(experts, 2, 2 * capacity, model_width),
        w_output,
        gain_two,
        router,
        cotangent,
        saved,
        group,
    )
    late, got_far = lax.optimization_barrier((late, got_far))
    own_late = late
    factors = factors[:3] + [got_far] + factors[3:] + [swap(got_far, "dc")]
    late = lax.all_to_all(late, GROUP_AXES, split_axis=0, concat_axis=0, tiled=True)
    left = left_of(which[None], factors, gain_one)
    gain_rows, grad_input = first_norm_of(own_late, hidden_grad, weights[:3], tokens, gain_one)
    late, left, gain_rows, beside = lax.optimization_barrier((late, left, gain_rows, beside))
    gather = gathered_grads if lax.axis_size("eh") == 2 else gathered_grads_plain
    grads, (grad_in, grad_out) = gather(
        late, left, gain_rows, place, small_rows, experts, beside
    )
    *grads, grad_norm, grad_ffn, grad_bias, grad_router = grads
    return (
        output,
        grad_input,
        grad_norm.reshape(model_width),
        *grads,
        grad_bias.T,
        grad_ffn.reshape(model_width),
        grad_router.T,
        grad_in[None],
        grad_out[None],
    )


def solution(mesh):
    exp_count, dp_count = mesh.shape["exp"], mesh.shape["dp"]
    fine = Mesh(
        mesh.devices.reshape(exp_count // 4, 2, 2, dp_count // 2, 2),
        TOKEN_AXES,
    )
    exp, dp = ("eh", "em", "ey"), ("dx", "dc")
    in_specs = (
        P(TOKEN_AXES, None),
        P(),
        P(),
        P(),
        P(),
        P(),
        P(),
        P(),
        P(),
        P(exp, None, dp),
        P(exp, dp, None),
        P(TOKEN_AXES, None),
        P(TOKEN_AXES),
        P(TOKEN_AXES, None),
    )
    out_specs = (
        P(TOKEN_AXES, None),
        P(TOKEN_AXES, None),
        P(),
        P(),
        P(),
        P(),
        P(),
        P(),
        P(),
        P(),
        P(exp, None, dp),
        P(exp, dp, None),
    )
    return jax.shard_map(
        per_device, mesh=fine, in_specs=in_specs, out_specs=out_specs, check_vma=False
    )
```

```python
import functools

import jax
import jax.numpy as jnp
import numpy as np
from jax import lax
from jax.experimental import pallas as pl
from jax.experimental.pallas import tpu as pltpu
from jax.sharding import Mesh
from jax.sharding import PartitionSpec as P

HEADS = 12
HEAD_DIM = 64
BUCKETS = 32
LANES = 128
VMEM_MIB = 63

norm_eps = 1e-06
score_scale = 0.125
masked_score = -1e30
far_limits = (11, 16, 22, 32, 45, 64, 90)

EXPERT_AXES = ("eh", "em", "ey", "dx")
GROUP_AXES = ("em", "ey", "dx", "dc")
TOKEN_AXES = ("eh", "em", "ey", "dx", "dc")


def bucket_of(offset):
    distance = jnp.abs(offset)
    far_bucket = jnp.full(distance.shape, 8, jnp.int32)
    for limit_value in far_limits:
        far_bucket = far_bucket + (distance >= limit_value).astype(jnp.int32)
    near_bucket = jnp.where(distance < 8, distance, far_bucket)
    return near_bucket + 16 * (offset > 0).astype(jnp.int32)


def dot_last(left_side, right_side):
    return lax.dot_general(
        left_side, right_side, (((1,), (1,)), ((), ())), preferred_element_type=jnp.float32
    )


def dot_first(left_side, right_side):
    return lax.dot_general(
        left_side, right_side, (((0,), (0,)), ((), ())), preferred_element_type=jnp.float32
    )


def norm_backward(values, factor, gain, grad_normed):
    scaled = gain * grad_normed
    grad_gain = jnp.sum(grad_normed * values * factor, axis=0, keepdims=True)
    grad_values = factor * scaled - values * factor * factor * factor * jnp.mean(
        scaled * values, axis=-1, keepdims=True
    )
    return (grad_values, grad_gain)


def swap(array, axis):
    return lax.ppermute(array, axis, perm=[(0, 1), (1, 0)])


def whole_spec():
    return pl.BlockSpec(memory_space=pltpu.VMEM)


def any_spec():
    return pl.BlockSpec(memory_space=pl.ANY)


def params(mib):
    return pltpu.CompilerParams(vmem_limit_bytes=mib * 1024 * 1024)


def cost(flops, moved):
    return pl.CostEstimate(flops=flops, bytes_accessed=moved, transcendentals=0)


def shaped(dims, kind):
    return jax.ShapeDtypeStruct(dims, kind)


class Arriving:
    def __init__(self, source, held, sem):
        self.held, self.pending = held, pltpu.make_async_copy(source, held, sem)
        self.pending.start()

    def ref(self):
        if self.pending is not None:
            self.pending.wait()
            self.pending = None
        return self.held

    def __getitem__(self, index):
        return self.ref()[index]

    @property
    def shape(self):
        return self.held.shape


def wait_all(*operands):
    for operand in operands:
        operand.ref()


class Leaving:
    def __init__(self, held, target, sem):
        self.held, self.copy = held, pltpu.make_async_copy(held, target, sem)

    def __setitem__(self, index, value):
        self.held[index] = value

    def __getitem__(self, index):
        return self.held[index]

    @property
    def shape(self):
        return self.held.shape

    def send(self):
        self.copy.start()

    def finish(self):
        self.copy.wait()


class Staying:
    def __init__(self, held):
        self.held = held

    def __setitem__(self, index, value):
        self.held[index] = value

    def __getitem__(self, index):
        return self.held[index]

    @property
    def shape(self):
        return self.held.shape

    def send(self):
        pass


def slot_rows(slot, capacity):
    if not mixed_tiles(capacity):
        return slot, slot + capacity
    main = capacity - 4
    tail = slot >= main
    return jnp.where(tail, slot + main, slot), jnp.where(tail, slot + main + 4, slot + main)


def mixed_tiles(capacity):
    return capacity > 4 and (capacity - 4) % 16 == 0


def staged(
    kernel,
    name,
    scalars,
    inputs,
    outputs,
    scratch,
    flops,
    moved,
    residents=(),
    kept=(),
    mib=VMEM_MIB,
):
    counts = (len(scalars), len(residents), len(inputs), len(kept), len(outputs))

    def body(*refs):
        refs = list(refs)
        take = lambda count: [refs.pop(0) for _ in range(count)]
        numbers, there, sources, staying, targets = [take(count) for count in counts]
        held_in, held_out = take(counts[2]), take(counts[4])
        sems = refs.pop(0)
        arriving = [
            Arriving(source, held, sems.at[i])
            for i, (source, held) in enumerate(zip(sources, held_in))
        ]
        leaving = [
            Leaving(held, target, sems.at[counts[2] + i])
            for i, (held, target) in enumerate(zip(held_out, targets))
        ]
        kernel(numbers, there + arriving, [Staying(ref) for ref in staying] + leaving, refs)
        for copy in leaving:
            copy.finish()

    return pl.pallas_call(
        body,
        out_shape=tuple(kept) + tuple(outputs),
        in_specs=[pl.BlockSpec(memory_space=pltpu.SMEM)] * counts[0]
        + [whole_spec()] * counts[1]
        + [any_spec()] * counts[2],
        out_specs=(whole_spec(),) * counts[3] + (any_spec(),) * counts[4],
        scratch_shapes=[pltpu.VMEM(x.shape, x.dtype) for x in inputs]
        + [pltpu.VMEM(x.shape, x.dtype) for x in outputs]
        + [pltpu.SemaphoreType.DMA((max(1, counts[2] + counts[4]),))]
        + list(scratch),
        compiler_params=params(mib),
        cost_estimate=cost(flops, moved),
        name=name,
    )(*scalars, *residents, *inputs)


def row_of(ref):
    return jnp.concatenate([ref[i : i + 1] for i in range(ref.shape[0])], axis=1)


def rms_factor(values):
    return lax.rsqrt(jnp.mean(values * values, axis=-1, keepdims=True) + norm_eps)


def pair_masks(rows):
    first = lax.broadcasted_iota(jnp.int32, (rows, LANES), 1) < HEAD_DIM
    return first


def stacked_heads(pair, first):
    zero = jnp.zeros_like(pair)
    return jnp.concatenate([jnp.where(first, pair, zero), jnp.where(first, zero, pair)], axis=0)


def offset_buckets(rows, length):
    lane = lax.broadcasted_iota(jnp.int32, (rows, 2 * length), 1)
    return bucket_of(jnp.where(lane < length, lane, lane - 2 * length))


def forward_kernel(numbers, inputs, outputs, scratch):
    (count_ref,) = numbers
    (
        tokens_ref,
        gain_ref,
        query_ref,
        key_ref,
        value_ref,
        bias_ref,
        routes_ref,
        output_ref,
        gain_two_ref,
        router_ref,
        cotangent_ref,
    ) = inputs
    (
        outgoing_ref,
        attended_ref,
        q_ref,
        k_ref,
        v_ref,
        probs_ref,
        hidden_ref,
        router_probs_ref,
        choose_ref,
        slot_ref,
    ) = outputs
    early, later = inputs[:7], inputs[7:]
    wait_all(*early)
    low = jnp.bfloat16
    length, width = tokens_ref.shape
    experts = router_ref.shape[0]
    capacity = outgoing_ref.shape[2] // 2
    inputs = tokens_ref[...].astype(jnp.float32)
    normed = (inputs * rms_factor(inputs) * row_of(gain_ref)).astype(low)
    for weight, out in ((query_ref, q_ref), (key_ref, k_ref), (value_ref, v_ref)):
        out[...] = jnp.dot(normed, weight[...], preferred_element_type=jnp.float32).astype(low)
        out.send()

    buckets = offset_buckets(BUCKETS, length)
    hot = buckets == lax.broadcasted_iota(jnp.int32, buckets.shape, 0)
    table = jnp.dot(
        bias_ref[...],
        jnp.where(hot, 1.0, 0.0),
        precision=lax.Precision.HIGHEST,
        preferred_element_type=jnp.float32,
    )
    live = lax.broadcasted_iota(jnp.int32, (length, length), 1) < count_ref[0]
    first = pair_masks(length)
    for pair in range(HEADS // 2):
        lanes = slice(pair * LANES, (pair + 1) * LANES)
        scores = dot_last(q_ref[:, lanes], stacked_heads(k_ref[:, lanes], first)) * score_scale
        weights = []
        for head in range(2):
            row = table[2 * pair + head : 2 * pair + head + 1]
            field = pltpu.roll(
                jnp.broadcast_to(row, (length, 2 * length)), 0, 1, stride=1, stride_axis=0
            )
            own = scores[:, head * length : (head + 1) * length] + field[:, :length]
            own = jnp.where(live, own, masked_score)
            own = jnp.exp(own - jnp.max(own, axis=1, keepdims=True))
            own = own / jnp.sum(own, axis=1, keepdims=True)
            probs_ref[pair, :, head * length : (head + 1) * length] = own
            weights.append(own.astype(low))
        both = jnp.concatenate(weights, axis=1)
        attended_ref[:, lanes] = jnp.dot(
            both, stacked_heads(v_ref[:, lanes], first), preferred_element_type=jnp.float32
        ).astype(low)

    attended_ref.send()
    probs_ref.send()
    wait_all(*later)
    hidden = inputs + jnp.dot(
        attended_ref[...], output_ref[...], preferred_element_type=jnp.float32
    )
    hidden_ref[...] = hidden
    hidden_ref.send()
    normed_two = (hidden * rms_factor(hidden) * row_of(gain_two_ref)).astype(low)
    logits = dot_last(normed_two, router_ref[...])
    router_probs = jnp.exp(logits - jnp.max(logits, axis=1, keepdims=True))
    router_probs = router_probs / jnp.sum(router_probs, axis=1, keepdims=True)
    router_probs_ref[...] = router_probs
    router_probs_ref.send()

    lane = lax.broadcasted_iota(jnp.int32, (length, length), 1)
    place = lax.broadcasted_iota(jnp.int32, (length, length), 0)
    routes = routes_ref[...]
    chosen = routes == lax.broadcasted_iota(jnp.int32, (experts, length), 0)
    chosen = jnp.where(chosen, 1.0, 0.0)
    alive = lax.broadcasted_iota(jnp.int32, (1, length), 1) < count_ref[0]
    before = jnp.where(place <= lane, 1.0, 0.0).astype(low)
    running = jnp.dot(
        (chosen * jnp.where(alive, 1.0, 0.0)).astype(low),
        before,
        preferred_element_type=jnp.float32,
    )
    slot = jnp.sum(running * chosen, axis=0, keepdims=True).astype(jnp.int32) - 1
    kept = alive & (slot < capacity)
    columns = [
        jnp.where(kept, routes * (2 * capacity) + row, -1) for row in slot_rows(slot, capacity)
    ]
    slot_ref[...] = jnp.concatenate(columns, axis=0)
    slot_ref.send()
    unit = jnp.where(place == lane, 1.0, 0.0).astype(low)
    choose = dot_last(unit, chosen.astype(low))
    choose_ref[...] = choose
    choose_ref.send()
    gate = jnp.sum(router_probs * choose, axis=1, keepdims=True)
    scaled = (gate * cotangent_ref[...].astype(jnp.float32)).astype(low)
    row = lax.broadcasted_iota(jnp.int32, (experts * 2 * capacity, length), 0)
    spread = jnp.concatenate(
        [
            jnp.where(row == columns[0], 1.0, 0.0).astype(low),
            jnp.where(row == columns[1], 1.0, 0.0).astype(low),
        ],
        axis=1,
    )
    packed = jnp.dot(
        spread,
        jnp.concatenate([normed_two, scaled], axis=0),
        preferred_element_type=jnp.float32,
    )
    for expert in range(experts):
        rows = packed[expert * 2 * capacity : (expert + 1) * 2 * capacity].astype(low)
        outgoing_ref[expert, 0] = rows
        outgoing_ref[expert, 1] = rows
    outgoing_ref.send()


def forward_of(count, tokens, gain, weights, bias, gain_two, router, routes, cotangent, capacity):
    length, width = tokens.shape
    experts = router.shape[0]
    low = jnp.bfloat16
    outputs = (
        shaped((experts, 2, 2 * capacity, width), low),
        shaped((length, width), low),
        shaped((length, width), low),
        shaped((length, width), low),
        shaped((length, width), low),
        shaped((HEADS // 2, length, 2 * length), jnp.float32),
        shaped((length, width), jnp.float32),
        shaped((length, experts), jnp.float32),
        shaped((length, experts), jnp.float32),
        shaped((2, length), jnp.int32),
    )
    query, key, value, output = weights
    inputs = (tokens, gain, query, key, value, bias, routes, output, gain_two, router, cotangent)
    return staged(
        forward_kernel,
        "forward",
        (count,),
        inputs,
        outputs,
        (),
        10 * length * width * width,
        10 * width * width,
    )


def backward_kernel(numbers, inputs, outputs, scratch):
    (
        came_ref,
        slot_ref,
        hidden_ref,
        router_probs_ref,
        choose_ref,
        cotangent_ref,
        gain_two_ref,
        router_ref,
        output_ref,
        v_ref,
        probs_ref,
        q_ref,
        k_ref,
    ) = inputs
    late_ref, hidden_grad_ref, out_ref = outputs
    sums, tail = scratch
    early, later = inputs[1:9], inputs[9:]
    wait_all(*early)
    low = jnp.bfloat16
    length, width = hidden_ref.shape
    experts = router_ref.shape[0]
    capacity = came_ref.shape[2] // 2
    group = late_ref.shape[0]
    small_rows = tail.shape[0] // group
    top = cotangent_ref[...].astype(jnp.float32)
    slots = experts * 2 * capacity
    came = came_ref[:, 0].astype(jnp.float32) + came_ref[:, 1].astype(jnp.float32)
    came = came.reshape(slots, width).astype(low)
    row = lax.broadcasted_iota(jnp.int32, (slots, length), 0)
    spread = jnp.concatenate(
        [
            jnp.where(row == slot_ref[0:1], 1.0, 0.0).astype(low),
            jnp.where(row == slot_ref[1:2], 1.0, 0.0).astype(low),
        ],
        axis=1,
    )
    back = dot_first(spread, came)
    returned, d_normed_two = back[:length], back[length:]
    hidden = hidden_ref[...]
    router_probs, choose = router_probs_ref[...], choose_ref[...]
    gate = jnp.sum(router_probs * choose, axis=1, keepdims=True)
    out_ref[...] = (hidden + gate * returned).astype(low)
    out_ref.send()
    d_gate = jnp.sum(top * returned, axis=1, keepdims=True)
    d_probs = choose * d_gate
    d_logits = router_probs * (
        d_probs - jnp.sum(router_probs * d_probs, axis=1, keepdims=True)
    )
    d_logits = d_logits.astype(low)
    factor = rms_factor(hidden)
    gain_two = row_of(gain_two_ref)
    normed_two = (hidden * factor * gain_two).astype(low)
    grad_router = dot_first(d_logits, normed_two)
    d_normed_two = d_normed_two + jnp.dot(
        d_logits, router_ref[...], preferred_element_type=jnp.float32
    )
    d_from_norm, grad_ffn = norm_backward(hidden, factor, gain_two, d_normed_two)
    d_hidden = top + d_from_norm
    hidden_grad_ref[...] = d_hidden
    hidden_grad_ref.send()
    d_mixed = d_hidden.astype(low)
    d_attended = dot_last(d_mixed, output_ref[...]).astype(low)
    flipped = d_mixed.T
    for head in range(HEADS):
        at = 3 * HEADS + head
        late_ref[at // 3, at % 3 * HEAD_DIM : (at % 3 + 1) * HEAD_DIM] = flipped[
            head * HEAD_DIM : (head + 1) * HEAD_DIM
        ]

    wait_all(*later)
    first = pair_masks(length)
    upper = lax.broadcasted_iota(jnp.int32, (LANES, length), 0) < HEAD_DIM
    lane = lax.broadcasted_iota(jnp.int32, (length, length), 1)
    place = lax.broadcasted_iota(jnp.int32, (length, length), 0)
    reverse = jnp.where(place + lane == length - 1, 1.0, 0.0).astype(low)
    for pair in range(HEADS // 2):
        lanes = slice(pair * LANES, (pair + 1) * LANES)
        upstream = d_attended[:, lanes]
        probs = probs_ref[pair]
        d_probs = dot_last(upstream, stacked_heads(v_ref[:, lanes], first))
        parts = []
        for head in range(2):
            span = slice(head * length, (head + 1) * length)
            own, grad = probs[:, span], d_probs[:, span]
            parts.append(own * (grad - jnp.sum(own * grad, axis=1, keepdims=True)))
        d_scores = jnp.concatenate(parts, axis=1).astype(low)
        d_values = dot_first(upstream, probs.astype(low))
        d_values = jnp.where(upper, d_values[:, :length], d_values[:, length:])
        d_keys = dot_first(q_ref[:, lanes], d_scores) * score_scale
        d_keys = jnp.where(upper, d_keys[:, :length], d_keys[:, length:])
        d_queries = jnp.dot(
            d_scores, stacked_heads(k_ref[:, lanes], first), preferred_element_type=jnp.float32
        )
        d_queries = (d_queries * score_scale).astype(low)
        for which, value in enumerate(
            (d_queries.T, d_keys.astype(low), d_values.astype(low))
        ):
            for head in range(2):
                at = which * HEADS + 2 * pair + head
                late_ref[at // 3, at % 3 * HEAD_DIM : (at % 3 + 1) * HEAD_DIM] = value[
                    head * HEAD_DIM : (head + 1) * HEAD_DIM
                ]
        upside = jnp.dot(reverse, d_scores, preferred_element_type=jnp.float32)
        for head in range(2):
            own = upside[:, head * length : (head + 1) * length]
            own = jnp.concatenate([own, jnp.zeros_like(own)], axis=1)
            own = pltpu.roll(own, 0, 1, stride=1, stride_axis=0)
            at = 2 * pair + head
            sums[at % 4, at // 4 : at // 4 + 1] = jnp.sum(own, axis=0, keepdims=True)

    shift = lax.broadcasted_iota(jnp.int32, (2 * length, LANES), 0) - (length - 1)
    bucket = bucket_of(shift)
    lane_wide = lax.broadcasted_iota(jnp.int32, (2 * length, LANES), 1)
    bias_rows = 0.0
    for quarter in range(4):
        hot = jnp.where(bucket + quarter * BUCKETS == lane_wide, 1.0, 0.0)
        bias_rows = bias_rows + jnp.dot(
            sums[quarter],
            hot,
            precision=lax.Precision.HIGHEST,
            preferred_element_type=jnp.float32,
        )
    chunks = width // LANES
    tail[...] = jnp.zeros_like(tail)
    for chunk in range(chunks):
        lanes = slice(chunk * LANES, (chunk + 1) * LANES)
        tail[chunk : chunk + 1] = grad_ffn[:, lanes]
        for expert in range(experts):
            at = chunks + HEADS // 4 + expert * chunks + chunk
            tail[at : at + 1] = grad_router[expert : expert + 1, lanes]
    tail[chunks : chunks + HEADS // 4] = bias_rows[: HEADS // 4]
    block = 4 * width // group
    for at in range(group):
        own = tail[at * small_rows : (at + 1) * small_rows]
        high = own.astype(low).astype(jnp.float32)
        late_ref[at, block:] = jnp.concatenate([high, own - high], axis=0).astype(low)
    late_ref.send()


def backward_of(came, weight, gain_two, router, cotangent, saved, group):
    length, width = cotangent.shape
    experts = router.shape[0]
    low = jnp.bfloat16
    small_rows = -(-small_count(width, experts) // group)
    block = 4 * width // group
    outputs = (
        shaped((group, block + 2 * small_rows, length), low),
        shaped((length, width), jnp.float32),
        shaped((length, width), low),
    )
    scratch = (
        pltpu.VMEM((4, 8, 2 * length), jnp.float32),
        pltpu.VMEM((group * small_rows, LANES), jnp.float32),
    )
    q, k, v, probs, hidden, router_probs, choose, slot = saved
    inputs = (slot, hidden, router_probs, choose, cotangent, gain_two, router, weight)
    return staged(
        backward_kernel,
        "backward",
        (),
        (*inputs, v, probs, q, k),
        outputs,
        scratch,
        4 * length * width * width,
        10 * width * width,
        residents=(came,),
        mib=62,
    )


def first_norm_kernel(numbers, inputs, outputs, scratch):
    late_ref, hidden_grad_ref, query_ref, key_ref, value_ref, tokens_ref, gain_ref = inputs
    gain_out, grad_ref = outputs
    wait_all(*inputs)
    d_normed = 0.0
    each = late_ref.shape[0] // 4
    block = query_ref.shape[0] // each
    for which, weight in enumerate((query_ref, key_ref, value_ref)):
        turned = [late_ref[i, :block] for i in range(which * each, (which + 1) * each)]
        d_normed = d_normed + lax.dot_general(
            jnp.concatenate(turned, axis=0),
            weight[...],
            (((0,), (1,)), ((), ())),
            preferred_element_type=jnp.float32,
        )
    inputs = tokens_ref[...].astype(jnp.float32)
    d_first, grad_norm = norm_backward(
        inputs, rms_factor(inputs), row_of(gain_ref), d_normed
    )
    grad_ref[...] = (hidden_grad_ref[...] + d_first).astype(jnp.bfloat16)
    grad_ref.send()
    gain_out[...] = jnp.zeros(gain_out.shape, jnp.float32)
    for chunk in range(gain_ref.shape[0]):
        gain_out[chunk : chunk + 1] = grad_norm[:, chunk * LANES : (chunk + 1) * LANES]
    gain_out.send()


def first_norm_of(late, hidden_grad, weights, tokens, gain):
    length, width = tokens.shape
    low = jnp.bfloat16
    rows = -(-gain.shape[0] // 8) * 8
    return staged(
        first_norm_kernel,
        "first_norm",
        (),
        (late, hidden_grad, *weights, tokens, gain),
        (shaped((length, width), low),),
        (),
        6 * length * width * width,
        8 * width * width,
        kept=(shaped((rows, LANES), jnp.float32),),
        mib=56,
    )


def small_count(width, experts):
    return (1 + experts) * (width // LANES) + HEADS // 4


def pick_kernel(numbers, inputs, outputs, scratch):
    (which_ref,), (*pieces, tokens_ref) = numbers, inputs
    which = which_ref[0]
    pieces = [piece.ref() for piece in pieces]
    rows = pieces[0].shape[0]
    tokens_ref = tokens_ref.ref()
    if len(pieces) > 1:
        for part, piece in enumerate(pieces):
            outputs[0][part * rows : (part + 1) * rows] = piece[...]
        outputs[0].send()
    for out, turn in zip(outputs[-2:], (3, 1)):

        @pl.when(which == turn)
        def _():
            for part, piece in enumerate(pieces):
                out[part * rows : (part + 1) * rows] = piece[...]

        @pl.when(which != turn)
        def _():
            out[...] = tokens_ref[...]

        out.send()


def picked(which, pieces, tokens):
    outputs = (shaped(tokens.shape, tokens.dtype),) * (2 if len(pieces) == 1 else 3)
    return staged(
        pick_kernel,
        "picked",
        (which,),
        (*pieces, tokens),
        outputs,
        (),
        0,
        10 * tokens.size,
    )


def left_kernel(numbers, inputs, outputs, scratch):
    (which_ref,), (*pieces, gain_ref), (left_ref,) = numbers, inputs, outputs
    which = which_ref[0]
    scale = row_of(gain_ref)
    wait_all(*pieces)
    count = pieces[0].shape[0]
    spans = [
        (piece, at, slice(number * count + at, number * count + at + LANES))
        for number, piece in enumerate(pieces)
        for at in range(0, count, LANES)
    ]

    @pl.when(which < 3)
    def _():
        for piece, at, span in spans:
            own = piece[at : at + LANES].astype(jnp.float32)
            own = (own * rms_factor(own) * scale).astype(jnp.bfloat16)
            left_ref[:, span] = own.T

    @pl.when(which == 3)
    def _():
        for piece, at, span in spans:
            left_ref[:, span] = piece[at : at + LANES].T

    left_ref.send()


def left_of(which, pieces, gain):
    count, width = pieces[0].shape
    total = count * len(pieces)
    kept = (shaped((width, total), jnp.bfloat16),)
    inputs = (*pieces, gain)
    (left,) = staged(
        left_kernel,
        "left",
        (which,),
        inputs,
        (),
        (),
        10 * total * width,
        6 * total * width,
        kept=kept,
        mib=44,
    )
    return left


gelu_scale = 0.7978845608028654
gelu_cubic = 0.044715


def hidden_pass(rows, slots, part_in, part_out):
    inner = jnp.dot(rows, part_in[...], preferred_element_type=jnp.float32)
    upstream = dot_last(slots, part_out[...])
    square = inner * inner
    bent = jnp.tanh(gelu_scale * (inner + gelu_cubic * (square * inner)))
    active = (inner * (0.5 * (1.0 + bent))).astype(jnp.bfloat16)
    slope = 0.5 * (1.0 + bent) + 0.5 * inner * (1.0 - bent * bent) * (
        gelu_scale * (1.0 + 3.0 * gelu_cubic * square)
    )
    return active, (upstream * slope).astype(jnp.bfloat16)


def expert_pass(rows, slots, weights):
    result, d_rows = 0.0, 0.0
    for part_in, part_out in weights:
        active, d_inner = hidden_pass(rows, slots, part_in, part_out)
        result = result + jnp.dot(active, part_out[...], preferred_element_type=jnp.float32)
        d_rows = d_rows + dot_last(d_inner, part_in[...])
    return result, d_rows


def four_of_eight(shape):
    return lax.broadcasted_iota(jnp.int32, shape, 0) & 7 < 4


def sorted_rows(blocks_ref):
    number, height, width = blocks_ref.shape
    main = height // 2 - 4
    mixed = blocks_ref[:, 2 * main :].astype(jnp.float32).reshape(number * 8, width)
    ahead = four_of_eight(mixed.shape)
    second = pltpu.roll(mixed, number * 8 - 4, 0)
    zero = jnp.zeros_like(mixed)
    sorted_kinds = []
    for whole, rest in (
        (blocks_ref[:, :main], mixed),
        (blocks_ref[:, main : 2 * main], second),
    ):
        rest = jnp.where(ahead, rest, zero).astype(jnp.bfloat16)
        sorted_kinds.append(jnp.concatenate([whole.reshape(number * main, width), rest], axis=0))
    return sorted_kinds


def expert_kernel(numbers, inputs, outputs, scratch):
    blocks_ref, in_a, out_a, in_b, out_b = inputs
    (back_ref,) = outputs
    low = jnp.bfloat16
    blocks, height, width = blocks_ref.shape
    main = height // 2 - 4
    count = blocks * main
    rows, slots = sorted_rows(blocks_ref)
    result, d_rows = 0.0, 0.0
    for part_in, part_out in ((in_a, out_a), (in_b, out_b)):
        wait_all(part_in, part_out)
        part_result, part_rows = expert_pass(rows, slots, ((part_in, part_out),))
        result, d_rows = result + part_result, d_rows + part_rows
    back_ref[:, :main] = result[:count].reshape(blocks, main, width).astype(low)
    back_ref[:, main : 2 * main] = d_rows[:count].reshape(blocks, main, width).astype(low)
    mixed = result[count:]
    mixed = jnp.where(four_of_eight(mixed.shape), mixed, pltpu.roll(d_rows[count:], 4, 0))
    back_ref[:, 2 * main :] = mixed.reshape(blocks, 8, width).astype(low)
    back_ref.send()


def sorting(number, height):
    half, capacity = number * height // 2, height // 2
    place = np.arange(2 * half)
    sort = place % half // capacity * height + place // half * capacity + place % capacity
    unsort = np.empty_like(sort)
    unsort[sort] = place
    return jnp.asarray(np.stack([sort, unsort], axis=1), jnp.int32)


def rows_by_product(rows_ref, order_ref):
    count = rows_ref.shape[0]
    lanes = lax.broadcasted_iota(jnp.int32, (count, count), 1)
    sort = jnp.where(order_ref[:, 0:1] == lanes, 1.0, 0.0).astype(jnp.bfloat16)
    ordered = jnp.dot(sort, rows_ref[...], preferred_element_type=jnp.float32)
    ordered = ordered.astype(jnp.bfloat16)
    return ordered[: count // 2], ordered[count // 2 :]


def expert_sorting_kernel(numbers, inputs, outputs, scratch):
    rows_ref, order_ref, in_a, out_a, in_b, out_b = inputs
    (back_ref,) = outputs
    count = rows_ref.shape[0]
    rows, slots = rows_by_product(rows_ref, order_ref)
    result, d_rows = expert_pass(rows, slots, ((in_a, out_a), (in_b, out_b)))
    lanes = lax.broadcasted_iota(jnp.int32, (count, count), 1)
    unsort = jnp.where(order_ref[:, 1:2] == lanes, 1.0, 0.0).astype(jnp.bfloat16)
    both = jnp.concatenate([result.astype(jnp.bfloat16), d_rows.astype(jnp.bfloat16)], axis=0)
    back_ref[...] = jnp.dot(unsort, both, preferred_element_type=jnp.float32).astype(jnp.bfloat16)
    back_ref.send()


def expert_rows_of(blocks, part_weights):
    number, height, width = blocks.shape
    hidden_width = part_weights[0].shape[1]
    flops, moved = 8 * number * height * width * hidden_width, 12 * width * width
    if mixed_tiles(height // 2):
        (back,) = staged(
            expert_kernel,
            "expert_rows",
            (),
            part_weights,
            (shaped(blocks.shape, blocks.dtype),),
            (),
            flops,
            moved,
            residents=(blocks,),
            mib=62,
        )
        return back
    (back,) = staged(
        expert_sorting_kernel,
        "expert_rows",
        (),
        (blocks.reshape(-1, width), sorting(number, height), *part_weights),
        (shaped((number * height, width), blocks.dtype),),
        (),
        flops,
        moved,
    )
    return back.reshape(blocks.shape)


def grads_kernel(mixed, numbers, inputs, outputs, scratch):
    wait_all(*inputs)
    if mixed:
        blocks_ref, part_in, part_out, *got = inputs
        rows, slots = sorted_rows(blocks_ref)
    else:
        rows_ref, order_ref, part_in, part_out, *got = inputs
        rows, slots = rows_by_product(rows_ref, order_ref)
    active, d_inner = hidden_pass(rows, slots, part_in, part_out)
    for number, (left, right) in enumerate(((rows, d_inner), (active, slots))):
        grad = dot_first(left, right)
        if got:
            outputs[number][...] = grad + got[number][...].astype(jnp.float32)
        else:
            outputs[number][...] = grad.astype(jnp.bfloat16)
        outputs[number].send()


def expert_grads_of(blocks, part_in, part_out, *got):
    number, height, width = blocks.shape
    hidden_width = part_in.shape[1]
    mixed = mixed_tiles(height // 2)
    kind = jnp.float32 if got else jnp.bfloat16
    outputs = (shaped((width, hidden_width), kind), shaped((hidden_width, width), kind))
    rows = (blocks,) if mixed else (blocks.reshape(-1, width), sorting(number, height))
    return staged(
        functools.partial(grads_kernel, mixed),
        "own_grads" if got else "sent_grads",
        (),
        (*rows, part_in, part_out, *got),
        outputs,
        (),
        0 if got else 4 * number * height * width * hidden_width,
        0 if got else 8 * width * width,
    )


def in_parts(values):
    high = values.astype(jnp.bfloat16).astype(jnp.float32)
    return jnp.concatenate([high, values - high], axis=0).astype(jnp.bfloat16)


def from_parts(parts):
    parts = parts.astype(jnp.float32)
    rows = parts.shape[0] // 2
    return parts[:rows] + parts[rows:]


def block_kernel(numbers, inputs, outputs, scratch):
    (bits_ref,), (late_ref, left_ref, gain_ref), (block_ref,) = numbers, inputs, outputs
    group = late_ref.shape[0]
    part = left_ref.shape[0] // 2
    block = left_ref.shape[0] * 4 // group
    edge = block - LANES
    half = part // 2
    gain_edge = block_ref.shape[1] - 2 * gain_ref.shape[0]
    odd = bits_ref[3] == 1
    here = bits_ref[0] * 8 + bits_ref[1] * 4 + bits_ref[2] * 2 + bits_ref[3]
    right = jnp.concatenate(
        [late_ref[here ^ factor_order(i), :block] for i in range(group)], axis=1
    )
    right = jnp.where(odd, jnp.concatenate([right[edge:], right[:edge]], axis=0), right)
    total = dot_last(left_ref[...], right)
    first = pair_masks(half)
    small = in_parts(from_parts(jnp.sum(late_ref[:, block:].astype(jnp.float32), axis=0)))
    gain = in_parts(gain_ref[...])
    for side in range(2):
        own = total[side * part : (side + 1) * part]
        block_ref[side, :part] = own[:, :LANES].astype(jnp.bfloat16)
        rest = own[:, LANES:]
        rest = jnp.concatenate([rest, rest], axis=1)
        upper, lower = rest[:half], rest[half:]
        even = jnp.where(first, upper, lower)
        packed = jnp.where(odd, jnp.where(first, lower, upper), even)
        block_ref[side, part : part + half] = packed.astype(jnp.bfloat16)
        block_ref[side, part + half : gain_edge] = small
        block_ref[side, gain_edge:] = gain


def block_of(bits, late, left, gain, small_rows):
    group, rows, length = late.shape
    width = left.shape[0]
    height = 3 * width // 4 + 2 * (small_rows + gain.shape[0])
    (block,) = staged(
        block_kernel,
        "grad_block",
        (bits,),
        (),
        (),
        (),
        8 * width * width * length,
        2 * left.size,
        residents=(late, left, gain),
        kept=(shaped((2, height, LANES), jnp.bfloat16),),
        mib=24,
    )
    return block


def share_kernel(edge, small_rows, numbers, inputs, outputs, scratch):
    (own_ref, got_ref), (share_ref,) = inputs, outputs
    gain_edge = edge + 2 * small_rows
    for side in range(2):
        own = own_ref[side, :edge].astype(jnp.float32) + got_ref[side, :edge].astype(jnp.float32)
        share_ref[side, :edge] = own.astype(jnp.bfloat16)
        for rows in (slice(edge, gain_edge), slice(gain_edge, None)):
            share_ref[side, rows] = in_parts(
                from_parts(own_ref[side, rows]) + from_parts(got_ref[side, rows])
            )


def share_of(own, got, edge, small_rows):
    (share,) = staged(
        functools.partial(share_kernel, edge, small_rows),
        "share",
        (),
        (),
        (),
        (),
        own.size,
        6 * own.size,
        residents=(own, got),
        kept=(shaped(own.shape, own.dtype),),
        mib=8,
    )
    return share


def assemble_kernel(weights, small_rows, bits_ref, sources, outs, made, out_sems, put_small):
    em, ey, dx, dc = [bits_ref[i] for i in range(4)]
    part = made.shape[1] // 2
    half = part // 2
    edge = part + half
    first = pair_masks(half)
    def copy_of(number, side, target):
        rows = pl.ds(side * part, part)
        return pltpu.make_async_copy(
            made.at[number, rows], target.at[rows], out_sems.at[2 * number + side]
        )

    for number, weight in enumerate(weights):
        truth = (em ^ (weight // 2)) * 2 + (ey ^ (weight % 2))
        for side in range(2):
            for here in range(4):

                @pl.when(dx * 2 + dc == here)
                def _():
                    own = [
                        sources[4 * number + 2 * ((i ^ here) & 1) + ((i ^ here) >> 1)]
                        for i in range(4)
                    ]
                    rows = slice(side * part, (side + 1) * part)
                    upper = slice(side * part, side * part + half)
                    lower = slice(side * part + half, (side + 1) * part)
                    for twin in range(2):
                        even, odd = own[2 * twin], own[2 * twin + 1]
                        at = 3 * twin * LANES
                        made[number, rows, at : at + LANES] = even[side, :part].astype(jnp.float32)
                        made[number, rows, at + 2 * LANES : at + 3 * LANES] = odd[
                            side, :part
                        ].astype(jnp.float32)
                        left = even[side, part:edge].astype(jnp.float32)
                        right = odd[side, part:edge].astype(jnp.float32)
                        middle = slice(at + LANES, at + 2 * LANES)
                        made[number, upper, middle] = jnp.where(first, left, right)
                        made[number, lower, middle] = pltpu.roll(
                            jnp.where(first, right, left), HEAD_DIM, 1
                        )
                    for i in range(4 if side == 0 else 0):
                        tail = own[i][0, edge:].astype(jnp.float32)
                        gain = tail[2 * small_rows :]
                        gain_rows = gain.shape[0] // 2
                        put_small(
                            number,
                            i,
                            jnp.concatenate(
                                [
                                    tail[:small_rows] + tail[small_rows : 2 * small_rows],
                                    gain[:gain_rows] + gain[gain_rows:],
                                ],
                                axis=0,
                            ),
                        )

            for i in range(4):

                @pl.when(truth == i)
                def _():
                    copy_of(number, side, outs[i]).start()

    for number, weight in enumerate(weights):
        truth = (em ^ (weight // 2)) * 2 + (ey ^ (weight % 2))
        for i in range(4):

            @pl.when(truth == i)
            def _():
                for side in range(2):
                    copy_of(number, side, outs[i]).wait()


def first_half_kernel(small_rows, bits_ref, *refs):
    sources, outs, small_out, made, out_sems = refs[:8], refs[8:12], refs[12], refs[13], refs[14]

    def put_small(number, i, rows):
        small_out[number, i] = rows

    assemble_kernel((0, 2), small_rows, bits_ref, sources, outs, made, out_sems, put_small)


def second_half_kernel(small_rows, bits_ref, *refs):
    sources, small_ref, outs = refs[:8], refs[8], refs[13:17]
    norm_out, ffn_out, bias_out, router_out = refs[17:21]
    made, tail, out_sems = refs[21:]
    em, ey = bits_ref[0], bits_ref[1]
    for number in range(2):
        tail[(em ^ number) * 2 + ey] = small_ref[number]

    def put_small(number, i, rows):
        tail[(em ^ number) * 2 + (ey ^ 1), i] = rows

    assemble_kernel((1, 3), small_rows, bits_ref, sources, outs, made, out_sems, put_small)

    def small_row(at):
        at, row = divmod(at, small_rows)
        return tail[at // 4, at % 4, row : row + 1]

    chunks = made.shape[2] // LANES
    total = 0.0
    for at in range(16):
        total = total + tail[at // 4, at % 4, small_rows:]
    norm_out[...] = total[:chunks]
    for chunk in range(chunks):
        lanes = slice(chunk * LANES, (chunk + 1) * LANES)
        ffn_out[chunk : chunk + 1] = small_row(chunk)
        for expert in range(router_out.shape[0]):
            router_out[expert : expert + 1, lanes] = small_row(
                chunks + HEADS // 4 + expert * chunks + chunk
            )
    for head in range(HEADS):
        at = head % 4 * BUCKETS
        bias_out[head : head + 1] = small_row(chunks + head // 4)[:, at : at + BUCKETS]


def first_half(bits, sources, small_rows, width):
    gain_rows = (sources[0].shape[1] - 3 * width // 4 - 2 * small_rows) // 2
    *grads, small = pl.pallas_call(
        functools.partial(first_half_kernel, small_rows),
        out_shape=(shaped((width, width), jnp.float32),) * 4
        + (shaped((2, 4, small_rows + gain_rows, LANES), jnp.float32),),
        in_specs=[pl.BlockSpec(memory_space=pltpu.SMEM)] + [whole_spec()] * 8,
        out_specs=(any_spec(),) * 4 + (whole_spec(),),
        scratch_shapes=[
            pltpu.VMEM((2, width, width), jnp.float32),
            pltpu.SemaphoreType.DMA((4,)),
        ],
        compiler_params=params(16),
        cost_estimate=cost(8 * width * width, 12 * width * width),
        name="first_half",
    )(bits, *sources)
    return grads, small


def second_half(bits, sources, small, grads, small_rows, width, experts):
    return pl.pallas_call(
        functools.partial(second_half_kernel, small_rows),
        out_shape=(shaped((width, width), jnp.float32),) * 4
        + (
            shaped((width // LANES, LANES), jnp.float32),
            shaped((width // LANES, LANES), jnp.float32),
            shaped((HEADS, BUCKETS), jnp.float32),
            shaped((experts, width), jnp.float32),
        ),
        in_specs=[pl.BlockSpec(memory_space=pltpu.SMEM)]
        + [whole_spec()] * 9
        + [any_spec()] * 4,
        out_specs=(any_spec(),) * 4 + (whole_spec(),) * 4,
        input_output_aliases={10 + i: i for i in range(4)},
        scratch_shapes=[
            pltpu.VMEM((2, width, width), jnp.float32),
            pltpu.VMEM((4, 4) + small.shape[2:], jnp.float32),
            pltpu.SemaphoreType.DMA((4,)),
        ],
        compiler_params=params(16),
        cost_estimate=cost(8 * width * width, 12 * width * width),
        name="second_half",
    )(bits, *sources, small, *grads)


def place_in_group():
    place = [lax.axis_index(axis) for axis in ("em", "ey", "dx", "dc")]
    return (2 * place[0] + place[1]).astype(jnp.int32), jnp.stack(place).astype(jnp.int32)


def factor_order(at):
    return (at & 1) * 2 + (at >> 1 & 1) * 4 + (at >> 2 & 1) * 8 + (at >> 3)


def with_other(rows, axis):
    return jnp.concatenate([rows, swap(rows, axis)], axis=0)


def gathered_grads(late, left, gain_rows, place, small_rows, experts, beside):
    width = left.shape[0]
    block = block_of(place, late, left, gain_rows, small_rows)
    block, beside = lax.optimization_barrier((block, beside))
    beside = expert_grads_of(*beside)
    got, beside = lax.optimization_barrier((swap(block, "eh"), beside))
    near = share_of(block, got, 3 * width // 4, small_rows)
    far, near_x, near_y = swap(near, "em"), swap(near, "dx"), swap(near, "ey")
    far_x, far_y = swap(near_x, "em"), swap(far, "ey")
    near_both = swap(near_y, "dx")
    far_both = swap(near_both, "em")

    def both_cores(*sources):
        return sources + tuple(swap(source, "dc") for source in sources)

    sources = both_cores(near, near_x) + both_cores(far, far_x)
    grads, small = first_half(place, sources, small_rows, width)
    sources = both_cores(near_y, near_both) + both_cores(far_y, far_both)
    grads = second_half(place, sources, small, grads, small_rows, width, experts)
    return grads, beside


def gathered_grads_plain(late, left, gain_rows, place, small_rows, experts, beside):
    group, rows, length = late.shape
    width = left.shape[0]
    block = 4 * width // group
    small = jnp.sum(late[:, block:].astype(jnp.float32), axis=0)
    small = lax.psum(small[:small_rows] + small[small_rows:], "eh")
    order = jnp.asarray([factor_order(at) for at in range(group)], jnp.int32)
    order = order ^ lax.axis_index(GROUP_AXES)
    late_block = jnp.take(late[:, :block], order, axis=0)
    late_block = late_block.transpose(1, 0, 2).reshape(block, group * length)
    grad_block = dot_last(late_block, left)
    mine = lax.psum_scatter(grad_block, "eh", scatter_dimension=0, tiled=True)
    grads = lax.all_gather(mine.astype(jnp.bfloat16), "eh", axis=0, tiled=True)
    grads = lax.all_gather(grads, GROUP_AXES, axis=0, tiled=True)
    small = lax.all_gather(small, GROUP_AXES, axis=0, tiled=True).reshape(-1)
    grads = grads.reshape(4, width, width).transpose(0, 2, 1).astype(jnp.float32)
    sizes = (width, HEADS * BUCKETS, experts * width)
    ends = np.cumsum(sizes)
    pieces = [small[end - size : end] for end, size in zip(ends, sizes)]
    pieces[1], pieces[2] = pieces[1].reshape(HEADS, BUCKETS), pieces[2].reshape(experts, width)
    grad_norm = lax.psum(gain_rows, TOKEN_AXES)[: width // LANES]
    return (*grads, grad_norm, *pieces), expert_grads_of(*beside)


def per_device(
    tokens,
    norm_gain,
    w_query,
    w_key,
    w_value,
    w_output,
    rel_bias,
    ffn_gain,
    w_router,
    w_in,
    w_out,
    routes,
    lengths,
    cotangent,
):
    length, model_width = tokens.shape
    experts = w_router.shape[1]
    group = lax.axis_size(GROUP_AXES)
    capacity = max(2, (5 * length + 4 * experts - 1) // (4 * experts))
    small_rows = -(-small_count(model_width, experts) // group)
    gain_one, gain_two = norm_gain.reshape(-1, LANES), ffn_gain.reshape(-1, LANES)
    weights = (w_query, w_key, w_value, w_output)
    router = w_router.T

    w_in_own, w_out_own = w_in[0], w_out[0]
    w_in_other, w_out_other = swap(w_in_own, "dc"), swap(w_out_own, "dc")
    outgoing, attended, *saved = forward_of(
        lengths,
        tokens,
        gain_one,
        weights,
        rel_bias.T,
        gain_two,
        router,
        routes.reshape(1, length),
        cotangent,
        capacity,
    )
    which, place = place_in_group()
    outgoing, near_tokens = lax.optimization_barrier((outgoing, with_other(tokens, "dx")))
    outgoing = outgoing.reshape(2 * experts, 2 * capacity, model_width)
    incoming = lax.all_to_all(outgoing, EXPERT_AXES, split_axis=0, concat_axis=0, tiled=True)
    far_tokens = swap(near_tokens, "ey")
    near_attended, own_near, given_near = picked(
        which[None], (attended, swap(attended, "dx")), near_tokens
    )
    far_attended, got_near = swap(near_attended, "ey"), swap(given_near, "em")
    incoming, far_tokens, _ = lax.optimization_barrier((incoming, far_tokens, given_near))
    sent_back = expert_rows_of(incoming, (w_in_own, w_out_own, w_in_other, w_out_other))
    sent_back, far_attended, got_near = lax.optimization_barrier(
        (sent_back, far_attended, got_near)
    )
    came_back = lax.all_to_all(sent_back, EXPERT_AXES, split_axis=0, concat_axis=0, tiled=True)
    own_far, given_far = picked(which[None], (far_attended,), far_tokens)
    incoming, _ = lax.optimization_barrier((incoming, sent_back))
    in_other, out_other = expert_grads_of(incoming, w_in_other, w_out_other)
    factors = [own_near, own_far, got_near]
    factors = factors + [swap(rows, "dc") for rows in factors]
    came_back, factors, given_far, in_other, out_other = lax.optimization_barrier(
        (came_back, factors, given_far, in_other, out_other)
    )
    got_far = swap(given_far, "em")
    beside = (incoming, w_in_own, w_out_own, swap(in_other, "dc"), swap(out_other, "dc"))

    late, hidden_grad, output = backward_of(
        came_back.reshape(experts, 2, 2 * capacity, model_width),
        w_output,
        gain_two,
        router,
        cotangent,
        saved,
        group,
    )
    late, got_far = lax.optimization_barrier((late, got_far))
    own_late = late
    factors = factors[:3] + [got_far] + factors[3:] + [swap(got_far, "dc")]
    late = lax.all_to_all(late, GROUP_AXES, split_axis=0, concat_axis=0, tiled=True)
    left = left_of(which[None], factors, gain_one)
    gain_rows, grad_input = first_norm_of(own_late, hidden_grad, weights[:3], tokens, gain_one)
    late, left, gain_rows, beside = lax.optimization_barrier((late, left, gain_rows, beside))
    gather = gathered_grads if lax.axis_size("eh") == 2 else gathered_grads_plain
    grads, (grad_in, grad_out) = gather(
        late, left, gain_rows, place, small_rows, experts, beside
    )
    *grads, grad_norm, grad_ffn, grad_bias, grad_router = grads
    return (
        output,
        grad_input,
        grad_norm.reshape(model_width),
        *grads,
        grad_bias.T,
        grad_ffn.reshape(model_width),
        grad_router.T,
        grad_in[None],
        grad_out[None],
    )


def solution(mesh):
    exp_count, dp_count = mesh.shape["exp"], mesh.shape["dp"]
    fine = Mesh(
        mesh.devices.reshape(exp_count // 4, 2, 2, dp_count // 2, 2),
        TOKEN_AXES,
    )
    exp, dp = ("eh", "em", "ey"), ("dx", "dc")
    in_specs = (
        P(TOKEN_AXES, None),
        P(),
        P(),
        P(),
        P(),
        P(),
        P(),
        P(),
        P(),
        P(exp, None, dp),
        P(exp, dp, None),
        P(TOKEN_AXES, None),
        P(TOKEN_AXES),
        P(TOKEN_AXES, None),
    )
    out_specs = (
        P(TOKEN_AXES, None),
        P(TOKEN_AXES, None),
        P(),
        P(),
        P(),
        P(),
        P(),
        P(),
        P(),
        P(),
        P(exp, None, dp),
        P(exp, dp, None),
    )
    return jax.shard_map(
        per_device, mesh=fine, in_specs=in_specs, out_specs=out_specs, check_vma=False
    )
```
